512 devices in a mesh: member: 8 (over z_lo, core), grid: 64 (over x, y, z_hi).
Axes of the slice: x: 4, y: 8, z: 8 (z_hi: 2, z_lo: 4; z = z_hi * 4 + z_lo), core: 2. Of those that a mesh axis runs over, the one named last changes fastest.
Arguments:
- latent: bfloat16 [8, 1024, 32768], P('member', None, 'grid'), may hold values from -6 to 6
- w_in: bfloat16 [1024, 512], replicated, may hold values from -0.1875 to 0.1875
- b_in: float32 [512], replicated, may hold values from -3 to 3
- output_weight: bfloat16 [512, 83], replicated, may hold values from -0.25 to 0.25
- output_bias: float32 [83], replicated, may hold values from -3 to 3
- observed_field: float32 [83, 32768], P(None, 'grid'), may hold values from -6 to 6
- area: float32 [32768], P('grid'), may hold values from 0.2 to 2
Outputs:
- loss: float32 [32768], P('grid')
- grad_w_in: bfloat16 [1024, 512], replicated
- grad_b_in: float32 [512], replicated
- grad_w_out: float32 [512, 83], replicated
- grad_b_out: float32 [83], replicated
The draws below stay inside these ranges and needn't reach their ends.
All inputs are finite; a program needn't handle non-finite values.
Results may differ from the reference program's by a relative error of at most 0.006.
Values may be sent and summed in bfloat16 or wider, within the bound.
A program may use at most 64 MiB of HBM per device.

```python
import math
import jax
import jax.numpy as jnp
from jax import lax

DIN = 1024
HID = 512
VARS = 83
RUN_COUNT = 8
COLUMNS = 32768


def steps_of(key, extent, pieces, low, top_value):
    factor_of = 1.0
    for position, shards_of in pieces:
        heights = jax.random.uniform(jax.random.fold_in(jax.random.fold_in(key, 6), position), (shards_of,), jnp.float32, low / len(pieces), top_value / len(pieces))
        factor_of = factor_of * jnp.repeat(jnp.exp(heights), extent[position] // shards_of).reshape((-1,) + (1,) * (len(extent) - 1 - position))
    return factor_of


def bell_draw(rng, dims, spread, limit, cuts=(), held_as=jnp.bfloat16):
    array = jax.random.normal(rng, dims, jnp.float32) * spread
    if len(cuts) > 0:
        array = steps_of(rng, dims, cuts, -0.22, 0.18) * array
    return jnp.clip(array, min=-limit, max=limit).astype(held_as)


def setup_inputs(seed: int = 0) -> dict:
    key_of = jax.random.split(jax.random.key(seed), 8)
    return {
        "latent": bell_draw(key_of[0], (RUN_COUNT, DIN, COLUMNS), 1.0, 6.0, ((0, 8), (2, 64))),
        "w_in": bell_draw(key_of[1], (DIN, HID), DIN ** -0.5, 0.1875),
        "b_in": bell_draw(key_of[2], (HID,), 0.5, 3.0, (), jnp.float32),
        "output_weight": bell_draw(key_of[3], (HID, VARS), HID ** -0.5, 0.25),
        "output_bias": bell_draw(key_of[4], (VARS,), 0.5, 3.0, (), jnp.float32),
        "observed_field": bell_draw(key_of[5], (VARS, COLUMNS), 1.0, 6.0, ((1, 64),), jnp.float32),
        "area": jnp.clip(jnp.exp(math.log(2.0) - 2.3025851 * jax.random.uniform(key_of[6], (COLUMNS,), jnp.float32) ** steps_of(key_of[6], (COLUMNS,), ((0, 64),), -0.2, 0.2)), 0.2, 2.0),
    }


EPSILON = 1e-05

def activation(values):
    return jax.nn.gelu(values, approximate=True)

def euclid_norm(run_difference):
    return jnp.sqrt(lax.optimization_barrier(jnp.mean(run_difference * run_difference, axis=-2)) + EPSILON)

def reference(latent, w_in, b_in, output_weight, output_bias, observed_field, area):
    quantity_number = observed_field.shape[0]
    stacked_runs = []
    for run_number in range(RUN_COUNT):
        pre_act = jnp.dot(w_in.T, latent[run_number], preferred_element_type=jnp.float32) + b_in[:, None]
        hidden_units = activation(pre_act).astype(jnp.bfloat16)
        stacked_runs.append((jnp.dot(output_weight.T, hidden_units, preferred_element_type=jnp.float32) + output_bias[:, None]).astype(jnp.bfloat16))
    coupling_factor = area * (quantity_number * math.sqrt(RUN_COUNT / COLUMNS))
    loss = jnp.zeros((COLUMNS,), jnp.float32)
    grad_w_in = jnp.zeros((DIN, HID), jnp.float32)
    grad_b_in = jnp.zeros((HID,), jnp.float32)
    grad_w_out = jnp.zeros((HID, VARS), jnp.float32)
    grad_b_out = jnp.zeros((VARS,), jnp.float32)
    for run_number in range(RUN_COUNT):
        current_run_field = stacked_runs[run_number].astype(jnp.float32)
        observation_norm = euclid_norm(current_run_field - observed_field)
        couple_derivative = jnp.zeros((VARS, COLUMNS), jnp.float32)
        pair_dist = jnp.zeros((COLUMNS,), jnp.float32)
        for compared_run in range(RUN_COUNT):
            run_difference = current_run_field - stacked_runs[compared_run].astype(jnp.float32)
            pair_len = euclid_norm(run_difference)
            couple_derivative = couple_derivative + run_difference / (quantity_number * pair_len)
            pair_dist = pair_dist + pair_len
        loss = loss + observation_norm / RUN_COUNT - pair_dist / (2.0 * RUN_COUNT * RUN_COUNT)
        derivative_wrt_run = coupling_factor * ((current_run_field - observed_field) / (quantity_number * observation_norm) / RUN_COUNT - couple_derivative / (RUN_COUNT * RUN_COUNT))
        grad_low = derivative_wrt_run.astype(jnp.bfloat16)
        pre_act = jnp.dot(w_in.T, latent[run_number], preferred_element_type=jnp.float32) + b_in[:, None]
        hidden_full, gelu_back = jax.vjp(activation, pre_act)
        hidden_units = hidden_full.astype(jnp.bfloat16)
        grad_w_out = grad_w_out + jnp.dot(hidden_units, grad_low.T, preferred_element_type=jnp.float32)
        grad_b_out = grad_b_out + lax.optimization_barrier(jnp.sum(derivative_wrt_run, axis=1))
        grad_hidden = jnp.dot(output_weight, grad_low, preferred_element_type=jnp.float32)
        grad_pre = gelu_back(grad_hidden)[0]
        grad_b_in = grad_b_in + lax.optimization_barrier(jnp.sum(grad_pre, axis=1))
        grad_w_in = grad_w_in + jnp.dot(latent[run_number], grad_pre.astype(jnp.bfloat16).T, preferred_element_type=jnp.float32)
    return (loss, grad_w_in.astype(jnp.bfloat16), grad_b_in, grad_w_out, grad_b_out)
```

```python
import math

import jax
import jax.numpy as jnp
from jax import lax
from jax.experimental import pallas as pl
from jax.experimental.pallas import tpu as pltpu
from jax.sharding import PartitionSpec as P

MESH = pl.DeviceIdType.MESH
F32 = jnp.float32
BF16 = jnp.bfloat16
EPSILON = 1e-05
GELU_A = math.sqrt(2.0 / math.pi)
GELU_B = 0.044715

DIN, HID, VARS = 1024, 512, 83
COLS = 512
FOLD = 48
NX, NU = 4, 8
FAR4 = (2, 1, 3)
FAR8 = (4, 3, 5, 2, 6, 1, 7)
N_SEMS = 160


def dot(a, b):
    return jnp.dot(a, b, preferred_element_type=F32)


def dot_nt(a, b):
    return lax.dot_general(a, b, (((1,), (1,)), ((), ())), preferred_element_type=F32)


def kernel(
    total_columns,
    lat_hbm, win_hbm, bin_ref, wo_ref, bo_ref, obs_ref, area_ref,
    loss_ref, gw_ref, small_ref, gwo_ref,
    lat, win, win_t, bias, pre, dgelu, hidden, wop, wop_t, row, obs_pad,
    f_send, f_recv, g_send, g_recv, loss_recv, gl, gp,
    sib_send, sib_recv, own, part,
    x0_recv, s0, u0_recv, v0_recv, u1_recv, s1, x1_recv, v1_recv,
    wo_part, wo_send, wo_recv, wo_rs, wox_recv, wou_src, wou_recv, wov_recv,
    sm_c, sm_x, sm_u, sm_v,
    local_sems, send_sems, recv_sems,
):
    member, grid = lax.axis_index("member"), lax.axis_index("grid")
    c, zlo = member % 2, member // 2
    a, b = zlo // 2, zlo % 2
    zhi, y, x = grid % 2, (grid // 2) % 8, grid // 16
    z = zhi * 4 + zlo
    u = y * (1 - c) + z * c
    v = z * (1 - c) + y * c

    def device(x, y, z, c):
        return ((z % 4) * 2 + c, (x * 8 + y) * 2 + z // 4)

    def to_x(k):
        return device((x + k) % 4, y, z, c)

    def to_u(k):
        return device(x, (y + k * (1 - c)) % 8, (z + k * c) % 8, c)

    def to_v(k):
        return device(x, (y + k * c) % 8, (z + k * (1 - c)) % 8, c)

    sibling = (zlo * 2 + 1 - c, grid)

    def flip(bit, by):
        return 1 - bit if by else bit

    def member_of(rel):
        ra, rb, rc = rel
        return (2 * flip(a, ra) + flip(b, rb)) * 2 + flip(c, rc)

    rels = [(ra, rb, rc) for ra in (1, 0) for rb in (1, 0) for rc in (1, 0)][:-1]

    started = []

    def send(src, dst, to):
        i = len(started)
        copy = pltpu.make_async_remote_copy(
            src_ref=src, dst_ref=dst, send_sem=send_sems.at[i], recv_sem=recv_sems.at[i],
            device_id=to, device_id_type=MESH,
        )
        copy.start()
        started.append(copy)
        return copy

    def arrived(copies):
        for copy in copies:
            copy.wait_recv()

    barrier = pltpu.get_barrier_semaphore()
    partners = (
        [(member_of(rel), grid) for rel in rels]
        + [to_x(k) for k in FAR4] + [to_u(k) for k in FAR8] + [to_v(k) for k in FAR8]
    )
    for partner in partners:
        pl.semaphore_signal(barrier, inc=1, device_id=partner, device_id_type=MESH)

    halves = [1 - a, a]
    load_w = [
        pltpu.make_async_copy(
            win_hbm.at[pl.ds(512 * i, 512)], win.at[pl.ds(512 * i, 512)], local_sems.at[i])
        for i in range(2)
    ]
    load_l = [
        pltpu.make_async_copy(
            lat_hbm.at[0, :, pl.ds(pl.multiple_of(h * 256, 256), 256)],
            lat.at[:, pl.ds(pl.multiple_of(h * 256, 256), 256)], local_sems.at[2 + i])
        for i, h in enumerate(halves)
    ]
    for copy in load_w + load_l:
        copy.start()

    for i in range(4):
        bias[pl.ds(128 * i, 128), :] = jnp.transpose(
            jnp.broadcast_to(bin_ref[:, pl.ds(128 * i, 128)], (128, 128)))
    wop[...] = jnp.zeros_like(wop)
    wop[:, 0:VARS] = wo_ref[...]
    wop_t[...] = jnp.transpose(wop[...])
    row[...] = jnp.zeros_like(row)
    row[:, 0:VARS] = bo_ref[...]
    bias_out = jnp.transpose(jnp.broadcast_to(row[...], (128, 128)))[0:2 * FOLD]
    lane = lax.broadcasted_iota(jnp.int32, (FOLD, 128), 1)
    low_lane = lane < 64
    low_row = lax.broadcasted_iota(jnp.int32, (1, 128), 1) < 64

    def swap(value):
        return pltpu.roll(value, 64, 1)

    for i in range(2):
        load_w[i].wait()
        for r in range(2):
            at = 512 * i + 256 * r
            win_t[:, pl.ds(at, 256)] = jnp.transpose(win[pl.ds(at, 256), :])

    f_copies = []
    for i, h in enumerate(halves):
        cols = pl.ds(pl.multiple_of(h * 256, 256), 256)
        load_l[i].wait()
        pre[:, cols] = dot(win_t[...], lat[:, cols])

        def activate(r, _):
            rows = pl.ds(pl.multiple_of(r * 64, 64), 64)
            shift = bias[rows, :]
            value = pre[rows, cols] + jnp.concatenate([shift, shift], axis=1)
            pre[rows, cols] = value
            inner = GELU_A * (value + GELU_B * (value * value * value))
            hidden[rows, cols] = (0.5 * value * (1.0 + jnp.tanh(inner))).astype(BF16)
            return 0

        lax.fori_loop(0, HID // 64, activate, 0)
        field = dot(wop_t[0:2 * FOLD, :], hidden[:, cols])
        for t in range(2):
            chunk = (field[:, 128 * t:128 * t + 128] + bias_out).astype(BF16).astype(F32)
            lo, hi = chunk[0:FOLD], chunk[FOLD:2 * FOLD]
            f_send[i, t, 0] = jnp.where(low_lane, lo, swap(hi)).astype(BF16)
            f_send[i, t, 1] = jnp.where(low_lane, swap(lo), hi).astype(BF16)
        if i == 0:
            pl.semaphore_wait(barrier, len(partners))
        for rel in rels:
            if rel[0] == 1 - i:
                src = f_send.at[i, flip(b, rel[1]), flip(c, rel[2])]
                f_copies.append(send(src, f_recv.at[member], (member_of(rel), grid)))
    f_recv[pl.ds(member, 1)] = f_send[1, pl.ds(b, 1), pl.ds(c, 1)].reshape(1, FOLD, 128)

    def derive(r, _):
        rows = pl.ds(pl.multiple_of(r * 32, 32), 32)
        value = pre[rows, :]
        square = value * value
        t = jnp.tanh(GELU_A * (value + GELU_B * (value * square)))
        dgelu[rows, :] = 0.5 * (1.0 + t) + (0.5 * GELU_A) * value * (1.0 - t * t) * (
            1.0 + (3.0 * GELU_B) * square)
        return 0

    lax.fori_loop(0, HID // 32, derive, 0)
    obs_pad[...] = jnp.zeros_like(obs_pad)
    own_cols = pl.ds(pl.multiple_of(zlo * 128, 128), 128)
    obs_pad[0:VARS, :] = obs_ref[:, own_cols]
    lo, hi = obs_pad[0:FOLD], obs_pad[FOLD:2 * FOLD]
    first = c == 0
    observed = jnp.where(low_lane, jnp.where(first, lo, swap(lo)), jnp.where(first, swap(hi), hi))
    area = area_ref[:, own_cols]
    area = jnp.where(low_row, jnp.where(first, area, swap(area)), jnp.where(first, swap(area), area))
    factor = area * (VARS * math.sqrt(8 / total_columns))
    gl[2 * FOLD:128, :] = jnp.zeros((128 - 2 * FOLD, COLS), BF16)

    def norm(difference):
        total = jnp.sum(difference * difference, axis=0, keepdims=True)
        square = (total + swap(total)) / VARS + EPSILON
        inverse = lax.rsqrt(square)
        return square * inverse, inverse

    arrived(f_copies)
    fields = [f_recv[i].astype(F32) for i in range(8)]
    grads = []
    true_total = jnp.zeros((1, 128), F32)
    for m in range(8):
        difference = fields[m] - observed
        distance, inverse = norm(difference)
        true_total = true_total + distance
        grads.append(difference * (factor * inverse * (1.0 / (VARS * 8))))
    pair_total = jnp.full((1, 128), 8.0 * math.sqrt(EPSILON), F32)
    for m in range(8):
        for n in range(m + 1, 8):
            difference = fields[m] - fields[n]
            distance, inverse = norm(difference)
            pair_total = pair_total + 2.0 * distance
            pull = difference * (factor * inverse * (1.0 / (VARS * 64)))
            grads[m] = grads[m] - pull
            grads[n] = grads[n] + pull
    for m in range(8):
        g_send[m] = grads[m].astype(BF16)
    g_copies = []
    for rel in rels:
        there = member_of(rel)
        g_copies.append(send(g_send.at[there], g_recv.at[member], (there, grid)))
    g_recv[pl.ds(member, 1)] = g_send[pl.ds(member, 1)]
    loss = true_total * (1.0 / 8) - pair_total * (1.0 / 128)
    loss_recv[pl.ds(member, 1)] = jnp.broadcast_to(loss, (1, 8, 128))
    loss_copies = [
        send(loss_recv.at[member], loss_recv.at[member], (member_of(rel), grid)) for rel in rels]

    arrived(g_copies)
    for t in range(4):
        left, right = g_recv[2 * t].astype(F32), g_recv[2 * t + 1].astype(F32)
        cols = pl.ds(128 * t, 128)
        gl[0:FOLD, cols] = jnp.where(low_lane, left, swap(right)).astype(BF16)
        gl[FOLD:2 * FOLD, cols] = jnp.where(low_lane, swap(left), right).astype(BF16)

    def grad_hidden(r, _):
        rows = pl.ds(pl.multiple_of(r * 128, 128), 128)
        gp[rows, :] = (dot(wop[rows, :], gl[...]) * dgelu[rows, :]).astype(BF16)
        return 0

    lax.fori_loop(0, HID // 128, grad_hidden, 0)

    sib_copies = [None, None]
    for q in (1, 0):
        rows = pl.ds(pl.multiple_of((1 - c) * 512 + q * 256, 256), 256)
        sib_send[q] = dot_nt(lat[rows, :], gp[...]).astype(BF16)
        sib_copies[q] = send(sib_send.at[q], sib_recv.at[q], sibling)
    wo_part[...] = dot_nt(hidden[...], gl[...])
    wo_send[...] = wo_part[pl.ds(pl.multiple_of((1 - c) * 256, 256), 256), :].astype(BF16)
    wo_copy = send(wo_send, wo_recv, sibling)
    ones = jnp.ones((16, COLS), BF16)
    sum_in = dot_nt(ones, gp[...])[0:1]
    sum_out = dot_nt(ones, gl[...])[0:1]
    rows8 = lax.broadcasted_iota(jnp.int32, (8, 128), 0)
    tile = jnp.where(rows8 == 4, sum_out, 0.0)
    for i in range(4):
        tile = jnp.where(rows8 == i, sum_in[:, 128 * i:128 * i + 128], tile)
    sm_c[pl.ds(c, 1)] = tile.reshape(1, 8, 128)
    smc_copy = send(sm_c.at[c], sm_c.at[c], sibling)

    x_cols = pl.ds(pl.multiple_of(x * 128, 128), 128)
    u_rows = pl.ds(pl.multiple_of(u * 32, 32), 32)

    def own_half(q):
        rows = pl.ds(pl.multiple_of(c * 512 + q * 256, 256), 256)
        own[q] = dot_nt(lat[rows, :], gp[...])

    def merge(q):
        sib_copies[q].wait_recv()
        part[q] = (own[q] + sib_recv[q].astype(F32)).astype(BF16)

    own_half(1)
    merge(1)
    u1_copies = []
    for k in FAR8:
        rows = pl.ds(pl.multiple_of((u + k) % 8 * 32, 32), 32)
        u1_copies.append(send(part.at[1, rows], u1_recv.at[k - 1], to_u(k)))
    own_half(0)
    merge(0)
    x0_copies = []
    for k in FAR4:
        cols = pl.ds(pl.multiple_of((x + k) % 4 * 128, 128), 128)
        x0_copies.append(send(part.at[0, :, cols], x0_recv.at[k - 1], to_x(k)))
    wo_copy.wait_recv()
    wo_rs[...] = (
        wo_part[pl.ds(pl.multiple_of(c * 256, 256), 256), :] + wo_recv[...].astype(F32)).astype(BF16)
    wox_copies = []
    for k in FAR4:
        rows = pl.ds(pl.multiple_of((x + k) % 4 * 64, 64), 64)
        wox_copies.append(send(wo_rs.at[rows], wox_recv.at[k - 1], to_x(k)))
    smc_copy.wait_recv()
    sm_x[pl.ds(x, 1)] = (sm_c[0] + sm_c[1]).reshape(1, 8, 128)
    smx_copies = [send(sm_x.at[x], sm_x.at[x], to_x(k)) for k in FAR4]

    arrived(x0_copies)
    total = part[0, :, x_cols].astype(F32)
    for k in range(3):
        total = total + x0_recv[k].astype(F32)
    s0[...] = total.astype(BF16)
    u0_copies = []
    for k in FAR8:
        rows = pl.ds(pl.multiple_of((u + k) % 8 * 32, 32), 32)
        u0_copies.append(send(s0.at[rows], u0_recv.at[k - 1], to_u(k)))
    arrived(wox_copies)
    total = wo_rs[pl.ds(pl.multiple_of(x * 64, 64), 64), :].astype(F32)
    for k in range(3):
        total = total + wox_recv[k].astype(F32)
    wou_src[...] = total
    wou_copies = []
    for k in FAR8:
        rows = pl.ds(pl.multiple_of((u + k) % 8 * 8, 8), 8)
        wou_copies.append(send(wou_src.at[rows], wou_recv.at[k - 1], to_u(k)))
    arrived(smx_copies)
    sm_u[pl.ds(u, 1)] = (sm_x[0] + sm_x[1] + sm_x[2] + sm_x[3]).reshape(1, 8, 128)
    smu_copies = [send(sm_u.at[u], sm_u.at[u], to_u(k)) for k in FAR8]
    arrived(u1_copies)
    total = part[1, u_rows, :].astype(F32)
    for k in range(7):
        total = total + u1_recv[k].astype(F32)
    s1[...] = total.astype(BF16)
    x1_copies = []
    for k in FAR4:
        cols = pl.ds(pl.multiple_of((x + k) % 4 * 128, 128), 128)
        x1_copies.append(send(s1.at[:, cols], x1_recv.at[k - 1], to_x(k)))

    arrived(x1_copies)
    total = s1[:, x_cols].astype(F32)
    for k in range(3):
        total = total + x1_recv[k].astype(F32)
    v1_recv[pl.ds(v, 1)] = total.astype(BF16).reshape(1, 32, 128)
    v1_copies = [send(v1_recv.at[v], v1_recv.at[v], to_v(k)) for k in FAR8]
    arrived(u0_copies)
    total = s0[u_rows, :].astype(F32)
    for k in range(7):
        total = total + u0_recv[k].astype(F32)
    v0_recv[pl.ds(v, 1)] = total.astype(BF16).reshape(1, 32, 128)
    v0_copies = [send(v0_recv.at[v], v0_recv.at[v], to_v(k)) for k in FAR8]
    arrived(wou_copies)
    total = wou_src[pl.ds(pl.multiple_of(u * 8, 8), 8), :]
    for k in range(7):
        total = total + wou_recv[k]
    wov_recv[pl.ds(v, 1)] = total.reshape(1, 8, 128)
    wov_copies = [send(wov_recv.at[v], wov_recv.at[v], to_v(k)) for k in FAR8]
    arrived(smu_copies)
    total = sm_u[0]
    for k in range(1, 8):
        total = total + sm_u[k]
    sm_v[pl.ds(v, 1)] = total.reshape(1, 8, 128)
    smv_copies = [send(sm_v.at[v], sm_v.at[v], to_v(k)) for k in FAR8]

    base = c * 512

    def block(q, rows_at, rows, cols):
        return gw_ref.at[pl.ds(pl.multiple_of(base + q * 256 + rows_at, 32), rows), cols]

    arrived(v1_copies)
    total = v1_recv[0].astype(F32)
    for k in range(1, 8):
        total = total + v1_recv[k].astype(F32)
    spot = block(1, u * 32, 32, x_cols)
    spot[...] = total.astype(BF16)
    x1_copies = [send(spot, spot, to_x(k)) for k in FAR4]
    arrived(v0_copies)
    total = v0_recv[0].astype(F32)
    for k in range(1, 8):
        total = total + v0_recv[k].astype(F32)
    spot = block(0, u * 32, 32, x_cols)
    spot[...] = total.astype(BF16)
    u0_copies = [send(spot, spot, to_u(k)) for k in FAR8]
    arrived(wov_copies)
    total = wov_recv[0]
    for k in range(1, 8):
        total = total + wov_recv[k]
    spot = gwo_ref.at[pl.ds(pl.multiple_of(c * 256 + x * 64 + u * 8, 8), 8)]
    spot[...] = total
    wou_copies = [send(spot, spot, to_u(k)) for k in FAR8]
    arrived(smv_copies)
    total = sm_v[0]
    for k in range(1, 8):
        total = total + sm_v[k]
    small_ref[...] = total

    arrived(x1_copies)
    spot = block(1, u * 32, 32, pl.ds(0, 512))
    u1_copies = [send(spot, spot, to_u(k)) for k in FAR8]
    last = [send(spot, spot, sibling)]
    arrived(u0_copies)
    spot = block(0, 0, 256, x_cols)
    x0_copies = [send(spot, spot, to_x(k)) for k in FAR4]
    last.append(send(spot, spot, sibling))
    arrived(wou_copies)
    spot = gwo_ref.at[pl.ds(pl.multiple_of(c * 256 + x * 64, 64), 64)]
    wox_copies = [send(spot, spot, to_x(k)) for k in FAR4]
    last.append(send(spot, spot, sibling))

    for k, copy in zip(FAR4, x0_copies):
        copy.wait_recv()
        cols = pl.ds(pl.multiple_of((x + 4 - k) % 4 * 128, 128), 128)
        spot = block(0, 0, 256, cols)
        last.append(send(spot, spot, sibling))
    for k, copy in zip(FAR4, wox_copies):
        copy.wait_recv()
        spot = gwo_ref.at[pl.ds(pl.multiple_of(c * 256 + (x + 4 - k) % 4 * 64, 64), 64)]
        last.append(send(spot, spot, sibling))
    for k, copy in zip(FAR8, u1_copies):
        copy.wait_recv()
        spot = block(1, (u + 8 - k) % 8 * 32, 32, pl.ds(0, 512))
        last.append(send(spot, spot, sibling))

    arrived(loss_copies)
    for t in range(4):
        loss_ref[t:t + 1, :] = jnp.where(
            low_row, loss_recv[2 * t, 0:1, :], loss_recv[2 * t + 1, 0:1, :])
    arrived(last)
    for copy in started:
        copy.wait_send()


def per_device(latent, w_in, b_in, output_weight, output_bias, observed_field, area):
    total_columns = latent.shape[2] * lax.axis_size("grid")
    vmem = pl.BlockSpec(memory_space=pltpu.VMEM)
    hbm = pl.BlockSpec(memory_space=pl.ANY)

    def scratch(dtype, *shape):
        return pltpu.VMEM(shape, dtype)

    loss, grad_w_in, small, grad_w_out = pl.pallas_call(
        lambda *refs: kernel(total_columns, *refs),
        out_shape=(
            jax.ShapeDtypeStruct((4, 128), F32),
            jax.ShapeDtypeStruct((DIN, HID), BF16),
            jax.ShapeDtypeStruct((8, 128), F32),
            jax.ShapeDtypeStruct((HID, 128), F32),
        ),
        in_specs=[hbm, hbm, vmem, vmem, vmem, vmem, vmem],
        out_specs=(vmem, vmem, vmem, vmem),
        scratch_shapes=[
            scratch(BF16, DIN, COLS), scratch(BF16, DIN, HID), scratch(BF16, HID, DIN),
            scratch(F32, HID, 128), scratch(F32, HID, COLS), scratch(F32, HID, COLS),
            scratch(BF16, HID, COLS), scratch(BF16, HID, 128), scratch(BF16, 128, HID),
            scratch(F32, 1, 128), scratch(F32, 2 * FOLD, 128),
            scratch(BF16, 2, 2, 2, FOLD, 128), scratch(BF16, 8, FOLD, 128),
            scratch(BF16, 8, FOLD, 128), scratch(BF16, 8, FOLD, 128),
            scratch(F32, 8, 8, 128), scratch(BF16, 128, COLS), scratch(BF16, HID, COLS),
            scratch(BF16, 2, 256, HID), scratch(BF16, 2, 256, HID),
            scratch(F32, 2, 256, HID), scratch(BF16, 2, 256, HID),
            scratch(BF16, 3, 256, 128), scratch(BF16, 256, 128),
            scratch(BF16, 7, 32, 128), scratch(BF16, 8, 32, 128),
            scratch(BF16, 7, 32, HID), scratch(BF16, 32, HID),
            scratch(BF16, 3, 32, 128), scratch(BF16, 8, 32, 128),
            scratch(F32, HID, 128), scratch(BF16, 256, 128), scratch(BF16, 256, 128),
            scratch(BF16, 256, 128), scratch(BF16, 3, 64, 128),
            scratch(F32, 64, 128), scratch(F32, 7, 8, 128), scratch(F32, 8, 8, 128),
            scratch(F32, 2, 8, 128), scratch(F32, 4, 8, 128),
            scratch(F32, 8, 8, 128), scratch(F32, 8, 8, 128),
            pltpu.SemaphoreType.DMA((4,)),
            pltpu.SemaphoreType.DMA((N_SEMS,)), pltpu.SemaphoreType.DMA((N_SEMS,)),
        ],
        compiler_params=pltpu.CompilerParams(
            collective_id=0, has_side_effects=True, vmem_limit_bytes=40 * 2**20),
        cost_estimate=pl.CostEstimate(
            flops=4 * DIN * HID * COLS, bytes_accessed=4 * 2**20, transcendentals=2 * HID * COLS),
        name="energy_score_step",
    )(
        latent, w_in, b_in.reshape(1, HID), output_weight, output_bias.reshape(1, VARS),
        observed_field, area.reshape(1, COLS),
    )
    return (
        loss.reshape(COLS), grad_w_in, small[0:4].reshape(HID), grad_w_out[:, 0:VARS],
        small[4, 0:VARS],
    )


def solution(mesh):
    placed = (P("member", None, "grid"), P(), P(), P(), P(), P(None, "grid"), P("grid"))
    return jax.shard_map(
        per_device,
        mesh=mesh,
        in_specs=placed,
        out_specs=(P("grid"), P(), P(), P(), P()),
        check_vma=False,
    )
```

```python
import math

import jax
import jax.numpy as jnp
from jax import lax
from jax.experimental import pallas as pl
from jax.experimental.pallas import tpu as pltpu
from jax.sharding import PartitionSpec as P

MESH = pl.DeviceIdType.MESH
F32 = jnp.float32
BF16 = jnp.bfloat16
EPSILON = 1e-05
GELU_A = math.sqrt(2.0 / math.pi)
GELU_B = 0.044715

DIN, HID, VARS = 1024, 512, 83
COLS = 512
FOLD = 48
NX, NU = 4, 8
FAR4 = (2, 1, 3)
FAR8 = (4, 3, 5, 2, 6, 1, 7)
N_SEMS = 160


def dot(a, b):
    return jnp.dot(a, b, preferred_element_type=F32)


def dot_nt(a, b):
    return lax.dot_general(a, b, (((1,), (1,)), ((), ())), preferred_element_type=F32)


def dot_tn(a, b):
    return lax.dot_general(a, b, (((0,), (0,)), ((), ())), preferred_element_type=F32)


def kernel(
    total_columns,
    lat_hbm, win_hbm, bin_hbm, wo_hbm, bo_hbm, obs_hbm, area_hbm,
    loss_ref, gw_ref, gbin_ref, gwo_ref, gbo_ref,
    bin_ref, wo_ref, bo_ref, obs_ref, area_ref, gwo,
    lat, win, bias, pre, dgelu, hidden, wop, wop_t, row, obs_pad,
    f_send, f_recv, g_send, g_recv, loss_recv, gl, gp,
    sib_send, sib_recv, own, part,
    x0_recv, s0, u0_recv, u1_recv, s1, x1_recv, v_recv,
    wo_part, wo_send, wo_recv, wo_rs, wox_recv, wou_src, wou_recv, wov_recv,
    sm_c, sm_x,
    local_sems, send_sems, recv_sems,
):
    member, grid = lax.axis_index("member"), lax.axis_index("grid")
    c, zlo = member % 2, member // 2
    a, b = zlo // 2, zlo % 2
    zhi, y, x = grid % 2, (grid // 2) % 8, grid // 16
    z = zhi * 4 + zlo
    u = y * (1 - c) + z * c
    v = z * (1 - c) + y * c

    def device(x, y, z, c):
        return ((z % 4) * 2 + c, (x * 8 + y) * 2 + z // 4)

    def to_x(k):
        return device((x + k) % 4, y, z, c)

    def to_u(k):
        return device(x, (y + k * (1 - c)) % 8, (z + k * c) % 8, c)

    def to_v(k):
        return device(x, (y + k * c) % 8, (z + k * (1 - c)) % 8, c)

    sibling = (zlo * 2 + 1 - c, grid)

    def flip(bit, by):
        return 1 - bit if by else bit

    def member_of(rel):
        ra, rb, rc = rel
        return (2 * flip(a, ra) + flip(b, rb)) * 2 + flip(c, rc)

    rels = [(ra, rb, rc) for ra in (1, 0) for rb in (1, 0) for rc in (1, 0)][:-1]

    started, fences = [], [0, 0]

    def drain():
        for copy in started[fences[-2]:fences[-1]]:
            copy.wait_send()
        fences.append(len(started))

    def send(src, dst, to):
        i = len(started)
        copy = pltpu.make_async_remote_copy(
            src_ref=src, dst_ref=dst, send_sem=send_sems.at[i], recv_sem=recv_sems.at[i],
            device_id=to, device_id_type=MESH,
        )
        copy.start()
        started.append(copy)
        return copy

    def arrived(copies):
        for copy in copies:
            copy.wait_recv()

    barrier = pltpu.get_barrier_semaphore()
    partners = (
        [(member_of(rel), grid) for rel in rels]
        + [to_x(k) for k in FAR4] + [to_u(k) for k in FAR8] + [to_v(k) for k in FAR8]
    )
    for partner in partners:
        pl.semaphore_signal(barrier, inc=1, device_id=partner, device_id_type=MESH)

    halves = [1 - a, a]
    load_w = [
        pltpu.make_async_copy(
            win_hbm.at[pl.ds(512 * i, 512)], win.at[pl.ds(512 * i, 512)], local_sems.at[i])
        for i in range(2)
    ]
    load_l = [
        pltpu.make_async_copy(
            lat_hbm.at[0, :, pl.ds(pl.multiple_of(h * 256, 256), 256)],
            lat.at[:, pl.ds(pl.multiple_of(h * 256, 256), 256)], local_sems.at[2 + i])
        for i, h in enumerate(halves)
    ]
    load_small = [
        pltpu.make_async_copy(src, dst, local_sems.at[4 + i])
        for i, (src, dst) in enumerate((
            (bin_hbm, bin_ref), (wo_hbm, wo_ref), (bo_hbm, bo_ref),
            (obs_hbm, obs_ref), (area_hbm, area_ref)))
    ]
    for copy in load_w + load_small[:3] + load_l + load_small[3:]:
        copy.start()

    wop_t[...] = jnp.zeros_like(wop_t)
    row[...] = jnp.zeros_like(row)
    for copy in load_small[:3]:
        copy.wait()
    for i in range(4):
        bias[pl.ds(128 * i, 128), :] = jnp.transpose(
            jnp.broadcast_to(bin_ref[:, pl.ds(128 * i, 128)], (128, 128)))
    wop_t[0:VARS, :] = wo_ref[...]
    row[:, 0:VARS] = bo_ref[...]
    bias_out = jnp.transpose(jnp.broadcast_to(row[...], (128, 128)))[0:2 * FOLD]
    lane = lax.broadcasted_iota(jnp.int32, (FOLD, 128), 1)
    low_lane = lane < 64
    low_row = lax.broadcasted_iota(jnp.int32, (1, 128), 1) < 64

    def swap(value):
        return pltpu.roll(value, 64, 1)

    for copy in load_w:
        copy.wait()

    f_copies = []
    for i, h in enumerate(halves):
        cols = pl.ds(pl.multiple_of(h * 256, 256), 256)
        load_l[i].wait()
        pre[:, cols] = dot_tn(win[...], lat[:, cols])

        def activate(r, _):
            rows = pl.ds(pl.multiple_of(r * 128, 128), 128)
            shift = bias[rows, :]
            value = pre[rows, cols] + jnp.concatenate([shift, shift], axis=1)
            pre[rows, cols] = value
            inner = GELU_A * (value + GELU_B * (value * value * value))
            hidden[rows, cols] = (0.5 * value * (1.0 + jnp.tanh(inner))).astype(BF16)
            return 0

        lax.fori_loop(0, HID // 128, activate, 0)
        field = dot(wop_t[0:2 * FOLD, :], hidden[:, cols])
        for t in range(2):
            chunk = (field[:, 128 * t:128 * t + 128] + bias_out).astype(BF16).astype(F32)
            lo, hi = chunk[0:FOLD], chunk[FOLD:2 * FOLD]
            f_send[i, t, 0] = jnp.where(low_lane, lo, swap(hi)).astype(BF16)
            f_send[i, t, 1] = jnp.where(low_lane, swap(lo), hi).astype(BF16)
        if i == 0:
            pl.semaphore_wait(barrier, len(partners))
        for rel in rels:
            if rel[0] == 1 - i:
                src = f_send.at[i, flip(b, rel[1]), flip(c, rel[2])]
                f_copies.append(send(src, f_recv.at[member], (member_of(rel), grid)))
    f_recv[pl.ds(member, 1)] = f_send[1, pl.ds(b, 1), pl.ds(c, 1)].reshape(1, FOLD, 128)

    def derive(r, _):
        rows = pl.ds(pl.multiple_of(r * 128, 128), 128)
        value = pre[rows, :]
        square = value * value
        t = jnp.tanh(GELU_A * (value + GELU_B * (value * square)))
        dgelu[rows, :] = 0.5 * (1.0 + t) + (0.5 * GELU_A) * value * (1.0 - t * t) * (
            1.0 + (3.0 * GELU_B) * square)
        return 0

    lax.fori_loop(0, HID // 128, derive, 0)
    wop[...] = jnp.transpose(wop_t[...])
    for copy in load_small[3:]:
        copy.wait()
    obs_pad[...] = jnp.zeros_like(obs_pad)
    own_cols = pl.ds(pl.multiple_of(zlo * 128, 128), 128)
    obs_pad[0:VARS, :] = obs_ref[:, own_cols]
    lo, hi = obs_pad[0:FOLD], obs_pad[FOLD:2 * FOLD]
    first = c == 0
    observed = jnp.where(low_lane, jnp.where(first, lo, swap(lo)), jnp.where(first, swap(hi), hi))
    area = area_ref[:, own_cols]
    area = jnp.where(low_row, jnp.where(first, area, swap(area)), jnp.where(first, swap(area), area))
    factor = area * (VARS * math.sqrt(8 / total_columns))
    gl[2 * FOLD:128, :] = jnp.zeros((128 - 2 * FOLD, COLS), BF16)

    def norm(difference):
        total = jnp.sum(difference * difference, axis=0, keepdims=True)
        square = (total + swap(total)) / VARS + EPSILON
        inverse = lax.rsqrt(square)
        return square * inverse, inverse

    arrived(f_copies)
    fields = [f_recv[i].astype(F32) for i in range(8)]
    grads = []
    true_total = jnp.zeros((1, 128), F32)
    for m in range(8):
        difference = fields[m] - observed
        distance, inverse = norm(difference)
        true_total = true_total + distance
        grads.append(difference * (factor * inverse * (1.0 / (VARS * 8))))
    pair_total = jnp.full((1, 128), 8.0 * math.sqrt(EPSILON), F32)
    for m in range(8):
        for n in range(m + 1, 8):
            difference = fields[m] - fields[n]
            distance, inverse = norm(difference)
            pair_total = pair_total + 2.0 * distance
            pull = difference * (factor * inverse * (1.0 / (VARS * 64)))
            grads[m] = grads[m] - pull
            grads[n] = grads[n] + pull
    for m in range(8):
        g_send[m] = grads[m].astype(BF16)
    g_copies = []
    for rel in rels:
        there = member_of(rel)
        g_copies.append(send(g_send.at[there], g_recv.at[member], (there, grid)))
    g_recv[pl.ds(member, 1)] = g_send[pl.ds(member, 1)]
    loss = true_total * (1.0 / 8) - pair_total * (1.0 / 128)
    loss_recv[pl.ds(member, 1)] = jnp.broadcast_to(loss, (1, 8, 128))
    loss_copies = [
        send(loss_recv.at[member], loss_recv.at[member], (member_of(rel), grid)) for rel in rels]

    drain()
    arrived(g_copies)
    for t in range(4):
        left, right = g_recv[2 * t].astype(F32), g_recv[2 * t + 1].astype(F32)
        cols = pl.ds(128 * t, 128)
        gl[0:FOLD, cols] = jnp.where(low_lane, left, swap(right)).astype(BF16)
        gl[FOLD:2 * FOLD, cols] = jnp.where(low_lane, swap(left), right).astype(BF16)

    def grad_hidden(r, _):
        rows = pl.ds(pl.multiple_of(r * 128, 128), 128)
        gp[rows, :] = (dot(wop[rows, :], gl[...]) * dgelu[rows, :]).astype(BF16)
        return 0

    lax.fori_loop(0, HID // 128, grad_hidden, 0)

    sib_copies = [None, None]
    for q in (1, 0):
        rows = pl.ds(pl.multiple_of((1 - c) * 512 + q * 256, 256), 256)
        sib_send[q] = dot_nt(lat[rows, :], gp[...]).astype(BF16)
        sib_copies[q] = send(sib_send.at[q], sib_recv.at[q], sibling)
    wo_part[...] = dot_nt(hidden[...], gl[...])
    wo_send[...] = wo_part[pl.ds(pl.multiple_of((1 - c) * 256, 256), 256), :].astype(BF16)
    wo_copy = send(wo_send, wo_recv, sibling)
    ones = jnp.ones((16, COLS), BF16)
    sum_in = dot_nt(ones, gp[...])[0:1]
    sum_out = dot_nt(ones, gl[...])[0:1]
    rows8 = lax.broadcasted_iota(jnp.int32, (8, 128), 0)
    tile = jnp.where(rows8 == 4, sum_out, 0.0)
    for i in range(4):
        tile = jnp.where(rows8 == i, sum_in[:, 128 * i:128 * i + 128], tile)
    sm_c[pl.ds(c, 1)] = tile.reshape(1, 8, 128)
    smc_copy = send(sm_c.at[c], sm_c.at[c], sibling)

    x_cols = pl.ds(pl.multiple_of(x * 128, 128), 128)
    u_rows = pl.ds(pl.multiple_of(u * 32, 32), 32)

    def own_half(q):
        rows = pl.ds(pl.multiple_of(c * 512 + q * 256, 256), 256)
        own[q] = dot_nt(lat[rows, :], gp[...])

    def merge(q):
        sib_copies[q].wait_recv()
        part[q] = (own[q] + sib_recv[q].astype(F32)).astype(BF16)

    own_half(1)
    merge(1)
    u1_copies = []
    for k in FAR8:
        rows = pl.ds(pl.multiple_of((u + k) % 8 * 32, 32), 32)
        u1_copies.append(send(part.at[1, rows], u1_recv.at[k - 1], to_u(k)))
    own_half(0)
    merge(0)
    x0_copies = []
    for k in FAR4:
        cols = pl.ds(pl.multiple_of((x + k) % 4 * 128, 128), 128)
        x0_copies.append(send(part.at[0, :, cols], x0_recv.at[k - 1], to_x(k)))
    wo_copy.wait_recv()
    wo_rs[...] = (
        wo_part[pl.ds(pl.multiple_of(c * 256, 256), 256), :] + wo_recv[...].astype(F32)).astype(BF16)
    wox_copies = []
    for k in FAR4:
        rows = pl.ds(pl.multiple_of((x + k) % 4 * 64, 64), 64)
        wox_copies.append(send(wo_rs.at[rows], wox_recv.at[k - 1], to_x(k)))
    smc_copy.wait_recv()
    sm_x[pl.ds(x, 1)] = (sm_c[0] + sm_c[1]).reshape(1, 8, 128)
    smx_copies = [send(sm_x.at[x], sm_x.at[x], to_x(k)) for k in FAR4]

    drain()
    arrived(x0_copies)
    total = part[0, :, x_cols].astype(F32)
    for k in range(3):
        total = total + x0_recv[k].astype(F32)
    s0[...] = total.astype(BF16)
    u0_copies = []
    for k in FAR8:
        rows = pl.ds(pl.multiple_of((u + k) % 8 * 32, 32), 32)
        u0_copies.append(send(s0.at[rows], u0_recv.at[k - 1], to_u(k)))
    arrived(wox_copies)
    total = wo_rs[pl.ds(pl.multiple_of(x * 64, 64), 64), :].astype(F32)
    for k in range(3):
        total = total + wox_recv[k].astype(F32)
    arrived(smx_copies)
    small = sm_x[0] + sm_x[1] + sm_x[2] + sm_x[3]
    for j in range(8):
        wou_src[j, 0:8] = total[8 * j:8 * j + 8]
        wou_src[j, 8:16] = small
    wou_recv[pl.ds(u, 1)] = wou_src[pl.ds(u, 1)]
    wou_copies = [send(wou_src.at[(u + k) % 8], wou_recv.at[u], to_u(k)) for k in FAR8]
    arrived(u1_copies)
    total = part[1, u_rows, :].astype(F32)
    for k in range(7):
        total = total + u1_recv[k].astype(F32)
    s1[...] = total.astype(BF16)
    x1_copies = []
    for k in FAR4:
        cols = pl.ds(pl.multiple_of((x + k) % 4 * 128, 128), 128)
        x1_copies.append(send(s1.at[:, cols], x1_recv.at[k - 1], to_x(k)))

    arrived(x1_copies)
    total = s1[:, x_cols].astype(F32)
    for k in range(3):
        total = total + x1_recv[k].astype(F32)
    v_recv[v, 1] = total.astype(BF16)
    arrived(u0_copies)
    total = s0[u_rows, :].astype(F32)
    for k in range(7):
        total = total + u0_recv[k].astype(F32)
    v_recv[v, 0] = total.astype(BF16)
    v_copies = [send(v_recv.at[v], v_recv.at[v], to_v(k)) for k in FAR8]
    arrived(wou_copies)
    total = wou_recv[0]
    for k in range(1, 8):
        total = total + wou_recv[k]
    wov_recv[pl.ds(v, 1)] = total.reshape(1, 16, 128)
    wov_copies = [send(wov_recv.at[v], wov_recv.at[v], to_v(k)) for k in FAR8]
    drain()

    base = c * 512

    def block(q, rows_at, rows, cols):
        return gw_ref.at[pl.ds(pl.multiple_of(base + q * 256 + rows_at, 32), rows), cols]

    arrived(v_copies)
    total = v_recv[0].astype(F32)
    for k in range(1, 8):
        total = total + v_recv[k].astype(F32)
    total = total.astype(BF16)
    spot1 = block(1, u * 32, 32, x_cols)
    spot1[...] = total[1]
    spot0 = block(0, u * 32, 32, x_cols)
    spot0[...] = total[0]
    u0_copies = [send(spot0, spot0, to_u(k)) for k in FAR8]
    x1_copies = [send(spot1, spot1, to_x(k)) for k in FAR4]
    arrived(wov_copies)
    total = wov_recv[0]
    for k in range(1, 8):
        total = total + wov_recv[k]
    spot = gwo.at[pl.ds(pl.multiple_of(c * 256 + x * 64 + u * 8, 8), 8)]
    spot[...] = total[0:8]
    wou_copies = [send(spot, spot, to_u(k)) for k in FAR8]
    for i in range(4):
        gbin_ref[:, 128 * i:128 * i + 128] = total[8 + i:9 + i]
    gbo_ref[...] = total[12:13, 0:VARS]
    drain()

    arrived(x1_copies)
    spot = block(1, u * 32, 32, pl.ds(0, 512))
    u1_copies = [send(spot, spot, to_u(k)) for k in FAR8]
    last = [send(spot, spot, sibling)]
    arrived(u0_copies)
    spot = block(0, 0, 256, x_cols)
    x0_copies = [send(spot, spot, to_x(k)) for k in FAR4]
    last.append(send(spot, spot, sibling))
    arrived(wou_copies)
    spot = gwo.at[pl.ds(pl.multiple_of(c * 256 + x * 64, 64), 64)]
    wox_copies = [send(spot, spot, to_x(k)) for k in FAR4]
    last_wo = [send(spot, spot, sibling)]

    drain()
    arrived(loss_copies)
    for t in range(4):
        loss_ref[:, 128 * t:128 * t + 128] = jnp.where(
            low_row, loss_recv[2 * t, 0:1, :], loss_recv[2 * t + 1, 0:1, :])

    for k, copy in reversed(list(zip(FAR4, wox_copies))):
        copy.wait_recv()
        spot = gwo.at[pl.ds(pl.multiple_of(c * 256 + (x + 4 - k) % 4 * 64, 64), 64)]
        last_wo.append(send(spot, spot, sibling))
    near_u = [(k, copy, u1_copies) for k, copy in zip(FAR8, u1_copies)][::-1]
    near_x = [(k, copy, x0_copies) for k, copy in zip(FAR4, x0_copies)][::-1]
    for k, copy, group in near_u[:4] + near_x[:2] + near_u[4:] + near_x[2:]:
        copy.wait_recv()
        if group is x0_copies:
            cols = pl.ds(pl.multiple_of((x + 4 - k) % 4 * 128, 128), 128)
            spot = block(0, 0, 256, cols)
        else:
            spot = block(1, (u + 8 - k) % 8 * 32, 32, pl.ds(0, 512))
        last.append(send(spot, spot, sibling))
    arrived(last_wo)
    gwo_ref[...] = jnp.transpose(gwo[...])[0:VARS]
    arrived(last)
    drain()
    drain()


def deliver(*refs):
    results, places, sems = refs[0:5], refs[5:10], refs[10]
    copies = [
        pltpu.make_async_copy(src, dst, sems.at[i])
        for i, (src, dst) in enumerate(zip(results, places))
    ]
    for copy in copies:
        copy.start()
    for copy in copies:
        copy.wait()


def per_device(latent, w_in, b_in, output_weight, output_bias, observed_field, area):
    total_columns = latent.shape[2] * lax.axis_size("grid")
    vmem = pl.BlockSpec(memory_space=pltpu.VMEM)
    hbm = pl.BlockSpec(memory_space=pltpu.HBM)

    def scratch(dtype, *shape):
        return pltpu.VMEM(shape, dtype)

    results = (
        jax.ShapeDtypeStruct((1, COLS), F32),
        jax.ShapeDtypeStruct((DIN, HID), BF16),
        jax.ShapeDtypeStruct((1, HID), F32),
        jax.ShapeDtypeStruct((VARS, HID), F32),
        jax.ShapeDtypeStruct((1, VARS), F32),
    )
    operands = (
        latent, w_in, b_in.reshape(1, HID), output_weight.T, output_bias.reshape(1, VARS),
        observed_field, area.reshape(1, COLS),
    )
    made = pl.pallas_call(
        lambda *refs: kernel(total_columns, *refs),
        out_shape=results,
        in_specs=[hbm] * 7,
        out_specs=(vmem,) * 5,
        scratch_shapes=[
            scratch(F32, 1, HID), scratch(BF16, VARS, HID), scratch(F32, 1, VARS),
            scratch(F32, VARS, COLS), scratch(F32, 1, COLS), scratch(F32, HID, 128),
            scratch(BF16, DIN, COLS), scratch(BF16, DIN, HID),
            scratch(F32, HID, 128), scratch(F32, HID, COLS), scratch(F32, HID, COLS),
            scratch(BF16, HID, COLS), scratch(BF16, HID, 128), scratch(BF16, 128, HID),
            scratch(F32, 1, 128), scratch(F32, 2 * FOLD, 128),
            scratch(BF16, 2, 2, 2, FOLD, 128), scratch(BF16, 8, FOLD, 128),
            scratch(BF16, 8, FOLD, 128), scratch(BF16, 8, FOLD, 128),
            scratch(F32, 8, 8, 128), scratch(BF16, 128, COLS), scratch(BF16, HID, COLS),
            scratch(BF16, 2, 256, HID), scratch(BF16, 2, 256, HID),
            scratch(F32, 2, 256, HID), scratch(BF16, 2, 256, HID),
            scratch(BF16, 3, 256, 128), scratch(BF16, 256, 128),
            scratch(BF16, 7, 32, 128),
            scratch(BF16, 7, 32, HID), scratch(BF16, 32, HID),
            scratch(BF16, 3, 32, 128), scratch(BF16, 8, 2, 32, 128),
            scratch(F32, HID, 128), scratch(BF16, 256, 128), scratch(BF16, 256, 128),
            scratch(BF16, 256, 128), scratch(BF16, 3, 64, 128),
            scratch(F32, 8, 16, 128), scratch(F32, 8, 16, 128), scratch(F32, 8, 16, 128),
            scratch(F32, 2, 8, 128), scratch(F32, 4, 8, 128),
            pltpu.SemaphoreType.DMA((9,)),
            pltpu.SemaphoreType.DMA((N_SEMS,)), pltpu.SemaphoreType.DMA((N_SEMS,)),
        ],
        compiler_params=pltpu.CompilerParams(
            collective_id=0, has_side_effects=True, vmem_limit_bytes=40 * 2**20),
        cost_estimate=pl.CostEstimate(
            flops=4 * DIN * HID * COLS, bytes_accessed=4 * 2**20, transcendentals=2 * HID * COLS),
        name="energy_score_step",
    )(*[pltpu.with_memory_space_constraint(operand, pltpu.HBM) for operand in operands])
    loss, grad_w_in, grad_b_in, grad_w_out, grad_b_out = pl.pallas_call(
        deliver,
        out_shape=results,
        in_specs=[vmem] * 5,
        out_specs=(hbm,) * 5,
        scratch_shapes=[pltpu.SemaphoreType.DMA((5,))],
        name="deliver",
    )(*made)
    return (
        loss.reshape(COLS), grad_w_in, grad_b_in.reshape(HID), grad_w_out.T,
        grad_b_out.reshape(VARS),
    )


def solution(mesh):
    placed = (P("member", None, "grid"), P(), P(), P(), P(), P(None, "grid"), P("grid"))
    return jax.shard_map(
        per_device,
        mesh=mesh,
        in_specs=placed,
        out_specs=(P("grid"), P(), P(), P(), P()),
        check_vma=False,
    )
```

```python
import math

import jax
import jax.numpy as jnp
from jax import lax
from jax.experimental import pallas as pl
from jax.experimental.pallas import tpu as pltpu
from jax.sharding import PartitionSpec as P

MESH = pl.DeviceIdType.MESH
F32 = jnp.float32
BF16 = jnp.bfloat16
EPSILON = 1e-05
GELU_A = math.sqrt(2.0 / math.pi)
GELU_B = 0.044715

DIN, HID, VARS = 1024, 512, 83
COLS = 512
FOLD = 48
NX, NU = 4, 8
FAR4 = (2, 1, 3)
FAR8 = (4, 3, 5, 2, 6, 1, 7)
N_SENDS, N_RECEIVES = 24, 34


def dot(a, b):
    return jnp.dot(a, b, preferred_element_type=F32)


def dot_nt(a, b):
    return lax.dot_general(a, b, (((1,), (1,)), ((), ())), preferred_element_type=F32)


def dot_tn(a, b):
    return lax.dot_general(a, b, (((0,), (0,)), ((), ())), preferred_element_type=F32)


def kernel(
    total_columns,
    lat_hbm, win_hbm, bin_hbm, wo_hbm, bo_hbm, obs_hbm, area_hbm,
    loss_ref, gw_ref, gbin_ref, gwo_ref, gbo_ref,
    bin_ref, wo_ref, bo_ref, obs_ref, area_ref, gwo,
    lat, win, bias, pre, dgelu, hidden, wop, wop_t, row, obs_pad,
    f_send, f_recv, g_send, g_recv, loss_recv, gl, gp,
    sib_send, sib_recv, own, part,
    x0_recv, s0, u0_recv, u1_recv, s1, x1_recv, v_recv,
    wo_part, wo_send, wo_recv, wo_rs, wox_recv, wou_src, wou_recv, wov_recv,
    sm_c, sm_x,
    local_sems, send_sems, recv_sems,
):
    member, grid = lax.axis_index("member"), lax.axis_index("grid")
    c, zlo = member & 1, member >> 1
    a, b = zlo >> 1, zlo & 1
    zhi, y, x = grid & 1, (grid >> 1) & 7, grid >> 4
    z = zhi * 4 + zlo
    on_y = 1 - c
    u = y * on_y + z * c
    v = z * on_y + y * c

    def device(x, y, z):
        return ((z & 3) * 2 + c, (x * 8 + y) * 2 + (z >> 2))

    x_at = [(x + k) & 3 for k in range(4)]
    u_at = [(u + k) & 7 for k in range(8)]
    v_at = [(v + k) & 7 for k in range(8)]
    to_x = [(member, (x_at[k] * 8 + y) * 2 + zhi) for k in range(4)]
    to_u = [device(x, u_at[k] * on_y + y * c, z * on_y + u_at[k] * c) for k in range(8)]
    to_v = [device(x, y * on_y + v_at[k] * c, v_at[k] * on_y + z * c) for k in range(8)]

    sibling = (zlo * 2 + 1 - c, grid)

    def flip(bit, by):
        return 1 - bit if by else bit

    def member_of(rel):
        ra, rb, rc = rel
        return (2 * flip(a, ra) + flip(b, rb)) * 2 + flip(c, rc)

    rels = [(ra, rb, rc) for ra in (1, 0) for rb in (1, 0) for rc in (1, 0)][:-1]

    there = {rel: member_of(rel) for rel in rels}

    groups, fences, received = [], [0, 0], [0]

    class Group:
        def __init__(self, size, apart=0):
            self.size, self.index = size, len(groups)
            self.first, self.apart, self.count = received[0], apart, 0
            received[0] += max(apart, 1)
            groups.append(self)

        def copy(self, src, dst, to, number=0):
            return pltpu.make_async_remote_copy(
                src_ref=src, dst_ref=dst, send_sem=send_sems.at[self.index],
                recv_sem=recv_sems.at[self.first + number], device_id=to, device_id_type=MESH,
            )

        def send(self, src, dst, to):
            copy = self.copy(src, dst, to, self.count if self.apart else 0)
            self.count += 1
            copy.start()
            return copy

        def arrived(self):
            self.copy(self.size, self.size, sibling).wait_recv()

        def left(self):
            self.copy(self.size, self.size, sibling).wait_send()

    def drain():
        for group in groups[fences[-2]:fences[-1]]:
            group.left()
        fences.append(len(groups))

    barrier = pltpu.get_barrier_semaphore()
    partners = (
        [to_u[k] for k in FAR8] + [to_v[k] for k in FAR8]
        + [(there[rel], grid) for rel in rels] + [to_x[k] for k in FAR4]
    )
    for partner in partners:
        pl.semaphore_signal(barrier, inc=1, device_id=partner, device_id_type=MESH)

    halves = [1 - a, a]
    load_w = [
        pltpu.make_async_copy(
            win_hbm.at[pl.ds(512 * i, 512)], win.at[pl.ds(512 * i, 512)], local_sems.at[i])
        for i in range(2)
    ]
    load_l = [
        pltpu.make_async_copy(
            lat_hbm.at[0, :, pl.ds(pl.multiple_of(h * 256, 256), 256)],
            lat.at[:, pl.ds(pl.multiple_of(h * 256, 256), 256)], local_sems.at[2 + i])
        for i, h in enumerate(halves)
    ]
    load_small = [
        pltpu.make_async_copy(src, dst, local_sems.at[4 + i])
        for i, (src, dst) in enumerate((
            (bin_hbm, bin_ref), (wo_hbm, wo_ref), (bo_hbm, bo_ref),
            (obs_hbm, obs_ref), (area_hbm, area_ref)))
    ]
    for copy in load_w + load_small[:3] + load_l + load_small[3:]:
        copy.start()

    wop_t[...] = jnp.zeros_like(wop_t)
    row[...] = jnp.zeros_like(row)
    for copy in load_small[:3]:
        copy.wait()
    for i in range(4):
        bias[pl.ds(128 * i, 128), :] = jnp.transpose(
            jnp.broadcast_to(bin_ref[:, pl.ds(128 * i, 128)], (128, 128)))
    wop_t[0:VARS, :] = wo_ref[...]
    row[:, 0:VARS] = bo_ref[...]
    bias_out = jnp.transpose(jnp.broadcast_to(row[...], (128, 128)))[0:2 * FOLD]
    lane = lax.broadcasted_iota(jnp.int32, (FOLD, 128), 1)
    low_lane = lane < 64
    low_row = lax.broadcasted_iota(jnp.int32, (1, 128), 1) < 64

    def swap(value):
        return pltpu.roll(value, 64, 1)

    for copy in load_w:
        copy.wait()

    f_group = Group(f_recv.at[pl.ds(0, 7)])
    for i, h in enumerate(halves):
        cols = pl.ds(pl.multiple_of(h * 256, 256), 256)
        load_l[i].wait()
        pre[:, cols] = dot_tn(win[...], lat[:, cols])

        def activate(r, _):
            rows = pl.ds(pl.multiple_of(r * 128, 128), 128)
            shift = bias[rows, :]
            value = pre[rows, cols] + jnp.concatenate([shift, shift], axis=1)
            pre[rows, cols] = value
            inner = GELU_A * (value + GELU_B * (value * value * value))
            hidden[rows, cols] = (0.5 * value * (1.0 + jnp.tanh(inner))).astype(BF16)
            return 0

        lax.fori_loop(0, HID // 128, activate, 0)
        field = dot(wop_t[0:2 * FOLD, :], hidden[:, cols])
        for t in range(2):
            chunk = (field[:, 128 * t:128 * t + 128] + bias_out).astype(BF16).astype(F32)
            lo, hi = chunk[0:FOLD], chunk[FOLD:2 * FOLD]
            f_send[i, t, 0] = jnp.where(low_lane, lo, swap(hi)).astype(BF16)
            f_send[i, t, 1] = jnp.where(low_lane, swap(lo), hi).astype(BF16)
        if i == 0:
            pl.semaphore_wait(barrier, len(partners))
        for rel in rels:
            if rel[0] == 1 - i:
                src = f_send.at[i, flip(b, rel[1]), flip(c, rel[2])]
                f_group.send(src, f_recv.at[member], (there[rel], grid))
    f_recv[pl.ds(member, 1)] = f_send[1, pl.ds(b, 1), pl.ds(c, 1)].reshape(1, FOLD, 128)

    def derive(r, _):
        rows = pl.ds(pl.multiple_of(r * 128, 128), 128)
        value = pre[rows, :]
        square = value * value
        t = jnp.tanh(GELU_A * (value + GELU_B * (value * square)))
        dgelu[rows, :] = 0.5 * (1.0 + t) + (0.5 * GELU_A) * value * (1.0 - t * t) * (
            1.0 + (3.0 * GELU_B) * square)
        return 0

    lax.fori_loop(0, HID // 128, derive, 0)
    wop[...] = jnp.transpose(wop_t[...])
    for copy in load_small[3:]:
        copy.wait()
    obs_pad[...] = jnp.zeros_like(obs_pad)
    own_cols = pl.ds(pl.multiple_of(zlo * 128, 128), 128)
    obs_pad[0:VARS, :] = obs_ref[:, own_cols]
    lo, hi = obs_pad[0:FOLD], obs_pad[FOLD:2 * FOLD]
    first = c == 0
    observed = jnp.where(low_lane, jnp.where(first, lo, swap(lo)), jnp.where(first, swap(hi), hi))
    area = area_ref[:, own_cols]
    area = jnp.where(low_row, jnp.where(first, area, swap(area)), jnp.where(first, swap(area), area))
    factor = area * (VARS * math.sqrt(8 / total_columns))
    gl[2 * FOLD:128, :] = jnp.zeros((128 - 2 * FOLD, COLS), BF16)

    def norm(difference):
        total = jnp.sum(difference * difference, axis=0, keepdims=True)
        square = (total + swap(total)) / VARS + EPSILON
        inverse = lax.rsqrt(square)
        return square * inverse, inverse

    f_group.arrived()
    fields = [f_recv[i].astype(F32) for i in range(8)]
    grads = []
    true_total = jnp.zeros((1, 128), F32)
    for m in range(8):
        difference = fields[m] - observed
        distance, inverse = norm(difference)
        true_total = true_total + distance
        grads.append(difference * (factor * inverse * (1.0 / (VARS * 8))))
    pair_total = jnp.full((1, 128), 8.0 * math.sqrt(EPSILON), F32)
    for m in range(8):
        for n in range(m + 1, 8):
            difference = fields[m] - fields[n]
            distance, inverse = norm(difference)
            pair_total = pair_total + 2.0 * distance
            pull = difference * (factor * inverse * (1.0 / (VARS * 64)))
            grads[m] = grads[m] - pull
            grads[n] = grads[n] + pull
    for m in range(8):
        g_send[m] = grads[m].astype(BF16)
    g_group = Group(g_recv.at[pl.ds(0, 7)])
    for rel in rels:
        g_group.send(g_send.at[there[rel]], g_recv.at[member], (there[rel], grid))
    g_recv[pl.ds(member, 1)] = g_send[pl.ds(member, 1)]
    loss = true_total * (1.0 / 8) - pair_total * (1.0 / 128)
    loss_recv[pl.ds(member, 1)] = jnp.broadcast_to(loss, (1, 8, 128))
    loss_group = Group(loss_recv.at[pl.ds(0, 7)])
    for rel in rels:
        loss_group.send(loss_recv.at[member], loss_recv.at[member], (there[rel], grid))

    drain()
    g_group.arrived()
    for t in range(4):
        left, right = g_recv[2 * t].astype(F32), g_recv[2 * t + 1].astype(F32)
        cols = pl.ds(128 * t, 128)
        gl[0:FOLD, cols] = jnp.where(low_lane, left, swap(right)).astype(BF16)
        gl[FOLD:2 * FOLD, cols] = jnp.where(low_lane, swap(left), right).astype(BF16)

    def grad_hidden(r, _):
        rows = pl.ds(pl.multiple_of(r * 128, 128), 128)
        gp[rows, :] = (dot(wop[rows, :], gl[...]) * dgelu[rows, :]).astype(BF16)
        return 0

    lax.fori_loop(0, HID // 128, grad_hidden, 0)

    sib_groups = [Group(sib_recv.at[q]) for q in range(2)]
    for q in (1, 0):
        rows = pl.ds(pl.multiple_of((1 - c) * 512 + q * 256, 256), 256)
        sib_send[q] = dot_nt(lat[rows, :], gp[...]).astype(BF16)
        sib_groups[q].send(sib_send.at[q], sib_recv.at[q], sibling)
    wo_part[...] = dot_nt(hidden[...], gl[...])
    wo_send[...] = wo_part[pl.ds(pl.multiple_of((1 - c) * 256, 256), 256), :].astype(BF16)
    wo_group = Group(wo_recv)
    wo_group.send(wo_send, wo_recv, sibling)
    ones = jnp.ones((16, COLS), BF16)
    sum_in = dot_nt(ones, gp[...])[0:1]
    sum_out = dot_nt(ones, gl[...])[0:1]
    rows8 = lax.broadcasted_iota(jnp.int32, (8, 128), 0)
    tile = jnp.where(rows8 == 4, sum_out, 0.0)
    for i in range(4):
        tile = jnp.where(rows8 == i, sum_in[:, 128 * i:128 * i + 128], tile)
    sm_c[pl.ds(c, 1)] = tile.reshape(1, 8, 128)
    smc_group = Group(sm_c.at[0])
    smc_group.send(sm_c.at[c], sm_c.at[c], sibling)

    x_cols = pl.ds(pl.multiple_of(x * 128, 128), 128)
    u_rows = pl.ds(pl.multiple_of(u * 32, 32), 32)

    def own_half(q):
        rows = pl.ds(pl.multiple_of(c * 512 + q * 256, 256), 256)
        own[q] = dot_nt(lat[rows, :], gp[...])

    def merge(q):
        sib_groups[q].arrived()
        part[q] = (own[q] + sib_recv[q].astype(F32)).astype(BF16)

    own_half(1)
    merge(1)
    u1_group = Group(u1_recv)
    for k in FAR8:
        rows = pl.ds(pl.multiple_of(u_at[k] * 32, 32), 32)
        u1_group.send(part.at[1, rows], u1_recv.at[k - 1], to_u[k])
    own_half(0)
    merge(0)
    x0_group = Group(x0_recv)
    for k in FAR4:
        cols = pl.ds(pl.multiple_of(x_at[k] * 128, 128), 128)
        x0_group.send(part.at[0, :, cols], x0_recv.at[k - 1], to_x[k])
    wo_group.arrived()
    wo_rs[...] = (
        wo_part[pl.ds(pl.multiple_of(c * 256, 256), 256), :] + wo_recv[...].astype(F32)).astype(BF16)
    wox_group = Group(wox_recv)
    for k in FAR4:
        rows = pl.ds(pl.multiple_of(x_at[k] * 64, 64), 64)
        wox_group.send(wo_rs.at[rows], wox_recv.at[k - 1], to_x[k])
    smc_group.arrived()
    sm_x[pl.ds(x, 1)] = (sm_c[0] + sm_c[1]).reshape(1, 8, 128)
    smx_group = Group(sm_x.at[pl.ds(0, 3)])
    for k in FAR4:
        smx_group.send(sm_x.at[x], sm_x.at[x], to_x[k])

    drain()
    x0_group.arrived()
    total = part[0, :, x_cols].astype(F32)
    for k in range(3):
        total = total + x0_recv[k].astype(F32)
    s0[...] = total.astype(BF16)
    u0_group = Group(u0_recv)
    for k in FAR8:
        rows = pl.ds(pl.multiple_of(u_at[k] * 32, 32), 32)
        u0_group.send(s0.at[rows], u0_recv.at[k - 1], to_u[k])
    wox_group.arrived()
    total = wo_rs[pl.ds(pl.multiple_of(x * 64, 64), 64), :].astype(F32)
    for k in range(3):
        total = total + wox_recv[k].astype(F32)
    smx_group.arrived()
    small = sm_x[0] + sm_x[1] + sm_x[2] + sm_x[3]
    for j in range(8):
        wou_src[j, 0:8] = total[8 * j:8 * j + 8]
        wou_src[j, 8:16] = small
    wou_recv[pl.ds(u, 1)] = wou_src[pl.ds(u, 1)]
    wou_group = Group(wou_recv.at[pl.ds(0, 7)])
    for k in FAR8:
        wou_group.send(wou_src.at[u_at[k]], wou_recv.at[u], to_u[k])
    u1_group.arrived()
    total = part[1, u_rows, :].astype(F32)
    for k in range(7):
        total = total + u1_recv[k].astype(F32)
    s1[...] = total.astype(BF16)
    x1_group = Group(x1_recv)
    for k in FAR4:
        cols = pl.ds(pl.multiple_of(x_at[k] * 128, 128), 128)
        x1_group.send(s1.at[:, cols], x1_recv.at[k - 1], to_x[k])

    x1_group.arrived()
    total = s1[:, x_cols].astype(F32)
    for k in range(3):
        total = total + x1_recv[k].astype(F32)
    v_recv[v, 1] = total.astype(BF16)
    u0_group.arrived()
    total = s0[u_rows, :].astype(F32)
    for k in range(7):
        total = total + u0_recv[k].astype(F32)
    v_recv[v, 0] = total.astype(BF16)
    v_group = Group(v_recv.at[pl.ds(0, 7)])
    for k in FAR8:
        v_group.send(v_recv.at[v], v_recv.at[v], to_v[k])
    wou_group.arrived()
    total = wou_recv[0]
    for k in range(1, 8):
        total = total + wou_recv[k]
    wov_recv[pl.ds(v, 1)] = total.reshape(1, 16, 128)
    wov_group = Group(wov_recv.at[pl.ds(0, 7)])
    for k in FAR8:
        wov_group.send(wov_recv.at[v], wov_recv.at[v], to_v[k])
    drain()

    base = c * 512

    def block(q, rows_at, rows, cols):
        return gw_ref.at[pl.ds(pl.multiple_of(base + q * 256 + rows_at, 32), rows), cols]

    v_group.arrived()
    total = v_recv[0].astype(F32)
    for k in range(1, 8):
        total = total + v_recv[k].astype(F32)
    total = total.astype(BF16)
    spot1 = block(1, u * 32, 32, x_cols)
    spot1[...] = total[1]
    spot0 = block(0, u * 32, 32, x_cols)
    spot0[...] = total[0]
    u0_group = Group(u0_recv)
    for k in FAR8:
        u0_group.send(spot0, spot0, to_u[k])
    x1_group = Group(x1_recv)
    for k in FAR4:
        x1_group.send(spot1, spot1, to_x[k])
    wov_group.arrived()
    total = wov_recv[0]
    for k in range(1, 8):
        total = total + wov_recv[k]
    spot = gwo.at[pl.ds(pl.multiple_of(c * 256 + x * 64 + u * 8, 8), 8)]
    spot[...] = total[0:8]
    wou_group = Group(loss_recv.at[pl.ds(0, 7)])
    for k in FAR8:
        wou_group.send(spot, spot, to_u[k])
    for i in range(4):
        gbin_ref[:, 128 * i:128 * i + 128] = total[8 + i:9 + i]
    gbo_ref[...] = total[12:13, 0:VARS]
    drain()

    x1_group.arrived()
    spot = block(1, u * 32, 32, pl.ds(0, 512))
    u1_group = Group(u1_recv, apart=7)
    u1_copies = [u1_group.send(spot, spot, to_u[k]) for k in FAR8]
    last = Group(part)
    last.send(spot, spot, sibling)
    u0_group.arrived()
    spot = block(0, 0, 256, x_cols)
    x0_group = Group(x0_recv, apart=3)
    x0_copies = [x0_group.send(spot, spot, to_x[k]) for k in FAR4]
    last.send(spot, spot, sibling)
    wou_group.arrived()
    spot = gwo.at[pl.ds(pl.multiple_of(c * 256 + x * 64, 64), 64)]
    wox_group = Group(gwo.at[pl.ds(0, 192)], apart=3)
    wox_copies = [wox_group.send(spot, spot, to_x[k]) for k in FAR4]
    last_wo = Group(gwo.at[pl.ds(0, 256)])
    last_wo.send(spot, spot, sibling)

    drain()
    loss_group.arrived()
    for t in range(4):
        loss_ref[:, 128 * t:128 * t + 128] = jnp.where(
            low_row, loss_recv[2 * t, 0:1, :], loss_recv[2 * t + 1, 0:1, :])

    for k, copy in reversed(list(zip(FAR4, wox_copies))):
        copy.wait_recv()
        spot = gwo.at[pl.ds(pl.multiple_of(c * 256 + x_at[4 - k] * 64, 64), 64)]
        last_wo.send(spot, spot, sibling)
    near_u = [(k, copy, u1_copies) for k, copy in zip(FAR8, u1_copies)][::-1]
    near_x = [(k, copy, x0_copies) for k, copy in zip(FAR4, x0_copies)][::-1]
    for k, copy, group in near_u[:4] + near_x[:2] + near_u[4:] + near_x[2:]:
        copy.wait_recv()
        if group is x0_copies:
            cols = pl.ds(pl.multiple_of(x_at[4 - k] * 128, 128), 128)
            spot = block(0, 0, 256, cols)
        else:
            spot = block(1, u_at[8 - k] * 32, 32, pl.ds(0, 512))
        last.send(spot, spot, sibling)
    last_wo.arrived()
    gwo_ref[...] = jnp.transpose(gwo[...])[0:VARS]
    last.arrived()
    drain()
    drain()
    assert len(groups) == N_SENDS and received[0] == N_RECEIVES


def deliver(*refs):
    results, places, sems = refs[0:5], refs[5:10], refs[10]
    copies = [
        pltpu.make_async_copy(src, dst, sems.at[i])
        for i, (src, dst) in enumerate(zip(results, places))
    ]
    for copy in copies:
        copy.start()
    for copy in copies:
        copy.wait()


def per_device(latent, w_in, b_in, output_weight, output_bias, observed_field, area):
    total_columns = latent.shape[2] * lax.axis_size("grid")
    vmem = pl.BlockSpec(memory_space=pltpu.VMEM)
    hbm = pl.BlockSpec(memory_space=pltpu.HBM)

    def scratch(dtype, *shape):
        return pltpu.VMEM(shape, dtype)

    results = (
        jax.ShapeDtypeStruct((1, COLS), F32),
        jax.ShapeDtypeStruct((DIN, HID), BF16),
        jax.ShapeDtypeStruct((1, HID), F32),
        jax.ShapeDtypeStruct((VARS, HID), F32),
        jax.ShapeDtypeStruct((1, VARS), F32),
    )
    operands = (
        latent, w_in, b_in.reshape(1, HID), output_weight.T, output_bias.reshape(1, VARS),
        observed_field, area.reshape(1, COLS),
    )
    made = pl.pallas_call(
        lambda *refs: kernel(total_columns, *refs),
        out_shape=results,
        in_specs=[hbm] * 7,
        out_specs=(vmem,) * 5,
        scratch_shapes=[
            scratch(F32, 1, HID), scratch(BF16, VARS, HID), scratch(F32, 1, VARS),
            scratch(F32, VARS, COLS), scratch(F32, 1, COLS), scratch(F32, HID, 128),
            scratch(BF16, DIN, COLS), scratch(BF16, DIN, HID),
            scratch(F32, HID, 128), scratch(F32, HID, COLS), scratch(F32, HID, COLS),
            scratch(BF16, HID, COLS), scratch(BF16, HID, 128), scratch(BF16, 128, HID),
            scratch(F32, 1, 128), scratch(F32, 2 * FOLD, 128),
            scratch(BF16, 2, 2, 2, FOLD, 128), scratch(BF16, 8, FOLD, 128),
            scratch(BF16, 8, FOLD, 128), scratch(BF16, 8, FOLD, 128),
            scratch(F32, 8, 8, 128), scratch(BF16, 128, COLS), scratch(BF16, HID, COLS),
            scratch(BF16, 2, 256, HID), scratch(BF16, 2, 256, HID),
            scratch(F32, 2, 256, HID), scratch(BF16, 2, 256, HID),
            scratch(BF16, 3, 256, 128), scratch(BF16, 256, 128),
            scratch(BF16, 7, 32, 128),
            scratch(BF16, 7, 32, HID), scratch(BF16, 32, HID),
            scratch(BF16, 3, 32, 128), scratch(BF16, 8, 2, 32, 128),
            scratch(F32, HID, 128), scratch(BF16, 256, 128), scratch(BF16, 256, 128),
            scratch(BF16, 256, 128), scratch(BF16, 3, 64, 128),
            scratch(F32, 8, 16, 128), scratch(F32, 8, 16, 128), scratch(F32, 8, 16, 128),
            scratch(F32, 2, 8, 128), scratch(F32, 4, 8, 128),
            pltpu.SemaphoreType.DMA((9,)),
            pltpu.SemaphoreType.DMA((N_SENDS,)), pltpu.SemaphoreType.DMA((N_RECEIVES,)),
        ],
        compiler_params=pltpu.CompilerParams(
            collective_id=0, has_side_effects=True, vmem_limit_bytes=40 * 2**20),
        cost_estimate=pl.CostEstimate(
            flops=4 * DIN * HID * COLS, bytes_accessed=4 * 2**20, transcendentals=2 * HID * COLS),
        name="energy_score_step",
    )(*[pltpu.with_memory_space_constraint(operand, pltpu.HBM) for operand in operands])
    loss, grad_w_in, grad_b_in, grad_w_out, grad_b_out = pl.pallas_call(
        deliver,
        out_shape=results,
        in_specs=[vmem] * 5,
        out_specs=(hbm,) * 5,
        scratch_shapes=[pltpu.SemaphoreType.DMA((5,))],
        compiler_params=pltpu.CompilerParams(vmem_limit_bytes=4 * 2**20),
        name="deliver",
    )(*made)
    return (
        loss.reshape(COLS), grad_w_in, grad_b_in.reshape(HID), grad_w_out.T,
        grad_b_out.reshape(VARS),
    )


def solution(mesh):
    placed = (P("member", None, "grid"), P(), P(), P(), P(), P(None, "grid"), P("grid"))
    return jax.shard_map(
        per_device,
        mesh=mesh,
        in_specs=placed,
        out_specs=(P("grid"), P(), P(), P(), P()),
        check_vma=False,
    )
```

```python
import math

import jax
import jax.numpy as jnp
from jax import lax
from jax.experimental import pallas as pl
from jax.experimental.pallas import tpu as pltpu
from jax.sharding import PartitionSpec as P

MESH = pl.DeviceIdType.MESH
F32 = jnp.float32
BF16 = jnp.bfloat16
EPSILON = 1e-05
GELU_A = math.sqrt(2.0 / math.pi)
GELU_B = 0.044715

DIN, HID, VARS = 1024, 512, 83
COLS = 512
FOLD = 48
NX, NU = 4, 8
FAR4 = (2, 1, 3)
FAR8 = (4, 3, 5, 2, 6, 1, 7)
N_SENDS, N_RECEIVES = 24, 34


def dot(a, b):
    return jnp.dot(a, b, preferred_element_type=F32)


def dot_nt(a, b):
    return lax.dot_general(a, b, (((1,), (1,)), ((), ())), preferred_element_type=F32)


def dot_tn(a, b):
    return lax.dot_general(a, b, (((0,), (0,)), ((), ())), preferred_element_type=F32)


def kernel(
    total_columns,
    lat_hbm, win_hbm, bin_hbm, wo_hbm, bo_hbm, obs_hbm, area_hbm,
    loss_ref, gw_ref, gbin_ref, gwo_ref, gbo_ref,
    bin_ref, wo_ref, bo_ref, obs_ref, area_ref, gwo, gwo_low,
    lat, win, bias, pre, dgelu, hidden, wop, wop_t, row, obs_pad,
    f_send, f_recv, g_send, g_recv, loss_recv, gl, gp,
    sib_send, sib_recv, own, part,
    x0_recv, s0, u0_recv, u1_recv, s1, x1_recv, v_recv,
    wo_part, wo_send, wo_recv, wo_rs, wox_recv, wou_src, wou_recv, wov_recv,
    sm_c, sm_x,
    local_sems, send_sems, recv_sems,
):
    member, grid = lax.axis_index("member"), lax.axis_index("grid")
    c, zlo = member & 1, member >> 1
    a, b = zlo >> 1, zlo & 1
    zhi, y, x = grid & 1, (grid >> 1) & 7, grid >> 4
    z = zhi * 4 + zlo
    on_y = 1 - c
    u = y * on_y + z * c
    v = z * on_y + y * c

    def device(x, y, z):
        return ((z & 3) * 2 + c, (x * 8 + y) * 2 + (z >> 2))

    x_at = [(x + k) & 3 for k in range(4)]
    u_at = [(u + k) & 7 for k in range(8)]
    v_at = [(v + k) & 7 for k in range(8)]
    to_x = [(member, (x_at[k] * 8 + y) * 2 + zhi) for k in range(4)]
    to_u = [device(x, u_at[k] * on_y + y * c, z * on_y + u_at[k] * c) for k in range(8)]
    to_v = [device(x, y * on_y + v_at[k] * c, v_at[k] * on_y + z * c) for k in range(8)]

    sibling = (zlo * 2 + 1 - c, grid)

    def flip(bit, by):
        return 1 - bit if by else bit

    def member_of(rel):
        ra, rb, rc = rel
        return (2 * flip(a, ra) + flip(b, rb)) * 2 + flip(c, rc)

    rels = [(ra, rb, rc) for ra in (1, 0) for rb in (1, 0) for rc in (1, 0)][:-1]

    there = {rel: member_of(rel) for rel in rels}

    groups, fences, received = [], [0, 0], [0]

    class Group:
        def __init__(self, size, apart=0):
            self.size, self.index = size, len(groups)
            self.first, self.apart, self.count = received[0], apart, 0
            received[0] += max(apart, 1)
            groups.append(self)

        def copy(self, src, dst, to, number=0):
            return pltpu.make_async_remote_copy(
                src_ref=src, dst_ref=dst, send_sem=send_sems.at[self.index],
                recv_sem=recv_sems.at[self.first + number], device_id=to, device_id_type=MESH,
            )

        def send(self, src, dst, to):
            copy = self.copy(src, dst, to, self.count if self.apart else 0)
            self.count += 1
            copy.start()
            return copy

        def arrived(self):
            self.copy(self.size, self.size, sibling).wait_recv()

        def left(self):
            self.copy(self.size, self.size, sibling).wait_send()

    def drain():
        for group in groups[fences[-2]:fences[-1]]:
            group.left()
        fences.append(len(groups))

    halves = [1 - a, a]
    load_w = [
        pltpu.make_async_copy(
            win_hbm.at[pl.ds(512 * i, 512)], win.at[pl.ds(512 * i, 512)], local_sems.at[i])
        for i in range(2)
    ]
    load_l = [
        pltpu.make_async_copy(
            lat_hbm.at[0, :, pl.ds(pl.multiple_of(h * 256, 256), 256)],
            lat.at[:, pl.ds(pl.multiple_of(h * 256, 256), 256)], local_sems.at[2 + i])
        for i, h in enumerate(halves)
    ]
    load_small = [
        pltpu.make_async_copy(src, dst, local_sems.at[4 + i])
        for i, (src, dst) in enumerate((
            (bin_hbm, bin_ref), (wo_hbm, wo_ref), (bo_hbm, bo_ref),
            (obs_hbm, obs_ref), (area_hbm, area_ref)))
    ]
    for copy in load_w + load_l[:1] + load_small[:3]:
        copy.start()

    barrier = pltpu.get_barrier_semaphore()
    far, near = rels[:4], rels[4:]
    partners = (
        [way[k] for k in (4, 3, 5) for way in (to_u, to_v)] + [(there[rel], grid) for rel in far]
        + [way[k] for k in (2, 6) for way in (to_u, to_v)] + [to_x[2]]
        + [(there[rel], grid) for rel in near]
        + [way[k] for k in (1, 7) for way in (to_u, to_v)] + [to_x[1], to_x[3]]
    )
    for partner in partners:
        pl.semaphore_signal(barrier, inc=1, device_id=partner, device_id_type=MESH)
    for copy in load_l[1:] + load_small[3:]:
        copy.start()

    wop_t[...] = jnp.zeros_like(wop_t)
    row[...] = jnp.zeros_like(row)
    for copy in load_small[:3]:
        copy.wait()
    for i in range(4):
        bias[pl.ds(128 * i, 128), :] = jnp.transpose(
            jnp.broadcast_to(bin_ref[:, pl.ds(128 * i, 128)], (128, 128)))
    wop_t[0:VARS, :] = wo_ref[...]
    row[:, 0:VARS] = bo_ref[...]
    bias_out = jnp.transpose(jnp.broadcast_to(row[...], (128, 128)))[0:2 * FOLD]
    lane = lax.broadcasted_iota(jnp.int32, (FOLD, 128), 1)
    low_lane = lane < 64
    low_row = lax.broadcasted_iota(jnp.int32, (1, 128), 1) < 64

    def swap(value):
        return pltpu.roll(value, 64, 1)

    for copy in load_w:
        copy.wait()

    f_group = Group(f_recv.at[pl.ds(0, 7)])
    for i, h in enumerate(halves):
        cols = pl.ds(pl.multiple_of(h * 256, 256), 256)
        load_l[i].wait()
        pre[:, cols] = dot_tn(win[...], lat[:, cols])

        def activate(r, _):
            rows = pl.ds(pl.multiple_of(r * 128, 128), 128)
            shift = bias[rows, :]
            value = pre[rows, cols] + jnp.concatenate([shift, shift], axis=1)
            pre[rows, cols] = value
            inner = GELU_A * (value + GELU_B * (value * value * value))
            hidden[rows, cols] = (0.5 * value * (1.0 + jnp.tanh(inner))).astype(BF16)
            return 0

        lax.fori_loop(0, HID // 128, activate, 0)
        field = dot(wop_t[0:2 * FOLD, :], hidden[:, cols])
        for t in range(2):
            chunk = (field[:, 128 * t:128 * t + 128] + bias_out).astype(BF16).astype(F32)
            lo, hi = chunk[0:FOLD], chunk[FOLD:2 * FOLD]
            f_send[i, t, 0] = jnp.where(low_lane, lo, swap(hi)).astype(BF16)
            f_send[i, t, 1] = jnp.where(low_lane, swap(lo), hi).astype(BF16)
        if i == 0:
            pl.semaphore_wait(barrier, len(partners))
        for rel in rels:
            if rel[0] == 1 - i:
                src = f_send.at[i, flip(b, rel[1]), flip(c, rel[2])]
                f_group.send(src, f_recv.at[member], (there[rel], grid))
    f_recv[pl.ds(member, 1)] = f_send[1, pl.ds(b, 1), pl.ds(c, 1)].reshape(1, FOLD, 128)

    def derive(r, _):
        rows = pl.ds(pl.multiple_of(r * 128, 128), 128)
        value = pre[rows, :]
        square = value * value
        t = jnp.tanh(GELU_A * (value + GELU_B * (value * square)))
        dgelu[rows, :] = 0.5 * (1.0 + t) + (0.5 * GELU_A) * value * (1.0 - t * t) * (
            1.0 + (3.0 * GELU_B) * square)
        return 0

    lax.fori_loop(0, HID // 128, derive, 0)
    wop[...] = jnp.transpose(wop_t[...])
    for copy in load_small[3:]:
        copy.wait()
    obs_pad[...] = jnp.zeros_like(obs_pad)
    own_cols = pl.ds(pl.multiple_of(zlo * 128, 128), 128)
    obs_pad[0:VARS, :] = obs_ref[:, own_cols]
    lo, hi = obs_pad[0:FOLD], obs_pad[FOLD:2 * FOLD]
    first = c == 0
    observed = jnp.where(low_lane, jnp.where(first, lo, swap(lo)), jnp.where(first, swap(hi), hi))
    area = area_ref[:, own_cols]
    area = jnp.where(low_row, jnp.where(first, area, swap(area)), jnp.where(first, swap(area), area))
    factor = area * (VARS * math.sqrt(8 / total_columns))
    gl[2 * FOLD:128, :] = jnp.zeros((128 - 2 * FOLD, COLS), BF16)

    def norm(difference):
        total = jnp.sum(difference * difference, axis=0, keepdims=True)
        square = (total + swap(total)) / VARS + EPSILON
        inverse = lax.rsqrt(square)
        return square * inverse, inverse

    f_group.arrived()
    fields = [f_recv[i].astype(F32) for i in range(8)]
    grads = []
    true_total = jnp.zeros((1, 128), F32)
    for m in range(8):
        difference = fields[m] - observed
        distance, inverse = norm(difference)
        true_total = true_total + distance
        grads.append(difference * (factor * inverse * (1.0 / (VARS * 8))))
    pair_total = jnp.full((1, 128), 8.0 * math.sqrt(EPSILON), F32)
    for m in range(8):
        for n in range(m + 1, 8):
            difference = fields[m] - fields[n]
            distance, inverse = norm(difference)
            pair_total = pair_total + 2.0 * distance
            pull = difference * (factor * inverse * (1.0 / (VARS * 64)))
            grads[m] = grads[m] - pull
            grads[n] = grads[n] + pull
    for m in range(8):
        g_send[m] = grads[m].astype(BF16)
    g_group = Group(g_recv.at[pl.ds(0, 7)])
    for rel in rels:
        g_group.send(g_send.at[there[rel]], g_recv.at[member], (there[rel], grid))
    g_recv[pl.ds(member, 1)] = g_send[pl.ds(member, 1)]
    loss = true_total * (1.0 / 8) - pair_total * (1.0 / 128)
    loss_recv[pl.ds(member, 1)] = jnp.broadcast_to(loss, (1, 8, 128))
    loss_group = Group(loss_recv.at[pl.ds(0, 7)])
    for rel in rels:
        loss_group.send(loss_recv.at[member], loss_recv.at[member], (there[rel], grid))

    drain()
    g_group.arrived()
    for t in range(4):
        left, right = g_recv[2 * t].astype(F32), g_recv[2 * t + 1].astype(F32)
        cols = pl.ds(128 * t, 128)
        gl[0:FOLD, cols] = jnp.where(low_lane, left, swap(right)).astype(BF16)
        gl[FOLD:2 * FOLD, cols] = jnp.where(low_lane, swap(left), right).astype(BF16)

    def grad_hidden(r, _):
        rows = pl.ds(pl.multiple_of(r * 128, 128), 128)
        gp[rows, :] = (dot(wop[rows, :], gl[...]) * dgelu[rows, :]).astype(BF16)
        return 0

    lax.fori_loop(0, HID // 128, grad_hidden, 0)

    sib_groups = [Group(sib_recv.at[q]) for q in range(2)]
    for q in range(2):
        rows = pl.ds(pl.multiple_of((1 - c) * 512 + q * 256, 256), 256)
        sib_send[q] = dot_nt(lat[rows, :], gp[...]).astype(BF16)
        sib_groups[q].send(sib_send.at[q], sib_recv.at[q], sibling)
    wo_part[...] = dot_nt(hidden[...], gl[...])
    wo_send[...] = wo_part[pl.ds(pl.multiple_of((1 - c) * 256, 256), 256), :].astype(BF16)
    wo_group = Group(wo_recv)
    wo_group.send(wo_send, wo_recv, sibling)
    ones = jnp.ones((16, COLS), BF16)
    sum_in = dot_nt(ones, gp[...])[0:1]
    sum_out = dot_nt(ones, gl[...])[0:1]
    rows8 = lax.broadcasted_iota(jnp.int32, (8, 128), 0)
    tile = jnp.where(rows8 == 4, sum_out, 0.0)
    for i in range(4):
        tile = jnp.where(rows8 == i, sum_in[:, 128 * i:128 * i + 128], tile)
    sm_c[pl.ds(c, 1)] = tile.reshape(1, 8, 128)
    smc_group = Group(sm_c.at[0])
    smc_group.send(sm_c.at[c], sm_c.at[c], sibling)

    x_cols = pl.ds(pl.multiple_of(x * 128, 128), 128)
    u_rows = pl.ds(pl.multiple_of(u * 32, 32), 32)

    def own_half(q):
        rows = pl.ds(pl.multiple_of(c * 512 + q * 256, 256), 256)
        own[q] = dot_nt(lat[rows, :], gp[...])

    def merge(q):
        sib_groups[q].arrived()
        part[q] = (own[q] + sib_recv[q].astype(F32)).astype(BF16)

    own_half(0)
    own_half(1)
    merge(0)
    x0_group = Group(x0_recv)
    for k in FAR4:
        cols = pl.ds(pl.multiple_of(x_at[k] * 128, 128), 128)
        x0_group.send(part.at[0, :, cols], x0_recv.at[k - 1], to_x[k])
    merge(1)
    u1_group = Group(u1_recv)
    for k in FAR8:
        rows = pl.ds(pl.multiple_of(u_at[k] * 32, 32), 32)
        u1_group.send(part.at[1, rows], u1_recv.at[k - 1], to_u[k])
    wo_group.arrived()
    wo_rs[...] = (
        wo_part[pl.ds(pl.multiple_of(c * 256, 256), 256), :] + wo_recv[...].astype(F32)).astype(BF16)
    wox_group = Group(wox_recv)
    for k in FAR4:
        rows = pl.ds(pl.multiple_of(x_at[k] * 64, 64), 64)
        wox_group.send(wo_rs.at[rows], wox_recv.at[k - 1], to_x[k])
    smc_group.arrived()
    sm_x[pl.ds(x, 1)] = (sm_c[0] + sm_c[1]).reshape(1, 8, 128)
    smx_group = Group(sm_x.at[pl.ds(0, 3)])
    for k in FAR4:
        smx_group.send(sm_x.at[x], sm_x.at[x], to_x[k])

    drain()
    x0_group.arrived()
    total = part[0, :, x_cols].astype(F32)
    for k in range(3):
        total = total + x0_recv[k].astype(F32)
    s0[...] = total.astype(BF16)
    u0_group = Group(u0_recv)
    for k in FAR8:
        rows = pl.ds(pl.multiple_of(u_at[k] * 32, 32), 32)
        u0_group.send(s0.at[rows], u0_recv.at[k - 1], to_u[k])
    wox_group.arrived()
    total = wo_rs[pl.ds(pl.multiple_of(x * 64, 64), 64), :].astype(F32)
    for k in range(3):
        total = total + wox_recv[k].astype(F32)
    smx_group.arrived()
    small = sm_x[0] + sm_x[1] + sm_x[2] + sm_x[3]
    for j in range(8):
        wou_src[j, 0:8] = total[8 * j:8 * j + 8]
        wou_src[j, 8:16] = small
    wou_recv[pl.ds(u, 1)] = wou_src[pl.ds(u, 1)]
    wou_group = Group(wou_recv.at[pl.ds(0, 7)])
    for k in FAR8:
        wou_group.send(wou_src.at[u_at[k]], wou_recv.at[u], to_u[k])
    u1_group.arrived()
    total = part[1, u_rows, :].astype(F32)
    for k in range(7):
        total = total + u1_recv[k].astype(F32)
    s1[...] = total.astype(BF16)
    x1_group = Group(x1_recv)
    for k in FAR4:
        cols = pl.ds(pl.multiple_of(x_at[k] * 128, 128), 128)
        x1_group.send(s1.at[:, cols], x1_recv.at[k - 1], to_x[k])

    x1_group.arrived()
    total = s1[:, x_cols].astype(F32)
    for k in range(3):
        total = total + x1_recv[k].astype(F32)
    v_recv[v, 1] = total.astype(BF16)
    u0_group.arrived()
    total = s0[u_rows, :].astype(F32)
    for k in range(7):
        total = total + u0_recv[k].astype(F32)
    v_recv[v, 0] = total.astype(BF16)
    v_group = Group(v_recv.at[pl.ds(0, 7)])
    for k in FAR8:
        v_group.send(v_recv.at[v], v_recv.at[v], to_v[k])
    wou_group.arrived()
    total = wou_recv[0]
    for k in range(1, 8):
        total = total + wou_recv[k]
    wov_recv[pl.ds(v, 1)] = total.reshape(1, 16, 128)
    wov_group = Group(wov_recv.at[pl.ds(0, 7)])
    for k in FAR8:
        wov_group.send(wov_recv.at[v], wov_recv.at[v], to_v[k])
    drain()

    base = c * 512

    def block(q, rows_at, rows, cols):
        return gw_ref.at[pl.ds(pl.multiple_of(base + q * 256 + rows_at, 32), rows), cols]

    v_group.arrived()
    total = v_recv[0].astype(F32)
    for k in range(1, 8):
        total = total + v_recv[k].astype(F32)
    total = total.astype(BF16)
    spot1 = block(1, u * 32, 32, x_cols)
    spot1[...] = total[1]
    spot0 = block(0, u * 32, 32, x_cols)
    spot0[...] = total[0]
    u0_group = Group(u0_recv)
    for k in FAR8:
        u0_group.send(spot0, spot0, to_u[k])
    x1_group = Group(x1_recv)
    for k in FAR4:
        x1_group.send(spot1, spot1, to_x[k])
    wov_group.arrived()
    total = wov_recv[0]
    for k in range(1, 8):
        total = total + wov_recv[k]
    spot = gwo.at[pl.ds(pl.multiple_of(c * 256 + x * 64 + u * 8, 8), 8)]
    spot[...] = total[0:8]
    wou_group = Group(loss_recv.at[pl.ds(0, 7)])
    for k in FAR8:
        wou_group.send(spot, spot, to_u[k])
    for i in range(4):
        gbin_ref[:, 128 * i:128 * i + 128] = total[8 + i:9 + i]
    gbo_ref[...] = total[12:13, 0:VARS]
    drain()

    x1_group.arrived()
    spot = block(1, u * 32, 32, pl.ds(0, 512))
    u1_group = Group(u1_recv, apart=7)
    u1_copies = [u1_group.send(spot, spot, to_u[k]) for k in FAR8]
    last = Group(part)
    last.send(spot, spot, sibling)
    u0_group.arrived()
    spot = block(0, 0, 256, x_cols)
    x0_group = Group(x0_recv, apart=3)
    x0_copies = [x0_group.send(spot, spot, to_x[k]) for k in FAR4]
    last.send(spot, spot, sibling)
    wou_group.arrived()
    rows = pl.ds(pl.multiple_of(c * 256 + x * 64, 64), 64)
    spot = gwo_low.at[rows]
    spot[...] = gwo[rows].astype(BF16)
    wox_group = Group(wox_recv, apart=3)
    wox_copies = [wox_group.send(spot, spot, to_x[k]) for k in FAR4]
    last_wo = Group(wo_recv)
    last_wo.send(spot, spot, sibling)

    drain()
    loss_group.arrived()
    for t in range(4):
        loss_ref[:, 128 * t:128 * t + 128] = jnp.where(
            low_row, loss_recv[2 * t, 0:1, :], loss_recv[2 * t + 1, 0:1, :])

    for k, copy in reversed(list(zip(FAR4, wox_copies))):
        copy.wait_recv()
        spot = gwo_low.at[pl.ds(pl.multiple_of(c * 256 + x_at[4 - k] * 64, 64), 64)]
        last_wo.send(spot, spot, sibling)
    near_u = [(k, copy, u1_copies) for k, copy in zip(FAR8, u1_copies)][::-1]
    near_x = [(k, copy, x0_copies) for k, copy in zip(FAR4, x0_copies)][::-1]
    for k, copy, group in near_u[:4] + near_x[:2] + near_u[4:] + near_x[2:]:
        copy.wait_recv()
        if group is x0_copies:
            cols = pl.ds(pl.multiple_of(x_at[4 - k] * 128, 128), 128)
            spot = block(0, 0, 256, cols)
        else:
            spot = block(1, u_at[8 - k] * 32, 32, pl.ds(0, 512))
        last.send(spot, spot, sibling)
    last_wo.arrived()
    gwo_ref[...] = jnp.transpose(gwo_low[...].astype(F32))[0:VARS]
    last.arrived()
    drain()
    drain()
    assert len(groups) == N_SENDS and received[0] == N_RECEIVES


def deliver(*refs):
    results, places, sems = refs[0:5], refs[5:10], refs[10]
    copies = [
        pltpu.make_async_copy(src, dst, sems.at[i])
        for i, (src, dst) in enumerate(zip(results, places))
    ]
    for copy in copies:
        copy.start()
    for copy in copies:
        copy.wait()


def per_device(latent, w_in, b_in, output_weight, output_bias, observed_field, area):
    total_columns = latent.shape[2] * lax.axis_size("grid")
    vmem = pl.BlockSpec(memory_space=pltpu.VMEM)
    hbm = pl.BlockSpec(memory_space=pltpu.HBM)

    def scratch(dtype, *shape):
        return pltpu.VMEM(shape, dtype)

    results = (
        jax.ShapeDtypeStruct((1, COLS), F32),
        jax.ShapeDtypeStruct((DIN, HID), BF16),
        jax.ShapeDtypeStruct((1, HID), F32),
        jax.ShapeDtypeStruct((VARS, HID), F32),
        jax.ShapeDtypeStruct((1, VARS), F32),
    )
    operands = (
        latent, w_in, b_in.reshape(1, HID), output_weight.T, output_bias.reshape(1, VARS),
        observed_field, area.reshape(1, COLS),
    )
    made = pl.pallas_call(
        lambda *refs: kernel(total_columns, *refs),
        out_shape=results,
        in_specs=[hbm] * 7,
        out_specs=(vmem,) * 5,
        scratch_shapes=[
            scratch(F32, 1, HID), scratch(BF16, VARS, HID), scratch(F32, 1, VARS),
            scratch(F32, VARS, COLS), scratch(F32, 1, COLS), scratch(F32, HID, 128),
            scratch(BF16, HID, 128),
            scratch(BF16, DIN, COLS), scratch(BF16, DIN, HID),
            scratch(F32, HID, 128), scratch(F32, HID, COLS), scratch(F32, HID, COLS),
            scratch(BF16, HID, COLS), scratch(BF16, HID, 128), scratch(BF16, 128, HID),
            scratch(F32, 1, 128), scratch(F32, 2 * FOLD, 128),
            scratch(BF16, 2, 2, 2, FOLD, 128), scratch(BF16, 8, FOLD, 128),
            scratch(BF16, 8, FOLD, 128), scratch(BF16, 8, FOLD, 128),
            scratch(F32, 8, 8, 128), scratch(BF16, 128, COLS), scratch(BF16, HID, COLS),
            scratch(BF16, 2, 256, HID), scratch(BF16, 2, 256, HID),
            scratch(F32, 2, 256, HID), scratch(BF16, 2, 256, HID),
            scratch(BF16, 3, 256, 128), scratch(BF16, 256, 128),
            scratch(BF16, 7, 32, 128),
            scratch(BF16, 7, 32, HID), scratch(BF16, 32, HID),
            scratch(BF16, 3, 32, 128), scratch(BF16, 8, 2, 32, 128),
            scratch(F32, HID, 128), scratch(BF16, 256, 128), scratch(BF16, 256, 128),
            scratch(BF16, 256, 128), scratch(BF16, 3, 64, 128),
            scratch(F32, 8, 16, 128), scratch(F32, 8, 16, 128), scratch(F32, 8, 16, 128),
            scratch(F32, 2, 8, 128), scratch(F32, 4, 8, 128),
            pltpu.SemaphoreType.DMA((9,)),
            pltpu.SemaphoreType.DMA((N_SENDS,)), pltpu.SemaphoreType.DMA((N_RECEIVES,)),
        ],
        compiler_params=pltpu.CompilerParams(
            collective_id=0, has_side_effects=True, vmem_limit_bytes=40 * 2**20),
        cost_estimate=pl.CostEstimate(
            flops=4 * DIN * HID * COLS, bytes_accessed=4 * 2**20, transcendentals=2 * HID * COLS),
        name="energy_score_step",
    )(*[pltpu.with_memory_space_constraint(operand, pltpu.HBM) for operand in operands])
    loss, grad_w_in, grad_b_in, grad_w_out, grad_b_out = pl.pallas_call(
        deliver,
        out_shape=results,
        in_specs=[vmem] * 5,
        out_specs=(hbm,) * 5,
        scratch_shapes=[pltpu.SemaphoreType.DMA((5,))],
        compiler_params=pltpu.CompilerParams(vmem_limit_bytes=4 * 2**20),
        name="deliver",
    )(*made)
    return (
        loss.reshape(COLS), grad_w_in, grad_b_in.reshape(HID), grad_w_out.T,
        grad_b_out.reshape(VARS),
    )


def solution(mesh):
    placed = (P("member", None, "grid"), P(), P(), P(), P(), P(None, "grid"), P("grid"))
    return jax.shard_map(
        per_device,
        mesh=mesh,
        in_specs=placed,
        out_specs=(P("grid"), P(), P(), P(), P()),
        check_vma=False,
    )
```

```python
import math

import jax
import jax.numpy as jnp
from jax import lax
from jax.experimental import pallas as pl
from jax.experimental.pallas import tpu as pltpu
from jax.sharding import PartitionSpec as P

MESH = pl.DeviceIdType.MESH
F32 = jnp.float32
BF16 = jnp.bfloat16
EPSILON = 1e-05
GELU_A = math.sqrt(2.0 / math.pi)
GELU_B = 0.044715

DIN, HID, VARS = 1024, 512, 83
COLS = 512
FOLD = 48
NX, NU = 4, 8
FAR4 = (2, 1, 3)
FAR8 = (4, 3, 5, 2, 6, 1, 7)
N_SENDS, N_RECEIVES = 24, 28


def dot(a, b):
    return jnp.dot(a, b, preferred_element_type=F32)


def dot_nt(a, b):
    return lax.dot_general(a, b, (((1,), (1,)), ((), ())), preferred_element_type=F32)


def dot_tn(a, b):
    return lax.dot_general(a, b, (((0,), (0,)), ((), ())), preferred_element_type=F32)


def kernel(
    total_columns,
    lat_hbm, win_hbm, bin_hbm, wo_hbm, bo_hbm, obs_hbm, area_hbm,
    loss_ref, gw_ref, gbin_ref, gwo_ref, gbo_ref,
    bin_ref, wo_ref, bo_ref, obs_ref, area_ref, gwo, gwo_low,
    lat, win, bias, pre, dgelu, hidden, wop, wop_t, row, obs_pad,
    f_send, f_recv, g_send, g_recv, loss_recv, gl, gp,
    sib_send, sib_recv, own, part,
    x0_recv, s0, u0_recv, u1_recv, s1, x1_recv, v_recv,
    wo_part, wo_send, wo_recv, wo_rs, wox_recv, wou_src, wou_recv, wov_recv,
    sm_c, sm_x,
    local_sems, send_sems, recv_sems,
):
    member, grid = lax.axis_index("member"), lax.axis_index("grid")
    c, zlo = member & 1, member >> 1
    a, b = zlo >> 1, zlo & 1
    zhi, y, x = grid & 1, (grid >> 1) & 7, grid >> 4
    z = zhi * 4 + zlo
    on_y = 1 - c
    u = y * on_y + z * c
    v = z * on_y + y * c

    def device(x, y, z):
        return ((z & 3) * 2 + c, (x * 8 + y) * 2 + (z >> 2))

    x_at = [(x + k) & 3 for k in range(4)]
    u_at = [(u + k) & 7 for k in range(8)]
    v_at = [(v + k) & 7 for k in range(8)]
    to_x = [(member, (x_at[k] * 8 + y) * 2 + zhi) for k in range(4)]
    to_u = [device(x, u_at[k] * on_y + y * c, z * on_y + u_at[k] * c) for k in range(8)]
    to_v = [device(x, y * on_y + v_at[k] * c, v_at[k] * on_y + z * c) for k in range(8)]

    to_u_other = [(there_u[0] + 1 - 2 * c, there_u[1]) for there_u in to_u]
    sibling = (zlo * 2 + 1 - c, grid)

    def flip(bit, by):
        return 1 - bit if by else bit

    def member_of(rel):
        ra, rb, rc = rel
        return (2 * flip(a, ra) + flip(b, rb)) * 2 + flip(c, rc)

    rels = [(ra, rb, rc) for ra in (1, 0) for rb in (1, 0) for rc in (1, 0)][:-1]

    there = {rel: member_of(rel) for rel in rels}

    groups, fences, received = [], [0, 0], [0]

    class Group:
        def __init__(self, size, apart=0):
            self.size, self.index = size, len(groups)
            self.first, self.apart, self.count = received[0], apart, 0
            received[0] += max(apart, 1)
            groups.append(self)

        def copy(self, src, dst, to, number=0):
            return pltpu.make_async_remote_copy(
                src_ref=src, dst_ref=dst, send_sem=send_sems.at[self.index],
                recv_sem=recv_sems.at[self.first + number], device_id=to, device_id_type=MESH,
            )

        def send(self, src, dst, to):
            copy = self.copy(src, dst, to, self.count if self.apart else 0)
            self.count += 1
            copy.start()
            return copy

        def arrived(self):
            self.copy(self.size, self.size, sibling).wait_recv()

        def left(self):
            self.copy(self.size, self.size, sibling).wait_send()

    def drain():
        for group in groups[fences[-2]:fences[-1]]:
            group.left()
        fences.append(len(groups))

    halves = [1 - a, a]
    load_w = [
        pltpu.make_async_copy(
            win_hbm.at[pl.ds(512 * i, 512)], win.at[pl.ds(512 * i, 512)], local_sems.at[i])
        for i in range(2)
    ]
    load_l = [
        pltpu.make_async_copy(
            lat_hbm.at[0, :, pl.ds(pl.multiple_of(h * 256, 256), 256)],
            lat.at[:, pl.ds(pl.multiple_of(h * 256, 256), 256)], local_sems.at[2 + i])
        for i, h in enumerate(halves)
    ]
    load_small = [
        pltpu.make_async_copy(src, dst, local_sems.at[4 + i])
        for i, (src, dst) in enumerate((
            (bin_hbm, bin_ref), (wo_hbm, wo_ref), (bo_hbm, bo_ref),
            (obs_hbm, obs_ref), (area_hbm, area_ref)))
    ]
    for copy in load_w + load_l[:1] + load_small[:3]:
        copy.start()

    barrier = pltpu.get_barrier_semaphore()
    far, near = rels[:4], rels[4:]
    partners = (
        [way[k] for k in (4, 3, 5) for way in (to_u, to_u_other, to_v)]
        + [(there[rel], grid) for rel in far]
        + [way[k] for k in (2, 6) for way in (to_u, to_u_other, to_v)] + [to_x[2]]
        + [(there[rel], grid) for rel in near]
        + [way[k] for k in (1, 7) for way in (to_u, to_u_other, to_v)] + [to_x[1], to_x[3]]
    )
    for partner in partners:
        pl.semaphore_signal(barrier, inc=1, device_id=partner, device_id_type=MESH)
    for copy in load_l[1:] + load_small[3:]:
        copy.start()

    wop_t[...] = jnp.zeros_like(wop_t)
    row[...] = jnp.zeros_like(row)
    for copy in load_small[:3]:
        copy.wait()
    for i in range(4):
        bias[pl.ds(128 * i, 128), :] = jnp.transpose(
            jnp.broadcast_to(bin_ref[:, pl.ds(128 * i, 128)], (128, 128)))
    wop_t[0:VARS, :] = wo_ref[...]
    row[:, 0:VARS] = bo_ref[...]
    bias_out = jnp.transpose(jnp.broadcast_to(row[...], (128, 128)))[0:2 * FOLD]
    lane = lax.broadcasted_iota(jnp.int32, (FOLD, 128), 1)
    low_lane = lane < 64
    low_row = lax.broadcasted_iota(jnp.int32, (1, 128), 1) < 64

    def swap(value):
        return pltpu.roll(value, 64, 1)

    for copy in load_w:
        copy.wait()

    f_group = Group(f_recv.at[pl.ds(0, 7)])
    for i, h in enumerate(halves):
        cols = pl.ds(pl.multiple_of(h * 256, 256), 256)
        load_l[i].wait()
        pre[:, cols] = dot_tn(win[...], lat[:, cols])

        def activate(r, _):
            rows = pl.ds(pl.multiple_of(r * 128, 128), 128)
            shift = bias[rows, :]
            value = pre[rows, cols] + jnp.concatenate([shift, shift], axis=1)
            pre[rows, cols] = value
            inner = GELU_A * (value + GELU_B * (value * value * value))
            hidden[rows, cols] = (0.5 * value * (1.0 + jnp.tanh(inner))).astype(BF16)
            return 0

        lax.fori_loop(0, HID // 128, activate, 0)
        field = dot(wop_t[0:2 * FOLD, :], hidden[:, cols])
        for t in range(2):
            chunk = (field[:, 128 * t:128 * t + 128] + bias_out).astype(BF16).astype(F32)
            lo, hi = chunk[0:FOLD], chunk[FOLD:2 * FOLD]
            f_send[i, t, 0] = jnp.where(low_lane, lo, swap(hi)).astype(BF16)
            f_send[i, t, 1] = jnp.where(low_lane, swap(lo), hi).astype(BF16)
        if i == 0:
            pl.semaphore_wait(barrier, len(partners))
        for rel in rels:
            if rel[0] == 1 - i:
                src = f_send.at[i, flip(b, rel[1]), flip(c, rel[2])]
                f_group.send(src, f_recv.at[member], (there[rel], grid))
    f_recv[pl.ds(member, 1)] = f_send[1, pl.ds(b, 1), pl.ds(c, 1)].reshape(1, FOLD, 128)

    def derive(r, _):
        rows = pl.ds(pl.multiple_of(r * 128, 128), 128)
        value = pre[rows, :]
        square = value * value
        t = jnp.tanh(GELU_A * (value + GELU_B * (value * square)))
        dgelu[rows, :] = 0.5 * (1.0 + t) + (0.5 * GELU_A) * value * (1.0 - t * t) * (
            1.0 + (3.0 * GELU_B) * square)
        return 0

    lax.fori_loop(0, HID // 128, derive, 0)
    wop[...] = jnp.transpose(wop_t[...])
    for copy in load_small[3:]:
        copy.wait()
    obs_pad[...] = jnp.zeros_like(obs_pad)
    own_cols = pl.ds(pl.multiple_of(zlo * 128, 128), 128)
    obs_pad[0:VARS, :] = obs_ref[:, own_cols]
    lo, hi = obs_pad[0:FOLD], obs_pad[FOLD:2 * FOLD]
    first = c == 0
    observed = jnp.where(low_lane, jnp.where(first, lo, swap(lo)), jnp.where(first, swap(hi), hi))
    area = area_ref[:, own_cols]
    area = jnp.where(low_row, jnp.where(first, area, swap(area)), jnp.where(first, swap(area), area))
    factor = area * (VARS * math.sqrt(8 / total_columns))
    gl[2 * FOLD:128, :] = jnp.zeros((128 - 2 * FOLD, COLS), BF16)

    def norm(difference):
        total = jnp.sum(difference * difference, axis=0, keepdims=True)
        square = (total + swap(total)) / VARS + EPSILON
        inverse = lax.rsqrt(square)
        return square * inverse, inverse

    f_group.arrived()
    fields = [f_recv[i].astype(F32) for i in range(8)]
    grads = []
    true_total = jnp.zeros((1, 128), F32)
    for m in range(8):
        difference = fields[m] - observed
        distance, inverse = norm(difference)
        true_total = true_total + distance
        grads.append(difference * (factor * inverse * (1.0 / (VARS * 8))))
    pair_total = jnp.full((1, 128), 8.0 * math.sqrt(EPSILON), F32)
    for m in range(8):
        for n in range(m + 1, 8):
            difference = fields[m] - fields[n]
            distance, inverse = norm(difference)
            pair_total = pair_total + 2.0 * distance
            pull = difference * (factor * inverse * (1.0 / (VARS * 64)))
            grads[m] = grads[m] - pull
            grads[n] = grads[n] + pull
    for m in range(8):
        g_send[m] = grads[m].astype(BF16)
    g_group = Group(g_recv.at[pl.ds(0, 7)])
    for rel in rels:
        g_group.send(g_send.at[there[rel]], g_recv.at[member], (there[rel], grid))
    g_recv[pl.ds(member, 1)] = g_send[pl.ds(member, 1)]
    loss = true_total * (1.0 / 8) - pair_total * (1.0 / 128)
    loss_recv[pl.ds(member, 1)] = jnp.broadcast_to(loss, (1, 8, 128))
    loss_group = Group(loss_recv.at[pl.ds(0, 7)])
    for rel in rels:
        loss_group.send(loss_recv.at[member], loss_recv.at[member], (there[rel], grid))

    drain()
    g_group.arrived()
    for t in range(4):
        left, right = g_recv[2 * t].astype(F32), g_recv[2 * t + 1].astype(F32)
        cols = pl.ds(128 * t, 128)
        gl[0:FOLD, cols] = jnp.where(low_lane, left, swap(right)).astype(BF16)
        gl[FOLD:2 * FOLD, cols] = jnp.where(low_lane, swap(left), right).astype(BF16)

    def grad_hidden(r, _):
        rows = pl.ds(pl.multiple_of(r * 128, 128), 128)
        gp[rows, :] = (dot(wop[rows, :], gl[...]) * dgelu[rows, :]).astype(BF16)
        return 0

    lax.fori_loop(0, HID // 128, grad_hidden, 0)

    sib_groups = [Group(sib_recv.at[q]) for q in range(2)]
    for q in range(2):
        rows = pl.ds(pl.multiple_of((1 - c) * 512 + q * 256, 256), 256)
        sib_send[q] = dot_nt(lat[rows, :], gp[...]).astype(BF16)
        sib_groups[q].send(sib_send.at[q], sib_recv.at[q], sibling)
    wo_part[...] = dot_nt(hidden[...], gl[...])
    wo_send[...] = wo_part[pl.ds(pl.multiple_of((1 - c) * 256, 256), 256), :].astype(BF16)
    wo_group = Group(wo_recv)
    wo_group.send(wo_send, wo_recv, sibling)
    ones = jnp.ones((16, COLS), BF16)
    sum_in = dot_nt(ones, gp[...])[0:1]
    sum_out = dot_nt(ones, gl[...])[0:1]
    rows8 = lax.broadcasted_iota(jnp.int32, (8, 128), 0)
    tile = jnp.where(rows8 == 4, sum_out, 0.0)
    for i in range(4):
        tile = jnp.where(rows8 == i, sum_in[:, 128 * i:128 * i + 128], tile)
    sm_c[pl.ds(c, 1)] = tile.reshape(1, 8, 128)
    smc_group = Group(sm_c.at[0])
    smc_group.send(sm_c.at[c], sm_c.at[c], sibling)

    x_cols = pl.ds(pl.multiple_of(x * 128, 128), 128)
    u_rows = pl.ds(pl.multiple_of(u * 32, 32), 32)

    def own_half(q):
        rows = pl.ds(pl.multiple_of(c * 512 + q * 256, 256), 256)
        own[q] = dot_nt(lat[rows, :], gp[...])

    def merge(q):
        sib_groups[q].arrived()
        part[q] = (own[q] + sib_recv[q].astype(F32)).astype(BF16)

    own_half(0)
    own_half(1)
    merge(0)
    x0_group = Group(x0_recv)
    for k in FAR4:
        cols = pl.ds(pl.multiple_of(x_at[k] * 128, 128), 128)
        x0_group.send(part.at[0, :, cols], x0_recv.at[k - 1], to_x[k])
    merge(1)
    u1_group = Group(u1_recv)
    for k in FAR8:
        rows = pl.ds(pl.multiple_of(u_at[k] * 32, 32), 32)
        u1_group.send(part.at[1, rows], u1_recv.at[k - 1], to_u[k])
    wo_group.arrived()
    wo_rs[...] = (
        wo_part[pl.ds(pl.multiple_of(c * 256, 256), 256), :] + wo_recv[...].astype(F32)).astype(BF16)
    wox_group = Group(wox_recv)
    for k in FAR4:
        rows = pl.ds(pl.multiple_of(x_at[k] * 64, 64), 64)
        wox_group.send(wo_rs.at[rows], wox_recv.at[k - 1], to_x[k])
    smc_group.arrived()
    sm_x[pl.ds(x, 1)] = (sm_c[0] + sm_c[1]).reshape(1, 8, 128)
    smx_group = Group(sm_x.at[pl.ds(0, 3)])
    for k in FAR4:
        smx_group.send(sm_x.at[x], sm_x.at[x], to_x[k])

    drain()
    x0_group.arrived()
    total = part[0, :, x_cols].astype(F32)
    for k in range(3):
        total = total + x0_recv[k].astype(F32)
    s0[...] = total.astype(BF16)
    u0_group = Group(u0_recv)
    for k in FAR8:
        rows = pl.ds(pl.multiple_of(u_at[k] * 32, 32), 32)
        u0_group.send(s0.at[rows], u0_recv.at[k - 1], to_u[k])
    wox_group.arrived()
    total = wo_rs[pl.ds(pl.multiple_of(x * 64, 64), 64), :].astype(F32)
    for k in range(3):
        total = total + wox_recv[k].astype(F32)
    smx_group.arrived()
    small = sm_x[0] + sm_x[1] + sm_x[2] + sm_x[3]
    for j in range(8):
        wou_src[j, 0:8] = total[8 * j:8 * j + 8]
        wou_src[j, 8:16] = small
    wou_recv[pl.ds(u, 1)] = wou_src[pl.ds(u, 1)]
    wou_group = Group(wou_recv.at[pl.ds(0, 7)])
    for k in FAR8:
        wou_group.send(wou_src.at[u_at[k]], wou_recv.at[u], to_u[k])
    u1_group.arrived()
    total = part[1, u_rows, :].astype(F32)
    for k in range(7):
        total = total + u1_recv[k].astype(F32)
    s1[...] = total.astype(BF16)
    x1_group = Group(x1_recv)
    for k in FAR4:
        cols = pl.ds(pl.multiple_of(x_at[k] * 128, 128), 128)
        x1_group.send(s1.at[:, cols], x1_recv.at[k - 1], to_x[k])

    x1_group.arrived()
    total = s1[:, x_cols].astype(F32)
    for k in range(3):
        total = total + x1_recv[k].astype(F32)
    v_recv[v, 1] = total.astype(BF16)
    u0_group.arrived()
    total = s0[u_rows, :].astype(F32)
    for k in range(7):
        total = total + u0_recv[k].astype(F32)
    v_recv[v, 0] = total.astype(BF16)
    v_group = Group(v_recv.at[pl.ds(0, 7)])
    for k in FAR8:
        v_group.send(v_recv.at[v], v_recv.at[v], to_v[k])
    wou_group.arrived()
    total = wou_recv[0]
    for k in range(1, 8):
        total = total + wou_recv[k]
    wov_recv[pl.ds(v, 1)] = total.reshape(1, 16, 128)
    wov_group = Group(wov_recv.at[pl.ds(0, 7)])
    for k in FAR8:
        wov_group.send(wov_recv.at[v], wov_recv.at[v], to_v[k])
    drain()

    base = c * 512

    def block(q, rows_at, rows, cols):
        return gw_ref.at[pl.ds(pl.multiple_of(base + q * 256 + rows_at, 32), rows), cols]

    v_group.arrived()
    total = v_recv[0].astype(F32)
    for k in range(1, 8):
        total = total + v_recv[k].astype(F32)
    total = total.astype(BF16)
    spot1 = block(1, u * 32, 32, x_cols)
    spot1[...] = total[1]
    spot0 = block(0, u * 32, 32, x_cols)
    spot0[...] = total[0]
    u0_group = Group(u0_recv)
    for k in FAR8:
        u0_group.send(spot0, spot0, to_u[k])
    x1_group = Group(x1_recv)
    for k in FAR4:
        x1_group.send(spot1, spot1, to_x[k])
    wov_group.arrived()
    total = wov_recv[0]
    for k in range(1, 8):
        total = total + wov_recv[k]
    spot = gwo.at[pl.ds(pl.multiple_of(c * 256 + x * 64 + u * 8, 8), 8)]
    spot[...] = total[0:8]
    wou_group = Group(loss_recv.at[pl.ds(0, 7)])
    for k in FAR8:
        wou_group.send(spot, spot, to_u[k])
    for i in range(4):
        gbin_ref[:, 128 * i:128 * i + 128] = total[8 + i:9 + i]
    gbo_ref[...] = total[12:13, 0:VARS]
    drain()

    x1_group.arrived()
    spot = block(1, u * 32, 32, pl.ds(0, 512))
    u1_group, last = Group(u1_recv), Group(part)
    for k in FAR8:
        u1_group.send(spot, spot, to_u[k])
        last.send(spot, spot, to_u_other[k])
    last.send(spot, spot, sibling)
    u0_group.arrived()
    spot = block(0, 0, 256, x_cols)
    x0_group = Group(x0_recv, apart=3)
    x0_copies = [x0_group.send(spot, spot, to_x[k]) for k in FAR4]
    last.send(spot, spot, sibling)
    wou_group.arrived()
    rows = pl.ds(pl.multiple_of(c * 256 + x * 64, 64), 64)
    spot = gwo_low.at[rows]
    spot[...] = gwo[rows].astype(BF16)
    wox_group = Group(wox_recv, apart=3)
    wox_copies = [wox_group.send(spot, spot, to_x[k]) for k in FAR4]
    last_wo = Group(wo_recv)
    last_wo.send(spot, spot, sibling)

    drain()
    loss_group.arrived()
    for t in range(4):
        loss_ref[:, 128 * t:128 * t + 128] = jnp.where(
            low_row, loss_recv[2 * t, 0:1, :], loss_recv[2 * t + 1, 0:1, :])

    for k, copy in reversed(list(zip(FAR4, x0_copies))):
        copy.wait_recv()
        cols = pl.ds(pl.multiple_of(x_at[4 - k] * 128, 128), 128)
        spot = block(0, 0, 256, cols)
        last.send(spot, spot, sibling)
    for k, copy in reversed(list(zip(FAR4, wox_copies))):
        copy.wait_recv()
        spot = gwo_low.at[pl.ds(pl.multiple_of(c * 256 + x_at[4 - k] * 64, 64), 64)]
        last_wo.send(spot, spot, sibling)
    last_wo.arrived()
    gwo_ref[...] = jnp.transpose(gwo_low[...].astype(F32))[0:VARS]
    u1_group.arrived()
    last.arrived()
    drain()
    drain()
    assert len(groups) == N_SENDS and received[0] == N_RECEIVES


def deliver(*refs):
    results, places, sems = refs[0:5], refs[5:10], refs[10]
    copies = [
        pltpu.make_async_copy(src, dst, sems.at[i])
        for i, (src, dst) in enumerate(zip(results, places))
    ]
    for copy in copies:
        copy.start()
    for copy in copies:
        copy.wait()


def per_device(latent, w_in, b_in, output_weight, output_bias, observed_field, area):
    total_columns = latent.shape[2] * lax.axis_size("grid")
    vmem = pl.BlockSpec(memory_space=pltpu.VMEM)
    hbm = pl.BlockSpec(memory_space=pltpu.HBM)

    def scratch(dtype, *shape):
        return pltpu.VMEM(shape, dtype)

    results = (
        jax.ShapeDtypeStruct((1, COLS), F32),
        jax.ShapeDtypeStruct((DIN, HID), BF16),
        jax.ShapeDtypeStruct((1, HID), F32),
        jax.ShapeDtypeStruct((VARS, HID), F32),
        jax.ShapeDtypeStruct((1, VARS), F32),
    )
    operands = (
        latent, w_in, b_in.reshape(1, HID), output_weight.T, output_bias.reshape(1, VARS),
        observed_field, area.reshape(1, COLS),
    )
    made = pl.pallas_call(
        lambda *refs: kernel(total_columns, *refs),
        out_shape=results,
        in_specs=[hbm] * 7,
        out_specs=(vmem,) * 5,
        scratch_shapes=[
            scratch(F32, 1, HID), scratch(BF16, VARS, HID), scratch(F32, 1, VARS),
            scratch(F32, VARS, COLS), scratch(F32, 1, COLS), scratch(F32, HID, 128),
            scratch(BF16, HID, 128),
            scratch(BF16, DIN, COLS), scratch(BF16, DIN, HID),
            scratch(F32, HID, 128), scratch(F32, HID, COLS), scratch(F32, HID, COLS),
            scratch(BF16, HID, COLS), scratch(BF16, HID, 128), scratch(BF16, 128, HID),
            scratch(F32, 1, 128), scratch(F32, 2 * FOLD, 128),
            scratch(BF16, 2, 2, 2, FOLD, 128), scratch(BF16, 8, FOLD, 128),
            scratch(BF16, 8, FOLD, 128), scratch(BF16, 8, FOLD, 128),
            scratch(F32, 8, 8, 128), scratch(BF16, 128, COLS), scratch(BF16, HID, COLS),
            scratch(BF16, 2, 256, HID), scratch(BF16, 2, 256, HID),
            scratch(F32, 2, 256, HID), scratch(BF16, 2, 256, HID),
            scratch(BF16, 3, 256, 128), scratch(BF16, 256, 128),
            scratch(BF16, 7, 32, 128),
            scratch(BF16, 7, 32, HID), scratch(BF16, 32, HID),
            scratch(BF16, 3, 32, 128), scratch(BF16, 8, 2, 32, 128),
            scratch(F32, HID, 128), scratch(BF16, 256, 128), scratch(BF16, 256, 128),
            scratch(BF16, 256, 128), scratch(BF16, 3, 64, 128),
            scratch(F32, 8, 16, 128), scratch(F32, 8, 16, 128), scratch(F32, 8, 16, 128),
            scratch(F32, 2, 8, 128), scratch(F32, 4, 8, 128),
            pltpu.SemaphoreType.DMA((9,)),
            pltpu.SemaphoreType.DMA((N_SENDS,)), pltpu.SemaphoreType.DMA((N_RECEIVES,)),
        ],
        compiler_params=pltpu.CompilerParams(
            collective_id=0, has_side_effects=True, vmem_limit_bytes=40 * 2**20),
        cost_estimate=pl.CostEstimate(
            flops=4 * DIN * HID * COLS, bytes_accessed=4 * 2**20, transcendentals=2 * HID * COLS),
        name="energy_score_step",
    )(*[pltpu.with_memory_space_constraint(operand, pltpu.HBM) for operand in operands])
    loss, grad_w_in, grad_b_in, grad_w_out, grad_b_out = pl.pallas_call(
        deliver,
        out_shape=results,
        in_specs=[vmem] * 5,
        out_specs=(hbm,) * 5,
        scratch_shapes=[pltpu.SemaphoreType.DMA((5,))],
        compiler_params=pltpu.CompilerParams(vmem_limit_bytes=4 * 2**20),
        name="deliver",
    )(*made)
    return (
        loss.reshape(COLS), grad_w_in, grad_b_in.reshape(HID), grad_w_out.T,
        grad_b_out.reshape(VARS),
    )


def solution(mesh):
    placed = (P("member", None, "grid"), P(), P(), P(), P(), P(None, "grid"), P("grid"))
    return jax.shard_map(
        per_device,
        mesh=mesh,
        in_specs=placed,
        out_specs=(P("grid"), P(), P(), P(), P()),
        check_vma=False,
    )
```

```python
import math

import jax
import jax.numpy as jnp
from jax import lax
from jax.experimental import pallas as pl
from jax.experimental.pallas import tpu as pltpu
from jax.sharding import PartitionSpec as P

MESH = pl.DeviceIdType.MESH
F32 = jnp.float32
BF16 = jnp.bfloat16
EPSILON = 1e-05
GELU_A = math.sqrt(2.0 / math.pi)
GELU_B = 0.044715

DIN, HID, VARS = 1024, 512, 83
COLS = 512
FOLD = 48
UNIT = 48
NX, NU = 4, 8
FAR4 = (2, 1, 3)
FAR8 = (4, 3, 5, 2, 6, 1, 7)
N_SENDS, N_RECEIVES = 18, 20


def dot(a, b):
    return jnp.dot(a, b, preferred_element_type=F32)


def dot_nt(a, b):
    return lax.dot_general(a, b, (((1,), (1,)), ((), ())), preferred_element_type=F32)


def dot_tn(a, b):
    return lax.dot_general(a, b, (((0,), (0,)), ((), ())), preferred_element_type=F32)


def kernel(
    total_columns,
    lat_hbm, win_hbm, bin_hbm, wo_hbm, bo_hbm, obs_hbm, area_hbm,
    loss_ref, gw_ref, gbin_ref, gwo_ref, gbo_ref,
    bin_ref, wo_ref, bo_ref, obs_ref, area_ref,
    lat, win, bias, pre, dgelu, hidden, wop, wop_t, row, obs_pad,
    f_send, f_recv, g_send, g_recv, loss_recv, gl, gp,
    sib_send, sib_recv, own, wo_part, wo_send, wo_recv, sm_c,
    part0, x0_recv, s0, u0_recv, part1, u1_recv, s1, x1_recv, v_recv,
    gather, gather_other,
    local_sems, send_sems, recv_sems,
):
    member, grid = lax.axis_index("member"), lax.axis_index("grid")
    c, zlo = member & 1, member >> 1
    a, b = zlo >> 1, zlo & 1
    zhi, y, x = grid & 1, (grid >> 1) & 7, grid >> 4
    z = zhi * 4 + zlo
    on_y = 1 - c
    u = y * on_y + z * c
    v = z * on_y + y * c

    def device(x, y, z):
        return ((z & 3) * 2 + c, (x * 8 + y) * 2 + (z >> 2))

    x_at = [(x + k) & 3 for k in range(4)]
    u_at = [(u + k) & 7 for k in range(8)]
    v_at = [(v + k) & 7 for k in range(8)]
    to_x = [(member, (x_at[k] * 8 + y) * 2 + zhi) for k in range(4)]
    to_u = [device(x, u_at[k] * on_y + y * c, z * on_y + u_at[k] * c) for k in range(8)]
    to_v = [device(x, y * on_y + v_at[k] * c, v_at[k] * on_y + z * c) for k in range(8)]

    to_u_other = [(there_u[0] + 1 - 2 * c, there_u[1]) for there_u in to_u]
    sibling = (zlo * 2 + 1 - c, grid)

    def flip(bit, by):
        return 1 - bit if by else bit

    def member_of(rel):
        ra, rb, rc = rel
        return (2 * flip(a, ra) + flip(b, rb)) * 2 + flip(c, rc)

    rels = [(ra, rb, rc) for ra in (1, 0) for rb in (1, 0) for rc in (1, 0)][:-1]

    there = {rel: member_of(rel) for rel in rels}

    groups, fences, received = [], [0, 0], [0]

    class Group:
        def __init__(self, size, apart=0):
            self.size, self.index = size, len(groups)
            self.first, self.apart, self.count = received[0], apart, 0
            received[0] += max(apart, 1)
            groups.append(self)

        def copy(self, src, dst, to, number=0):
            return pltpu.make_async_remote_copy(
                src_ref=src, dst_ref=dst, send_sem=send_sems.at[self.index],
                recv_sem=recv_sems.at[self.first + number], device_id=to, device_id_type=MESH,
            )

        def send(self, src, dst, to):
            copy = self.copy(src, dst, to, self.count if self.apart else 0)
            self.count += 1
            copy.start()
            return copy

        def arrived(self):
            self.copy(self.size, self.size, sibling).wait_recv()

        def left(self):
            self.copy(self.size, self.size, sibling).wait_send()

    def drain():
        for group in groups[fences[-2]:fences[-1]]:
            group.left()
        fences.append(len(groups))

    halves = [1 - a, a]
    load_w = [
        pltpu.make_async_copy(
            win_hbm.at[pl.ds(512 * i, 512)], win.at[pl.ds(512 * i, 512)], local_sems.at[i])
        for i in range(2)
    ]
    load_l = [
        pltpu.make_async_copy(
            lat_hbm.at[0, :, pl.ds(pl.multiple_of(h * 256, 256), 256)],
            lat.at[:, pl.ds(pl.multiple_of(h * 256, 256), 256)], local_sems.at[2 + i])
        for i, h in enumerate(halves)
    ]
    load_small = [
        pltpu.make_async_copy(src, dst, local_sems.at[4 + i])
        for i, (src, dst) in enumerate((
            (bin_hbm, bin_ref), (wo_hbm, wo_ref), (bo_hbm, bo_ref),
            (obs_hbm, obs_ref), (area_hbm, area_ref)))
    ]
    for copy in load_w + load_l[:1] + load_small[:3]:
        copy.start()

    barrier = pltpu.get_barrier_semaphore()
    far, near = rels[:4], rels[4:]
    partners = (
        [way[k] for k in (4, 3, 5) for way in (to_u, to_u_other, to_v)]
        + [(there[rel], grid) for rel in far]
        + [way[k] for k in (2, 6) for way in (to_u, to_u_other, to_v)] + [to_x[2]]
        + [(there[rel], grid) for rel in near]
        + [way[k] for k in (1, 7) for way in (to_u, to_u_other, to_v)] + [to_x[1], to_x[3]]
    )
    for partner in partners:
        pl.semaphore_signal(barrier, inc=1, device_id=partner, device_id_type=MESH)
    for copy in load_l[1:] + load_small[3:]:
        copy.start()

    wop_t[...] = jnp.zeros_like(wop_t)
    row[...] = jnp.zeros_like(row)
    for copy in load_small[:3]:
        copy.wait()
    for i in range(4):
        bias[pl.ds(128 * i, 128), :] = jnp.transpose(
            jnp.broadcast_to(bin_ref[:, pl.ds(128 * i, 128)], (128, 128)))
    wop_t[0:VARS, :] = wo_ref[...]
    row[:, 0:VARS] = bo_ref[...]
    bias_out = jnp.transpose(jnp.broadcast_to(row[...], (128, 128)))[0:2 * FOLD]
    lane = lax.broadcasted_iota(jnp.int32, (FOLD, 128), 1)
    low_lane = lane < 64
    low_row = lax.broadcasted_iota(jnp.int32, (1, 128), 1) < 64

    def swap(value):
        return pltpu.roll(value, 64, 1)

    for copy in load_w:
        copy.wait()

    f_group = Group(f_recv.at[pl.ds(0, 7)])
    for i, h in enumerate(halves):
        cols = pl.ds(pl.multiple_of(h * 256, 256), 256)
        load_l[i].wait()
        pre[:, cols] = dot_tn(win[...], lat[:, cols])

        def activate(r, _):
            rows = pl.ds(pl.multiple_of(r * 128, 128), 128)
            shift = bias[rows, :]
            value = pre[rows, cols] + jnp.concatenate([shift, shift], axis=1)
            pre[rows, cols] = value
            inner = GELU_A * (value + GELU_B * (value * value * value))
            hidden[rows, cols] = (0.5 * value * (1.0 + jnp.tanh(inner))).astype(BF16)
            return 0

        lax.fori_loop(0, HID // 128, activate, 0)
        field = dot(wop_t[0:2 * FOLD, :], hidden[:, cols])
        for t in range(2):
            chunk = (field[:, 128 * t:128 * t + 128] + bias_out).astype(BF16).astype(F32)
            lo, hi = chunk[0:FOLD], chunk[FOLD:2 * FOLD]
            f_send[i, t, 0] = jnp.where(low_lane, lo, swap(hi)).astype(BF16)
            f_send[i, t, 1] = jnp.where(low_lane, swap(lo), hi).astype(BF16)
        if i == 0:
            pl.semaphore_wait(barrier, len(partners))
        for rel in rels:
            if rel[0] == 1 - i:
                src = f_send.at[i, flip(b, rel[1]), flip(c, rel[2])]
                f_group.send(src, f_recv.at[member], (there[rel], grid))
    f_recv[pl.ds(member, 1)] = f_send[1, pl.ds(b, 1), pl.ds(c, 1)].reshape(1, FOLD, 128)

    def derive(r, _):
        rows = pl.ds(pl.multiple_of(r * 128, 128), 128)
        value = pre[rows, :]
        square = value * value
        t = jnp.tanh(GELU_A * (value + GELU_B * (value * square)))
        dgelu[rows, :] = 0.5 * (1.0 + t) + (0.5 * GELU_A) * value * (1.0 - t * t) * (
            1.0 + (3.0 * GELU_B) * square)
        return 0

    lax.fori_loop(0, HID // 128, derive, 0)
    wop[...] = jnp.transpose(wop_t[...])
    for copy in load_small[3:]:
        copy.wait()
    obs_pad[...] = jnp.zeros_like(obs_pad)
    own_cols = pl.ds(pl.multiple_of(zlo * 128, 128), 128)
    obs_pad[0:VARS, :] = obs_ref[:, own_cols]
    lo, hi = obs_pad[0:FOLD], obs_pad[FOLD:2 * FOLD]
    first = c == 0
    observed = jnp.where(low_lane, jnp.where(first, lo, swap(lo)), jnp.where(first, swap(hi), hi))
    area = area_ref[:, own_cols]
    area = jnp.where(low_row, jnp.where(first, area, swap(area)), jnp.where(first, swap(area), area))
    factor = area * (VARS * math.sqrt(8 / total_columns))
    gl[2 * FOLD:128, :] = jnp.zeros((128 - 2 * FOLD, COLS), BF16)

    def norm(difference):
        total = jnp.sum(difference * difference, axis=0, keepdims=True)
        square = (total + swap(total)) / VARS + EPSILON
        inverse = lax.rsqrt(square)
        return square * inverse, inverse

    f_group.arrived()
    fields = [f_recv[i].astype(F32) for i in range(8)]
    grads = []
    true_total = jnp.zeros((1, 128), F32)
    for m in range(8):
        difference = fields[m] - observed
        distance, inverse = norm(difference)
        true_total = true_total + distance
        grads.append(difference * (factor * inverse * (1.0 / (VARS * 8))))
    pair_total = jnp.full((1, 128), 8.0 * math.sqrt(EPSILON), F32)
    for m in range(8):
        for n in range(m + 1, 8):
            difference = fields[m] - fields[n]
            distance, inverse = norm(difference)
            pair_total = pair_total + 2.0 * distance
            pull = difference * (factor * inverse * (1.0 / (VARS * 64)))
            grads[m] = grads[m] - pull
            grads[n] = grads[n] + pull
    for m in range(8):
        g_send[m] = grads[m].astype(BF16)
    g_group = Group(g_recv.at[pl.ds(0, 7)])
    for rel in rels:
        g_group.send(g_send.at[there[rel]], g_recv.at[member], (there[rel], grid))
    g_recv[pl.ds(member, 1)] = g_send[pl.ds(member, 1)]
    loss = true_total * (1.0 / 8) - pair_total * (1.0 / 128)
    loss_recv[pl.ds(member, 1)] = jnp.broadcast_to(loss, (1, 8, 128))
    loss_group = Group(loss_recv.at[pl.ds(0, 7)])
    for rel in rels:
        loss_group.send(loss_recv.at[member], loss_recv.at[member], (there[rel], grid))

    drain()
    g_group.arrived()
    for t in range(4):
        left, right = g_recv[2 * t].astype(F32), g_recv[2 * t + 1].astype(F32)
        cols = pl.ds(128 * t, 128)
        gl[0:FOLD, cols] = jnp.where(low_lane, left, swap(right)).astype(BF16)
        gl[FOLD:2 * FOLD, cols] = jnp.where(low_lane, swap(left), right).astype(BF16)

    wo_part[...] = dot_nt(gl[...], hidden[...])
    wo_send[...] = wo_part[:, pl.ds(pl.multiple_of((1 - c) * 256, 256), 256)].astype(BF16)
    wo_group = Group(wo_recv)
    wo_group.send(wo_send, wo_recv, sibling)

    def grad_hidden(r, _):
        rows = pl.ds(pl.multiple_of(r * 128, 128), 128)
        gp[rows, :] = (dot(wop[rows, :], gl[...]) * dgelu[rows, :]).astype(BF16)
        return 0

    lax.fori_loop(0, HID // 128, grad_hidden, 0)

    sib_groups = [Group(sib_recv.at[q]) for q in range(2)]

    def other_half(q):
        rows = pl.ds(pl.multiple_of((1 - c) * 512 + q * 256, 256), 256)
        sib_send[q] = dot_nt(lat[rows, :], gp[...]).astype(BF16)
        sib_groups[q].send(sib_send.at[q], sib_recv.at[q], sibling)

    def own_half(q):
        rows = pl.ds(pl.multiple_of(c * 512 + q * 256, 256), 256)
        own[q] = dot_nt(lat[rows, :], gp[...])

    def merged(q):
        sib_groups[q].arrived()
        return (own[q] + sib_recv[q].astype(F32)).astype(BF16)

    other_half(0)
    ones = jnp.ones((16, COLS), BF16)
    sum_in = dot_nt(ones, gp[...])[0:1]
    sum_out = dot_nt(ones, gl[...])[0:1]
    rows8 = lax.broadcasted_iota(jnp.int32, (8, 128), 0)
    tile = jnp.where(rows8 == 4, sum_out, 0.0)
    for i in range(4):
        tile = jnp.where(rows8 == i, sum_in[:, 128 * i:128 * i + 128], tile)
    sm_c[pl.ds(c, 1)] = tile.reshape(1, 8, 128)
    smc_group = Group(sm_c.at[0])
    smc_group.send(sm_c.at[c], sm_c.at[c], sibling)
    other_half(1)
    own_half(0)
    own_half(1)

    x_cols = pl.ds(pl.multiple_of(x * 128, 128), 128)
    u_rows = pl.ds(pl.multiple_of(u * 32, 32), 32)

    wo_group.arrived()
    second = wo_part[:, pl.ds(pl.multiple_of(c * 256, 256), 256)] + wo_recv[...].astype(F32)
    smc_group.arrived()
    sums = jnp.concatenate([sm_c[0] + sm_c[1], jnp.zeros((8, 128), F32)], axis=0).astype(BF16)
    for j in range(4):
        cols = pl.ds(128 * j, 128)
        both = second[32 * j:32 * j + 32]
        part0[256:288, cols] = both[:, 0:128].astype(BF16)
        part0[288:320, cols] = both[:, 128:256].astype(BF16)
        part0[320:336, cols] = sums
    x0_recv[x, 320:336] = sums
    part0[0:256, :] = merged(0)
    x0_group = Group(x0_recv.at[pl.ds(0, 3)])
    for k in FAR4:
        cols = pl.ds(pl.multiple_of(x_at[k] * 128, 128), 128)
        x0_group.send(part0.at[:, cols], x0_recv.at[x], to_x[k])
    part1[...] = merged(1)
    u1_group = Group(u1_recv)
    for k in FAR8:
        rows = pl.ds(pl.multiple_of(u_at[k] * 32, 32), 32)
        u1_group.send(part1.at[rows], u1_recv.at[k - 1], to_u[k])

    drain()
    x0_group.arrived()
    total = part0[0:320, x_cols].astype(F32)
    for k in range(1, 4):
        total = total + x0_recv[x_at[k], 0:320].astype(F32)
    sums = x0_recv[0, 320:336].astype(F32)
    for k in range(1, 4):
        sums = sums + x0_recv[k, 320:336].astype(F32)
    for j in range(8):
        at = 256 + 32 * (j % 2) + 8 * (j // 2)
        s0[j] = jnp.concatenate(
            [total[32 * j:32 * j + 32], total[at:at + 8], sums[0:8]], axis=0).astype(BF16)
    u0_recv[pl.ds(u, 1)] = s0[pl.ds(u, 1)]
    u0_group = Group(u0_recv.at[pl.ds(0, 7)])
    for k in FAR8:
        u0_group.send(s0.at[u_at[k]], u0_recv.at[u], to_u[k])
    u1_group.arrived()
    total = part1[u_rows, :].astype(F32)
    for k in range(7):
        total = total + u1_recv[k].astype(F32)
    s1[...] = total.astype(BF16)
    x1_group = Group(x1_recv)
    for k in FAR4:
        cols = pl.ds(pl.multiple_of(x_at[k] * 128, 128), 128)
        x1_group.send(s1.at[:, cols], x1_recv.at[k - 1], to_x[k])

    x1_group.arrived()
    total = s1[:, x_cols].astype(F32)
    for k in range(3):
        total = total + x1_recv[k].astype(F32)
    v_recv[v, UNIT:UNIT + 32] = total.astype(BF16)
    u0_group.arrived()
    total = u0_recv[0].astype(F32)
    for k in range(1, 8):
        total = total + u0_recv[k].astype(F32)
    v_recv[v, 0:UNIT] = total.astype(BF16)
    v_group = Group(v_recv.at[pl.ds(0, 7)])
    for k in FAR8:
        v_group.send(v_recv.at[v], v_recv.at[v], to_v[k])
    drain()

    def block(rows_at, rows, cols):
        return gw_ref.at[pl.ds(pl.multiple_of(c * 512 + rows_at, 32), rows), cols]

    v_group.arrived()
    total = v_recv[0].astype(F32)
    for k in range(1, 8):
        total = total + v_recv[k].astype(F32)
    gather[x, u] = total[0:UNIT].astype(BF16)
    u0_group = Group(u0_recv.at[pl.ds(0, 7)])
    for k in FAR8:
        u0_group.send(gather.at[x, u], gather.at[x, u], to_u[k])
    spot = block(256 + u * 32, 32, x_cols)
    spot[...] = total[UNIT:UNIT + 32].astype(BF16)
    x1_group = Group(x1_recv)
    for k in FAR4:
        x1_group.send(spot, spot, to_x[k])
    for i in range(4):
        gbin_ref[:, 128 * i:128 * i + 128] = total[40 + i:41 + i]
    gbo_ref[...] = total[44:45, 0:VARS]
    drain()

    x1_group.arrived()
    spot = block(256 + u * 32, 32, pl.ds(0, 512))
    u1_group, last1 = Group(u1_recv), Group(part1)
    for k in FAR8:
        u1_group.send(spot, spot, to_u[k])
        last1.send(spot, spot, to_u_other[k])
    last1.send(spot, spot, sibling)
    u0_group.arrived()
    x0_group = Group(gather.at[pl.ds(0, 3)], apart=3)
    x0_copies = [x0_group.send(gather.at[x], gather.at[x], to_x[k]) for k in FAR4]
    last0 = Group(gather)
    last0.send(gather.at[x], gather_other.at[x], sibling)

    drain()
    loss_group.arrived()
    for t in range(4):
        loss_ref[:, 128 * t:128 * t + 128] = jnp.where(
            low_row, loss_recv[2 * t, 0:1, :], loss_recv[2 * t + 1, 0:1, :])

    for k, copy in reversed(list(zip(FAR4, x0_copies))):
        copy.wait_recv()
        last0.send(gather.at[x_at[4 - k]], gather_other.at[x_at[4 - k]], sibling)

    def place(source, core):
        for i in range(4):
            for j in range(8):
                rows = pl.ds(pl.multiple_of(core * 512 + 32 * j, 32), 32)
                gw_ref[rows, 128 * i:128 * i + 128] = source[i, j, 0:32]
                first_row = 32 * i + 8 * (j // 2)
                count = min(8, VARS - first_row)
                if count > 0:
                    cols = pl.ds(pl.multiple_of(core * 256 + 128 * (j % 2), 128), 128)
                    gwo_ref[first_row:first_row + count, cols] = source[i, j, 32:48].astype(F32)[0:count]

    place(gather, c)
    u1_group.arrived()
    last1.arrived()
    last0.arrived()
    place(gather_other, 1 - c)
    drain()
    drain()
    assert (len(groups), received[0]) == (N_SENDS, N_RECEIVES), (len(groups), received[0])


def deliver(*refs):
    results, places, sems = refs[0:5], refs[5:10], refs[10]
    copies = [
        pltpu.make_async_copy(src, dst, sems.at[i])
        for i, (src, dst) in enumerate(zip(results, places))
    ]
    for copy in copies:
        copy.start()
    for copy in copies:
        copy.wait()


def per_device(latent, w_in, b_in, output_weight, output_bias, observed_field, area):
    total_columns = latent.shape[2] * lax.axis_size("grid")
    vmem = pl.BlockSpec(memory_space=pltpu.VMEM)
    hbm = pl.BlockSpec(memory_space=pltpu.HBM)

    def scratch(dtype, *shape):
        return pltpu.VMEM(shape, dtype)

    results = (
        jax.ShapeDtypeStruct((1, COLS), F32),
        jax.ShapeDtypeStruct((DIN, HID), BF16),
        jax.ShapeDtypeStruct((1, HID), F32),
        jax.ShapeDtypeStruct((VARS, HID), F32),
        jax.ShapeDtypeStruct((1, VARS), F32),
    )
    operands = (
        latent, w_in, b_in.reshape(1, HID), output_weight.T, output_bias.reshape(1, VARS),
        observed_field, area.reshape(1, COLS),
    )
    made = pl.pallas_call(
        lambda *refs: kernel(total_columns, *refs),
        out_shape=results,
        in_specs=[hbm] * 7,
        out_specs=(vmem,) * 5,
        scratch_shapes=[
            scratch(F32, 1, HID), scratch(BF16, VARS, HID), scratch(F32, 1, VARS),
            scratch(F32, VARS, COLS), scratch(F32, 1, COLS),
            scratch(BF16, DIN, COLS), scratch(BF16, DIN, HID),
            scratch(F32, HID, 128), scratch(F32, HID, COLS), scratch(F32, HID, COLS),
            scratch(BF16, HID, COLS), scratch(BF16, HID, 128), scratch(BF16, 128, HID),
            scratch(F32, 1, 128), scratch(F32, 2 * FOLD, 128),
            scratch(BF16, 2, 2, 2, FOLD, 128), scratch(BF16, 8, FOLD, 128),
            scratch(BF16, 8, FOLD, 128), scratch(BF16, 8, FOLD, 128),
            scratch(F32, 8, 8, 128), scratch(BF16, 128, COLS), scratch(BF16, HID, COLS),
            scratch(BF16, 2, 256, HID), scratch(BF16, 2, 256, HID),
            scratch(F32, 2, 256, HID),
            scratch(F32, 128, HID), scratch(BF16, 128, 256), scratch(BF16, 128, 256),
            scratch(F32, 2, 8, 128),
            scratch(BF16, 336, HID), scratch(BF16, 4, 336, 128),
            scratch(BF16, 8, UNIT, 128), scratch(BF16, 8, UNIT, 128),
            scratch(BF16, 256, HID), scratch(BF16, 7, 32, HID),
            scratch(BF16, 32, HID), scratch(BF16, 3, 32, 128),
            scratch(BF16, 8, UNIT + 32, 128),
            scratch(BF16, 4, 8, UNIT, 128), scratch(BF16, 4, 8, UNIT, 128),
            pltpu.SemaphoreType.DMA((9,)),
            pltpu.SemaphoreType.DMA((N_SENDS,)), pltpu.SemaphoreType.DMA((N_RECEIVES,)),
        ],
        compiler_params=pltpu.CompilerParams(
            collective_id=0, has_side_effects=True, vmem_limit_bytes=40 * 2**20),
        cost_estimate=pl.CostEstimate(
            flops=4 * DIN * HID * COLS, bytes_accessed=4 * 2**20, transcendentals=2 * HID * COLS),
        name="energy_score_step",
    )(*[pltpu.with_memory_space_constraint(operand, pltpu.HBM) for operand in operands])
    loss, grad_w_in, grad_b_in, grad_w_out, grad_b_out = pl.pallas_call(
        deliver,
        out_shape=results,
        in_specs=[vmem] * 5,
        out_specs=(hbm,) * 5,
        scratch_shapes=[pltpu.SemaphoreType.DMA((5,))],
        compiler_params=pltpu.CompilerParams(vmem_limit_bytes=4 * 2**20),
        name="deliver",
    )(*made)
    return (
        loss.reshape(COLS), grad_w_in, grad_b_in.reshape(HID), grad_w_out.T,
        grad_b_out.reshape(VARS),
    )


def solution(mesh):
    placed = (P("member", None, "grid"), P(), P(), P(), P(), P(None, "grid"), P("grid"))
    return jax.shard_map(
        per_device,
        mesh=mesh,
        in_specs=placed,
        out_specs=(P("grid"), P(), P(), P(), P()),
        check_vma=False,
    )
```

```python
import math

import jax
import jax.numpy as jnp
from jax import lax
from jax.experimental import pallas as pl
from jax.experimental.pallas import tpu as pltpu
from jax.sharding import PartitionSpec as P

MESH = pl.DeviceIdType.MESH
F32 = jnp.float32
BF16 = jnp.bfloat16
EPSILON = 1e-05
GELU_A = math.sqrt(2.0 / math.pi)
GELU_B = 0.044715

DIN, HID, VARS = 1024, 512, 83
COLS = 512
FOLD = 48
ROWS0, ROWS1 = 128, 384
CHUNK0, CHUNK1 = ROWS0 // 8, ROWS1 // 8
UNIT = CHUNK0 + 16
NX, NU = 4, 8
FAR4 = (2, 1, 3)
FAR8 = (4, 3, 5, 2, 6, 1, 7)
N_SENDS, N_RECEIVES = 18, 26


def dot(a, b):
    return jnp.dot(a, b, preferred_element_type=F32)


def dot_nt(a, b):
    return lax.dot_general(a, b, (((1,), (1,)), ((), ())), preferred_element_type=F32)


def dot_tn(a, b):
    return lax.dot_general(a, b, (((0,), (0,)), ((), ())), preferred_element_type=F32)


def kernel(
    total_columns,
    lat_hbm, win_hbm, bin_hbm, wo_hbm, bo_hbm, obs_hbm, area_hbm,
    loss_ref, gw_ref, gbin_ref, gwo_ref, gbo_ref,
    bin_ref, wo_ref, bo_ref, obs_ref, area_ref,
    lat, win, bias, pre, dgelu, hidden, wop, wop_t, row, obs_pad,
    f_send, f_recv, g_send, g_recv, loss_recv, gl, gp,
    sib_send, sib_recv, own, wo_part, wo_send, wo_recv, sm_c,
    part0, x0_recv, s0, u0_recv, part1, u1_recv, s1, x1_recv, v_recv,
    gather, gather_other,
    local_sems, send_sems, recv_sems,
):
    member, grid = lax.axis_index("member"), lax.axis_index("grid")
    c, zlo = member & 1, member >> 1
    a, b = zlo >> 1, zlo & 1
    zhi, y, x = grid & 1, (grid >> 1) & 7, grid >> 4
    z = zhi * 4 + zlo
    on_y = 1 - c
    u = y * on_y + z * c
    v = z * on_y + y * c

    def device(x, y, z):
        return ((z & 3) * 2 + c, (x * 8 + y) * 2 + (z >> 2))

    x_at = [(x + k) & 3 for k in range(4)]
    u_at = [(u + k) & 7 for k in range(8)]
    v_at = [(v + k) & 7 for k in range(8)]
    to_x = [(member, (x_at[k] * 8 + y) * 2 + zhi) for k in range(4)]
    to_u = [device(x, u_at[k] * on_y + y * c, z * on_y + u_at[k] * c) for k in range(8)]
    to_v = [device(x, y * on_y + v_at[k] * c, v_at[k] * on_y + z * c) for k in range(8)]

    sibling = (zlo * 2 + 1 - c, grid)

    def flip(bit, by):
        return 1 - bit if by else bit

    def member_of(rel):
        ra, rb, rc = rel
        return (2 * flip(a, ra) + flip(b, rb)) * 2 + flip(c, rc)

    rels = [(ra, rb, rc) for ra in (1, 0) for rb in (1, 0) for rc in (1, 0)][:-1]

    there = {rel: member_of(rel) for rel in rels}

    groups, fences, received = [], [0, 0], [0]

    class Group:
        def __init__(self, size, apart=0):
            self.size, self.index = size, len(groups)
            self.first, self.apart, self.count = received[0], apart, 0
            received[0] += max(apart, 1)
            groups.append(self)

        def copy(self, src, dst, to, number=0):
            return pltpu.make_async_remote_copy(
                src_ref=src, dst_ref=dst, send_sem=send_sems.at[self.index],
                recv_sem=recv_sems.at[self.first + number], device_id=to, device_id_type=MESH,
            )

        def send(self, src, dst, to):
            copy = self.copy(src, dst, to, self.count if self.apart else 0)
            self.count += 1
            copy.start()
            return copy

        def arrived(self):
            self.copy(self.size, self.size, sibling).wait_recv()

        def left(self):
            self.copy(self.size, self.size, sibling).wait_send()

    def drain():
        for group in groups[fences[-2]:fences[-1]]:
            group.left()
        fences.append(len(groups))

    halves = [1 - a, a]
    load_w = [
        pltpu.make_async_copy(
            win_hbm.at[pl.ds(512 * i, 512)], win.at[pl.ds(512 * i, 512)], local_sems.at[i])
        for i in range(2)
    ]
    load_l = [
        pltpu.make_async_copy(
            lat_hbm.at[0, :, pl.ds(pl.multiple_of(h * 256, 256), 256)],
            lat.at[:, pl.ds(pl.multiple_of(h * 256, 256), 256)], local_sems.at[2 + i])
        for i, h in enumerate(halves)
    ]
    load_small = [
        pltpu.make_async_copy(src, dst, local_sems.at[4 + i])
        for i, (src, dst) in enumerate((
            (bin_hbm, bin_ref), (wo_hbm, wo_ref), (bo_hbm, bo_ref),
            (obs_hbm, obs_ref), (area_hbm, area_ref)))
    ]
    for copy in load_w + load_l[:1] + load_small[:3]:
        copy.start()

    barrier = pltpu.get_barrier_semaphore()
    far, near = rels[:4], rels[4:]
    partners = (
        [way[k] for k in (4, 3, 5) for way in (to_u, to_v)]
        + [(there[rel], grid) for rel in far]
        + [way[k] for k in (2, 6) for way in (to_u, to_v)] + [to_x[2]]
        + [(there[rel], grid) for rel in near]
        + [way[k] for k in (1, 7) for way in (to_u, to_v)] + [to_x[1], to_x[3]]
    )
    for partner in partners:
        pl.semaphore_signal(barrier, inc=1, device_id=partner, device_id_type=MESH)
    for copy in load_l[1:] + load_small[3:]:
        copy.start()

    wop_t[...] = jnp.zeros_like(wop_t)
    row[...] = jnp.zeros_like(row)
    for copy in load_small[:3]:
        copy.wait()
    for i in range(4):
        bias[pl.ds(128 * i, 128), :] = jnp.transpose(
            jnp.broadcast_to(bin_ref[:, pl.ds(128 * i, 128)], (128, 128)))
    wop_t[0:VARS, :] = wo_ref[...]
    row[:, 0:VARS] = bo_ref[...]
    bias_out = jnp.transpose(jnp.broadcast_to(row[...], (128, 128)))[0:2 * FOLD]
    lane = lax.broadcasted_iota(jnp.int32, (FOLD, 128), 1)
    low_lane = lane < 64
    low_row = lax.broadcasted_iota(jnp.int32, (1, 128), 1) < 64

    def swap(value):
        return pltpu.roll(value, 64, 1)

    for copy in load_w:
        copy.wait()

    f_group = Group(f_recv.at[pl.ds(0, 7)])
    for i, h in enumerate(halves):
        cols = pl.ds(pl.multiple_of(h * 256, 256), 256)
        load_l[i].wait()
        pre[:, cols] = dot_tn(win[...], lat[:, cols])

        def activate(r, _):
            rows = pl.ds(pl.multiple_of(r * 128, 128), 128)
            shift = bias[rows, :]
            value = pre[rows, cols] + jnp.concatenate([shift, shift], axis=1)
            pre[rows, cols] = value
            inner = GELU_A * (value + GELU_B * (value * value * value))
            hidden[rows, cols] = (0.5 * value * (1.0 + jnp.tanh(inner))).astype(BF16)
            return 0

        lax.fori_loop(0, HID // 128, activate, 0)
        field = dot(wop_t[0:2 * FOLD, :], hidden[:, cols])
        for t in range(2):
            chunk = (field[:, 128 * t:128 * t + 128] + bias_out).astype(BF16).astype(F32)
            lo, hi = chunk[0:FOLD], chunk[FOLD:2 * FOLD]
            f_send[i, t, 0] = jnp.where(low_lane, lo, swap(hi)).astype(BF16)
            f_send[i, t, 1] = jnp.where(low_lane, swap(lo), hi).astype(BF16)
        if i == 0:
            pl.semaphore_wait(barrier, len(partners))
        for rel in rels:
            if rel[0] == 1 - i:
                src = f_send.at[i, flip(b, rel[1]), flip(c, rel[2])]
                f_group.send(src, f_recv.at[member], (there[rel], grid))
    f_recv[pl.ds(member, 1)] = f_send[1, pl.ds(b, 1), pl.ds(c, 1)].reshape(1, FOLD, 128)

    def derive(r, _):
        rows = pl.ds(pl.multiple_of(r * 128, 128), 128)
        value = pre[rows, :]
        square = value * value
        t = jnp.tanh(GELU_A * (value + GELU_B * (value * square)))
        dgelu[rows, :] = 0.5 * (1.0 + t) + (0.5 * GELU_A) * value * (1.0 - t * t) * (
            1.0 + (3.0 * GELU_B) * square)
        return 0

    lax.fori_loop(0, HID // 128, derive, 0)
    wop[...] = jnp.transpose(wop_t[...])
    for copy in load_small[3:]:
        copy.wait()
    obs_pad[...] = jnp.zeros_like(obs_pad)
    own_cols = pl.ds(pl.multiple_of(zlo * 128, 128), 128)
    obs_pad[0:VARS, :] = obs_ref[:, own_cols]
    lo, hi = obs_pad[0:FOLD], obs_pad[FOLD:2 * FOLD]
    first = c == 0
    observed = jnp.where(low_lane, jnp.where(first, lo, swap(lo)), jnp.where(first, swap(hi), hi))
    area = area_ref[:, own_cols]
    area = jnp.where(low_row, jnp.where(first, area, swap(area)), jnp.where(first, swap(area), area))
    factor = area * (VARS * math.sqrt(8 / total_columns))
    gl[2 * FOLD:128, :] = jnp.zeros((128 - 2 * FOLD, COLS), BF16)

    def norm(difference):
        total = jnp.sum(difference * difference, axis=0, keepdims=True)
        square = (total + swap(total)) / VARS + EPSILON
        inverse = lax.rsqrt(square)
        return square * inverse, inverse

    f_group.arrived()
    fields = [f_recv[i].astype(F32) for i in range(8)]
    grads = []
    true_total = jnp.zeros((1, 128), F32)
    for m in range(8):
        difference = fields[m] - observed
        distance, inverse = norm(difference)
        true_total = true_total + distance
        grads.append(difference * (factor * inverse * (1.0 / (VARS * 8))))
    pair_total = jnp.full((1, 128), 8.0 * math.sqrt(EPSILON), F32)
    for m in range(8):
        for n in range(m + 1, 8):
            difference = fields[m] - fields[n]
            distance, inverse = norm(difference)
            pair_total = pair_total + 2.0 * distance
            pull = difference * (factor * inverse * (1.0 / (VARS * 64)))
            grads[m] = grads[m] - pull
            grads[n] = grads[n] + pull
    for m in range(8):
        g_send[m] = grads[m].astype(BF16)
    g_group = Group(g_recv.at[pl.ds(0, 7)])
    for rel in rels:
        g_group.send(g_send.at[there[rel]], g_recv.at[member], (there[rel], grid))
    g_recv[pl.ds(member, 1)] = g_send[pl.ds(member, 1)]
    loss = true_total * (1.0 / 8) - pair_total * (1.0 / 128)
    loss_recv[pl.ds(member, 1)] = jnp.broadcast_to(loss, (1, 8, 128))
    loss_group = Group(loss_recv.at[pl.ds(0, 7)])
    for rel in rels:
        loss_group.send(loss_recv.at[member], loss_recv.at[member], (there[rel], grid))

    drain()
    g_group.arrived()
    for t in range(4):
        left, right = g_recv[2 * t].astype(F32), g_recv[2 * t + 1].astype(F32)
        cols = pl.ds(128 * t, 128)
        gl[0:FOLD, cols] = jnp.where(low_lane, left, swap(right)).astype(BF16)
        gl[FOLD:2 * FOLD, cols] = jnp.where(low_lane, swap(left), right).astype(BF16)

    wo_part[...] = dot_nt(gl[...], hidden[...])
    wo_send[...] = wo_part[:, pl.ds(pl.multiple_of((1 - c) * 256, 256), 256)].astype(BF16)
    wo_group = Group(wo_recv)
    wo_group.send(wo_send, wo_recv, sibling)

    def grad_hidden(r, _):
        rows = pl.ds(pl.multiple_of(r * 128, 128), 128)
        gp[rows, :] = (dot(wop[rows, :], gl[...]) * dgelu[rows, :]).astype(BF16)
        return 0

    lax.fori_loop(0, HID // 128, grad_hidden, 0)

    half = (pl.ds(0, ROWS0), pl.ds(ROWS0, ROWS1))
    sib_groups = [Group(sib_recv.at[half[q]]) for q in range(2)]

    def rows_of(core, q):
        return pl.ds(pl.multiple_of(core * 512 + q * ROWS0, 128), (ROWS0, ROWS1)[q])

    def other_half(q):
        sib_send[half[q], :] = dot_nt(lat[rows_of(1 - c, q), :], gp[...]).astype(BF16)
        sib_groups[q].send(sib_send.at[half[q]], sib_recv.at[half[q]], sibling)

    def own_half(q):
        own[half[q], :] = dot_nt(lat[rows_of(c, q), :], gp[...])

    def merged(q):
        sib_groups[q].arrived()
        return (own[half[q], :] + sib_recv[half[q], :].astype(F32)).astype(BF16)

    other_half(0)
    ones = jnp.ones((16, COLS), BF16)
    sum_in = dot_nt(ones, gp[...])[0:1]
    sum_out = dot_nt(ones, gl[...])[0:1]
    rows8 = lax.broadcasted_iota(jnp.int32, (8, 128), 0)
    tile = jnp.where(rows8 == 4, sum_out, 0.0)
    for i in range(4):
        tile = jnp.where(rows8 == i, sum_in[:, 128 * i:128 * i + 128], tile)
    sm_c[pl.ds(c, 1)] = tile.reshape(1, 8, 128)
    smc_group = Group(sm_c.at[0])
    smc_group.send(sm_c.at[c], sm_c.at[c], sibling)
    other_half(1)
    own_half(0)
    own_half(1)

    x_cols = pl.ds(pl.multiple_of(x * 128, 128), 128)
    u_rows = pl.ds(pl.multiple_of(u * CHUNK1, 16), CHUNK1)
    last_rows = pl.ds(ROWS0 + 64, 16)

    wo_group.arrived()
    second = wo_part[:, pl.ds(pl.multiple_of(c * 256, 256), 256)] + wo_recv[...].astype(F32)
    smc_group.arrived()
    sums = jnp.concatenate([sm_c[0] + sm_c[1], jnp.zeros((8, 128), F32)], axis=0).astype(BF16)
    for j in range(4):
        cols = pl.ds(128 * j, 128)
        both = second[32 * j:32 * j + 32]
        part0[ROWS0:ROWS0 + 32, cols] = both[:, 0:128].astype(BF16)
        part0[ROWS0 + 32:ROWS0 + 64, cols] = both[:, 128:256].astype(BF16)
        part0[last_rows, cols] = sums
    x0_recv[x, last_rows] = sums
    part0[0:ROWS0, :] = merged(0)
    x0_group = Group(x0_recv.at[pl.ds(0, 3)])
    for k in FAR4:
        cols = pl.ds(pl.multiple_of(x_at[k] * 128, 128), 128)
        x0_group.send(part0.at[:, cols], x0_recv.at[x], to_x[k])
    part1[...] = merged(1)
    u1_group = Group(u1_recv)
    for k in FAR8:
        rows = pl.ds(pl.multiple_of(u_at[k] * CHUNK1, 16), CHUNK1)
        u1_group.send(part1.at[rows], u1_recv.at[k - 1], to_u[k])

    drain()
    x0_group.arrived()
    total = part0[0:ROWS0 + 64, x_cols].astype(F32)
    for k in range(1, 4):
        total = total + x0_recv[x_at[k], 0:ROWS0 + 64].astype(F32)
    sums = x0_recv[0, last_rows].astype(F32)
    for k in range(1, 4):
        sums = sums + x0_recv[k, last_rows].astype(F32)
    for j in range(8):
        at = ROWS0 + 32 * (j % 2) + 8 * (j // 2)
        s0[j] = jnp.concatenate(
            [total[CHUNK0 * j:CHUNK0 * (j + 1)], total[at:at + 8], sums[0:8]], axis=0).astype(BF16)
    u0_recv[pl.ds(u, 1)] = s0[pl.ds(u, 1)]
    u0_group = Group(u0_recv.at[pl.ds(0, 7)])
    for k in FAR8:
        u0_group.send(s0.at[u_at[k]], u0_recv.at[u], to_u[k])
    u1_group.arrived()
    total = part1[u_rows, :].astype(F32)
    for k in range(7):
        total = total + u1_recv[k].astype(F32)
    s1[...] = total.astype(BF16)
    x1_group = Group(x1_recv)
    for k in FAR4:
        cols = pl.ds(pl.multiple_of(x_at[k] * 128, 128), 128)
        x1_group.send(s1.at[:, cols], x1_recv.at[k - 1], to_x[k])

    x1_group.arrived()
    total = s1[:, x_cols].astype(F32)
    for k in range(3):
        total = total + x1_recv[k].astype(F32)
    v_recv[v, UNIT:UNIT + CHUNK1] = total.astype(BF16)
    u0_group.arrived()
    total = u0_recv[0].astype(F32)
    for k in range(1, 8):
        total = total + u0_recv[k].astype(F32)
    v_recv[v, 0:UNIT] = total.astype(BF16)
    v_group = Group(v_recv.at[pl.ds(0, 7)])
    for k in FAR8:
        v_group.send(v_recv.at[v], v_recv.at[v], to_v[k])
    drain()

    def block(rows_at, rows, cols):
        return gw_ref.at[pl.ds(pl.multiple_of(c * 512 + rows_at, 16), rows), cols]

    v_group.arrived()
    total = v_recv[0].astype(F32)
    for k in range(1, 8):
        total = total + v_recv[k].astype(F32)
    gather[x, u] = total[0:UNIT].astype(BF16)
    u0_group = Group(u0_recv.at[pl.ds(0, 7)])
    for k in FAR8:
        u0_group.send(gather.at[x, u], gather.at[x, u], to_u[k])
    spot = block(ROWS0 + u * CHUNK1, CHUNK1, x_cols)
    spot[...] = total[UNIT:UNIT + CHUNK1].astype(BF16)
    x1_group = Group(x1_recv)
    for k in FAR4:
        x1_group.send(spot, spot, to_x[k])
    for i in range(4):
        gbin_ref[:, 128 * i:128 * i + 128] = total[UNIT - 8 + i:UNIT - 7 + i]
    gbo_ref[...] = total[UNIT - 4:UNIT - 3, 0:VARS]
    drain()

    x1_group.arrived()
    spot = block(ROWS0 + u * CHUNK1, CHUNK1, pl.ds(0, 512))
    u1_group = Group(u1_recv, apart=7)
    u1_copies = [u1_group.send(spot, spot, to_u[k]) for k in FAR8]
    last1 = Group(part1)
    last1.send(spot, spot, sibling)
    u0_group.arrived()
    x0_group = Group(gather.at[pl.ds(0, 3)], apart=3)
    x0_copies = [x0_group.send(gather.at[x], gather.at[x], to_x[k]) for k in FAR4]
    last0 = Group(gather)
    last0.send(gather.at[x], gather_other.at[x], sibling)

    drain()
    loss_group.arrived()
    for t in range(4):
        loss_ref[:, 128 * t:128 * t + 128] = jnp.where(
            low_row, loss_recv[2 * t, 0:1, :], loss_recv[2 * t + 1, 0:1, :])

    near_u = [(k, copy, False) for k, copy in zip(FAR8, u1_copies)][::-1]
    near_x = [(k, copy, True) for k, copy in zip(FAR4, x0_copies)][::-1]
    for k, copy, along_x in near_u[:4] + near_x[:2] + near_u[4:] + near_x[2:]:
        copy.wait_recv()
        if along_x:
            last0.send(gather.at[x_at[4 - k]], gather_other.at[x_at[4 - k]], sibling)
        else:
            spot = block(ROWS0 + u_at[8 - k] * CHUNK1, CHUNK1, pl.ds(0, 512))
            last1.send(spot, spot, sibling)

    def place(source, core):
        for i in range(4):
            for j in range(8):
                rows = pl.ds(pl.multiple_of(core * 512 + CHUNK0 * j, 16), CHUNK0)
                gw_ref[rows, 128 * i:128 * i + 128] = source[i, j, 0:CHUNK0]
                first_row = 32 * i + 8 * (j // 2)
                count = min(8, VARS - first_row)
                if count > 0:
                    cols = pl.ds(pl.multiple_of(core * 256 + 128 * (j % 2), 128), 128)
                    gwo_ref[first_row:first_row + count, cols] = source[i, j, CHUNK0:UNIT].astype(F32)[0:count]

    place(gather, c)
    last1.arrived()
    last0.arrived()
    place(gather_other, 1 - c)
    drain()
    drain()
    assert (len(groups), received[0]) == (N_SENDS, N_RECEIVES), (len(groups), received[0])


def deliver(*refs):
    results, places, sems = refs[0:5], refs[5:10], refs[10]
    copies = [
        pltpu.make_async_copy(src, dst, sems.at[i])
        for i, (src, dst) in enumerate(zip(results, places))
    ]
    for copy in copies:
        copy.start()
    for copy in copies:
        copy.wait()


def per_device(latent, w_in, b_in, output_weight, output_bias, observed_field, area):
    total_columns = latent.shape[2] * lax.axis_size("grid")
    vmem = pl.BlockSpec(memory_space=pltpu.VMEM)
    hbm = pl.BlockSpec(memory_space=pltpu.HBM)

    def scratch(dtype, *shape):
        return pltpu.VMEM(shape, dtype)

    results = (
        jax.ShapeDtypeStruct((1, COLS), F32),
        jax.ShapeDtypeStruct((DIN, HID), BF16),
        jax.ShapeDtypeStruct((1, HID), F32),
        jax.ShapeDtypeStruct((VARS, HID), F32),
        jax.ShapeDtypeStruct((1, VARS), F32),
    )
    operands = (
        latent, w_in, b_in.reshape(1, HID), output_weight.T, output_bias.reshape(1, VARS),
        observed_field, area.reshape(1, COLS),
    )
    made = pl.pallas_call(
        lambda *refs: kernel(total_columns, *refs),
        out_shape=results,
        in_specs=[hbm] * 7,
        out_specs=(vmem,) * 5,
        scratch_shapes=[
            scratch(F32, 1, HID), scratch(BF16, VARS, HID), scratch(F32, 1, VARS),
            scratch(F32, VARS, COLS), scratch(F32, 1, COLS),
            scratch(BF16, DIN, COLS), scratch(BF16, DIN, HID),
            scratch(F32, HID, 128), scratch(F32, HID, COLS), scratch(F32, HID, COLS),
            scratch(BF16, HID, COLS), scratch(BF16, HID, 128), scratch(BF16, 128, HID),
            scratch(F32, 1, 128), scratch(F32, 2 * FOLD, 128),
            scratch(BF16, 2, 2, 2, FOLD, 128), scratch(BF16, 8, FOLD, 128),
            scratch(BF16, 8, FOLD, 128), scratch(BF16, 8, FOLD, 128),
            scratch(F32, 8, 8, 128), scratch(BF16, 128, COLS), scratch(BF16, HID, COLS),
            scratch(BF16, 512, HID), scratch(BF16, 512, HID),
            scratch(F32, 512, HID),
            scratch(F32, 128, HID), scratch(BF16, 128, 256), scratch(BF16, 128, 256),
            scratch(F32, 2, 8, 128),
            scratch(BF16, ROWS0 + 80, HID), scratch(BF16, 4, ROWS0 + 80, 128),
            scratch(BF16, 8, UNIT, 128), scratch(BF16, 8, UNIT, 128),
            scratch(BF16, ROWS1, HID), scratch(BF16, 7, CHUNK1, HID),
            scratch(BF16, CHUNK1, HID), scratch(BF16, 3, CHUNK1, 128),
            scratch(BF16, 8, UNIT + CHUNK1, 128),
            scratch(BF16, 4, 8, UNIT, 128), scratch(BF16, 4, 8, UNIT, 128),
            pltpu.SemaphoreType.DMA((9,)),
            pltpu.SemaphoreType.DMA((N_SENDS,)), pltpu.SemaphoreType.DMA((N_RECEIVES,)),
        ],
        compiler_params=pltpu.CompilerParams(
            collective_id=0, has_side_effects=True, vmem_limit_bytes=40 * 2**20),
        cost_estimate=pl.CostEstimate(
            flops=4 * DIN * HID * COLS, bytes_accessed=4 * 2**20, transcendentals=2 * HID * COLS),
        name="energy_score_step",
    )(*[pltpu.with_memory_space_constraint(operand, pltpu.HBM) for operand in operands])
    loss, grad_w_in, grad_b_in, grad_w_out, grad_b_out = pl.pallas_call(
        deliver,
        out_shape=results,
        in_specs=[vmem] * 5,
        out_specs=(hbm,) * 5,
        scratch_shapes=[pltpu.SemaphoreType.DMA((5,))],
        compiler_params=pltpu.CompilerParams(vmem_limit_bytes=4 * 2**20),
        name="deliver",
    )(*made)
    return (
        loss.reshape(COLS), grad_w_in, grad_b_in.reshape(HID), grad_w_out.T,
        grad_b_out.reshape(VARS),
    )


def solution(mesh):
    placed = (P("member", None, "grid"), P(), P(), P(), P(), P(None, "grid"), P("grid"))
    return jax.shard_map(
        per_device,
        mesh=mesh,
        in_specs=placed,
        out_specs=(P("grid"), P(), P(), P(), P()),
        check_vma=False,
    )
```

```python
import math

import jax
import jax.numpy as jnp
from jax import lax
from jax.experimental import pallas as pl
from jax.experimental.pallas import tpu as pltpu
from jax.sharding import PartitionSpec as P

MESH = pl.DeviceIdType.MESH
F32 = jnp.float32
BF16 = jnp.bfloat16
EPSILON = 1e-05
GELU_A = math.sqrt(2.0 / math.pi)
GELU_B = 0.044715

DIN, HID, VARS = 1024, 512, 83
COLS = 512
FOLD = 48
NX, NU = 4, 8
FAR4 = (2, 1, 3)
FAR8 = (4, 3, 5, 2, 6, 1, 7)
N_SENDS, N_RECEIVES = 24, 34


def dot(a, b):
    return jnp.dot(a, b, preferred_element_type=F32)


def dot_nt(a, b):
    return lax.dot_general(a, b, (((1,), (1,)), ((), ())), preferred_element_type=F32)


def dot_tn(a, b):
    return lax.dot_general(a, b, (((0,), (0,)), ((), ())), preferred_element_type=F32)


def kernel(
    total_columns,
    lat_hbm, win_hbm, bin_hbm, wo_hbm, bo_hbm, obs_hbm, area_hbm,
    loss_ref, gw_ref, gbin_ref, gwo_ref, gbo_ref,
    bin_ref, wo_ref, bo_ref, obs_ref, area_ref, gwo, gwo_low,
    lat, win, bias, pre, dgelu, hidden, wop, wop_t, row, obs_pad,
    f_send, f_recv, g_send, g_recv, loss_recv, gl, gp,
    sib_send, sib_recv, own, part,
    x0_recv, s0, u0_recv, u1_recv, s1, x1_recv, v_recv,
    wo_part, wo_send, wo_recv, wo_rs, wox_recv, wou_src, wou_recv, wov_recv,
    sm_c, sm_x,
    local_sems, send_sems, recv_sems,
):
    member, grid = lax.axis_index("member"), lax.axis_index("grid")
    c, zlo = member & 1, member >> 1
    a, b = zlo >> 1, zlo & 1
    zhi, y, x = grid & 1, (grid >> 1) & 7, grid >> 4
    z = zhi * 4 + zlo
    on_y = 1 - c
    u = y * on_y + z * c
    v = z * on_y + y * c

    def device(x, y, z):
        return ((z & 3) * 2 + c, (x * 8 + y) * 2 + (z >> 2))

    x_at = [(x + k) & 3 for k in range(4)]
    u_at = [(u + k) & 7 for k in range(8)]
    v_at = [(v + k) & 7 for k in range(8)]
    to_x = [(member, (x_at[k] * 8 + y) * 2 + zhi) for k in range(4)]
    to_u = [device(x, u_at[k] * on_y + y * c, z * on_y + u_at[k] * c) for k in range(8)]
    to_v = [device(x, y * on_y + v_at[k] * c, v_at[k] * on_y + z * c) for k in range(8)]

    to_u_other = [(there_u[0] + 1 - 2 * c, there_u[1]) for there_u in to_u]
    sibling = (zlo * 2 + 1 - c, grid)

    def flip(bit, by):
        return 1 - bit if by else bit

    def member_of(rel):
        ra, rb, rc = rel
        return (2 * flip(a, ra) + flip(b, rb)) * 2 + flip(c, rc)

    rels = [(ra, rb, rc) for ra in (1, 0) for rb in (1, 0) for rc in (1, 0)][:-1]

    there = {rel: member_of(rel) for rel in rels}

    groups, fences, received = [], [0, 0], [0]

    class Group:
        def __init__(self, size, apart=0):
            self.size, self.index = size, len(groups)
            self.first, self.apart, self.count = received[0], apart, 0
            received[0] += max(apart, 1)
            groups.append(self)

        def copy(self, src, dst, to, number=0):
            return pltpu.make_async_remote_copy(
                src_ref=src, dst_ref=dst, send_sem=send_sems.at[self.index],
                recv_sem=recv_sems.at[self.first + number], device_id=to, device_id_type=MESH,
            )

        def send(self, src, dst, to):
            copy = self.copy(src, dst, to, self.count if self.apart else 0)
            self.count += 1
            copy.start()
            return copy

        def arrived(self):
            self.copy(self.size, self.size, sibling).wait_recv()

        def left(self):
            self.copy(self.size, self.size, sibling).wait_send()

    def drain():
        for group in groups[fences[-2]:fences[-1]]:
            group.left()
        fences.append(len(groups))

    halves = [1 - a, a]
    load_w = [
        pltpu.make_async_copy(
            win_hbm.at[pl.ds(512 * i, 512)], win.at[pl.ds(512 * i, 512)], local_sems.at[i])
        for i in range(2)
    ]
    load_l = [
        pltpu.make_async_copy(
            lat_hbm.at[0, :, pl.ds(pl.multiple_of(h * 256, 256), 256)],
            lat.at[:, pl.ds(pl.multiple_of(h * 256, 256), 256)], local_sems.at[2 + i])
        for i, h in enumerate(halves)
    ]
    load_small = [
        pltpu.make_async_copy(src, dst, local_sems.at[4 + i])
        for i, (src, dst) in enumerate((
            (bin_hbm, bin_ref), (wo_hbm, wo_ref), (bo_hbm, bo_ref),
            (obs_hbm, obs_ref), (area_hbm, area_ref)))
    ]
    for copy in load_w + load_l[:1] + load_small[:3]:
        copy.start()

    barrier = pltpu.get_barrier_semaphore()
    far, near = rels[:4], rels[4:]
    partners = (
        [way[k] for k in (4, 3, 5) for way in (to_u, to_u_other, to_v)]
        + [(there[rel], grid) for rel in far]
        + [way[k] for k in (2, 6) for way in (to_u, to_u_other, to_v)] + [to_x[2]]
        + [(there[rel], grid) for rel in near]
        + [way[k] for k in (1, 7) for way in (to_u, to_u_other, to_v)] + [to_x[1], to_x[3]]
    )
    for partner in partners:
        pl.semaphore_signal(barrier, inc=1, device_id=partner, device_id_type=MESH)
    for copy in load_l[1:] + load_small[3:]:
        copy.start()

    wop_t[...] = jnp.zeros_like(wop_t)
    row[...] = jnp.zeros_like(row)
    for copy in load_small[:3]:
        copy.wait()
    for i in range(4):
        bias[pl.ds(128 * i, 128), :] = jnp.transpose(
            jnp.broadcast_to(bin_ref[:, pl.ds(128 * i, 128)], (128, 128)))
    wop_t[0:VARS, :] = wo_ref[...]
    row[:, 0:VARS] = bo_ref[...]
    bias_out = jnp.transpose(jnp.broadcast_to(row[...], (128, 128)))[0:2 * FOLD]
    lane = lax.broadcasted_iota(jnp.int32, (FOLD, 128), 1)
    low_lane = lane < 64
    low_row = lax.broadcasted_iota(jnp.int32, (1, 128), 1) < 64

    def swap(value):
        return pltpu.roll(value, 64, 1)

    for copy in load_w:
        copy.wait()

    f_group = Group(f_recv.at[pl.ds(0, 7)])
    for i, h in enumerate(halves):
        cols = pl.ds(pl.multiple_of(h * 256, 256), 256)
        load_l[i].wait()
        pre[:, cols] = dot_tn(win[...], lat[:, cols])

        def activate(r, _):
            rows = pl.ds(pl.multiple_of(r * 128, 128), 128)
            shift = bias[rows, :]
            value = pre[rows, cols] + jnp.concatenate([shift, shift], axis=1)
            pre[rows, cols] = value
            inner = GELU_A * (value + GELU_B * (value * value * value))
            hidden[rows, cols] = (0.5 * value * (1.0 + jnp.tanh(inner))).astype(BF16)
            return 0

        lax.fori_loop(0, HID // 128, activate, 0)
        field = dot(wop_t[0:2 * FOLD, :], hidden[:, cols])
        for t in range(2):
            chunk = (field[:, 128 * t:128 * t + 128] + bias_out).astype(BF16).astype(F32)
            lo, hi = chunk[0:FOLD], chunk[FOLD:2 * FOLD]
            f_send[i, t, 0] = jnp.where(low_lane, lo, swap(hi)).astype(BF16)
            f_send[i, t, 1] = jnp.where(low_lane, swap(lo), hi).astype(BF16)
        if i == 0:
            pl.semaphore_wait(barrier, len(partners))
        for rel in rels:
            if rel[0] == 1 - i:
                src = f_send.at[i, flip(b, rel[1]), flip(c, rel[2])]
                f_group.send(src, f_recv.at[member], (there[rel], grid))
    f_recv[pl.ds(member, 1)] = f_send[1, pl.ds(b, 1), pl.ds(c, 1)].reshape(1, FOLD, 128)

    def derive(r, _):
        rows = pl.ds(pl.multiple_of(r * 128, 128), 128)
        value = pre[rows, :]
        square = value * value
        t = jnp.tanh(GELU_A * (value + GELU_B * (value * square)))
        dgelu[rows, :] = 0.5 * (1.0 + t) + (0.5 * GELU_A) * value * (1.0 - t * t) * (
            1.0 + (3.0 * GELU_B) * square)
        return 0

    lax.fori_loop(0, HID // 128, derive, 0)
    wop[...] = jnp.transpose(wop_t[...])
    for copy in load_small[3:]:
        copy.wait()
    obs_pad[...] = jnp.zeros_like(obs_pad)
    own_cols = pl.ds(pl.multiple_of(zlo * 128, 128), 128)
    obs_pad[0:VARS, :] = obs_ref[:, own_cols]
    lo, hi = obs_pad[0:FOLD], obs_pad[FOLD:2 * FOLD]
    first = c == 0
    observed = jnp.where(low_lane, jnp.where(first, lo, swap(lo)), jnp.where(first, swap(hi), hi))
    area = area_ref[:, own_cols]
    area = jnp.where(low_row, jnp.where(first, area, swap(area)), jnp.where(first, swap(area), area))
    factor = area * (VARS * math.sqrt(8 / total_columns))
    gl[2 * FOLD:128, :] = jnp.zeros((128 - 2 * FOLD, COLS), BF16)

    def norm(difference):
        total = jnp.sum(difference * difference, axis=0, keepdims=True)
        square = (total + swap(total)) / VARS + EPSILON
        inverse = lax.rsqrt(square)
        return square * inverse, inverse

    f_group.arrived()
    fields = [f_recv[i].astype(F32) for i in range(8)]
    grads = []
    true_total = jnp.zeros((1, 128), F32)
    for m in range(8):
        difference = fields[m] - observed
        distance, inverse = norm(difference)
        true_total = true_total + distance
        grads.append(difference * (factor * inverse * (1.0 / (VARS * 8))))
    pair_total = jnp.full((1, 128), 8.0 * math.sqrt(EPSILON), F32)
    for m in range(8):
        for n in range(m + 1, 8):
            difference = fields[m] - fields[n]
            distance, inverse = norm(difference)
            pair_total = pair_total + 2.0 * distance
            pull = difference * (factor * inverse * (1.0 / (VARS * 64)))
            grads[m] = grads[m] - pull
            grads[n] = grads[n] + pull
    for m in range(8):
        g_send[m] = grads[m].astype(BF16)
    g_group = Group(g_recv.at[pl.ds(0, 7)], apart=7)
    g_copies = {
        rel: g_group.send(g_send.at[there[rel]], g_recv.at[member], (there[rel], grid))
        for rel in rels}
    g_recv[pl.ds(member, 1)] = g_send[pl.ds(member, 1)]
    loss = true_total * (1.0 / 8) - pair_total * (1.0 / 128)
    loss_recv[pl.ds(member, 1)] = jnp.broadcast_to(loss, (1, 8, 128))
    loss_group = Group(loss_recv.at[pl.ds(0, 7)])
    for rel in rels:
        loss_group.send(loss_recv.at[member], loss_recv.at[member], (there[rel], grid))

    drain()
    for ra, rb in ((0, 0), (0, 1), (1, 0), (1, 1)):
        for rel in rels:
            if rel[:2] == (ra, rb):
                g_copies[rel].wait_recv()
        t = 2 * flip(a, ra) + flip(b, rb)
        left, right = g_recv[2 * t].astype(F32), g_recv[2 * t + 1].astype(F32)
        cols = pl.ds(pl.multiple_of(128 * t, 128), 128)
        gl[0:FOLD, cols] = jnp.where(low_lane, left, swap(right)).astype(BF16)
        gl[FOLD:2 * FOLD, cols] = jnp.where(low_lane, swap(left), right).astype(BF16)
        gp[:, cols] = (dot(wop[...], gl[:, cols]) * dgelu[:, cols]).astype(BF16)

    sib_groups = [Group(sib_recv.at[q]) for q in range(2)]
    for q in range(2):
        rows = pl.ds(pl.multiple_of((1 - c) * 512 + q * 256, 256), 256)
        sib_send[q] = dot_nt(lat[rows, :], gp[...]).astype(BF16)
        sib_groups[q].send(sib_send.at[q], sib_recv.at[q], sibling)
    wo_part[...] = dot_nt(hidden[...], gl[...])
    wo_send[...] = wo_part[pl.ds(pl.multiple_of((1 - c) * 256, 256), 256), :].astype(BF16)
    wo_group = Group(wo_recv)
    wo_group.send(wo_send, wo_recv, sibling)
    ones = jnp.ones((16, COLS), BF16)
    sum_in = dot_nt(ones, gp[...])[0:1]
    sum_out = dot_nt(ones, gl[...])[0:1]
    rows8 = lax.broadcasted_iota(jnp.int32, (8, 128), 0)
    tile = jnp.where(rows8 == 4, sum_out, 0.0)
    for i in range(4):
        tile = jnp.where(rows8 == i, sum_in[:, 128 * i:128 * i + 128], tile)
    sm_c[pl.ds(c, 1)] = tile.reshape(1, 8, 128)
    smc_group = Group(sm_c.at[0])
    smc_group.send(sm_c.at[c], sm_c.at[c], sibling)

    x_cols = pl.ds(pl.multiple_of(x * 128, 128), 128)
    u_rows = pl.ds(pl.multiple_of(u * 32, 32), 32)

    def own_half(q):
        rows = pl.ds(pl.multiple_of(c * 512 + q * 256, 256), 256)
        own[q] = dot_nt(lat[rows, :], gp[...])

    def merge(q):
        sib_groups[q].arrived()
        part[q] = (own[q] + sib_recv[q].astype(F32)).astype(BF16)

    own_half(0)
    own_half(1)
    merge(0)
    x0_group = Group(x0_recv)
    for k in FAR4:
        cols = pl.ds(pl.multiple_of(x_at[k] * 128, 128), 128)
        x0_group.send(part.at[0, :, cols], x0_recv.at[k - 1], to_x[k])
    merge(1)
    u1_group = Group(u1_recv)
    for k in FAR8:
        rows = pl.ds(pl.multiple_of(u_at[k] * 32, 32), 32)
        u1_group.send(part.at[1, rows], u1_recv.at[k - 1], to_u[k])
    wo_group.arrived()
    wo_rs[...] = (
        wo_part[pl.ds(pl.multiple_of(c * 256, 256), 256), :] + wo_recv[...].astype(F32)).astype(BF16)
    wox_group = Group(wox_recv)
    for k in FAR4:
        rows = pl.ds(pl.multiple_of(x_at[k] * 64, 64), 64)
        wox_group.send(wo_rs.at[rows], wox_recv.at[k - 1], to_x[k])
    smc_group.arrived()
    sm_x[pl.ds(x, 1)] = (sm_c[0] + sm_c[1]).reshape(1, 8, 128)
    smx_group = Group(sm_x.at[pl.ds(0, 3)])
    for k in FAR4:
        smx_group.send(sm_x.at[x], sm_x.at[x], to_x[k])

    drain()
    x0_group.arrived()
    total = part[0, :, x_cols].astype(F32)
    for k in range(3):
        total = total + x0_recv[k].astype(F32)
    s0[...] = total.astype(BF16)
    u0_group = Group(u0_recv)
    for k in FAR8:
        rows = pl.ds(pl.multiple_of(u_at[k] * 32, 32), 32)
        u0_group.send(s0.at[rows], u0_recv.at[k - 1], to_u[k])
    wox_group.arrived()
    total = wo_rs[pl.ds(pl.multiple_of(x * 64, 64), 64), :].astype(F32)
    for k in range(3):
        total = total + wox_recv[k].astype(F32)
    smx_group.arrived()
    small = sm_x[0] + sm_x[1] + sm_x[2] + sm_x[3]
    for j in range(8):
        wou_src[j, 0:8] = total[8 * j:8 * j + 8]
        wou_src[j, 8:16] = small
    wou_recv[pl.ds(u, 1)] = wou_src[pl.ds(u, 1)]
    wou_group = Group(wou_recv.at[pl.ds(0, 7)])
    for k in FAR8:
        wou_group.send(wou_src.at[u_at[k]], wou_recv.at[u], to_u[k])
    u1_group.arrived()
    total = part[1, u_rows, :].astype(F32)
    for k in range(7):
        total = total + u1_recv[k].astype(F32)
    s1[...] = total.astype(BF16)
    x1_group = Group(x1_recv)
    for k in FAR4:
        cols = pl.ds(pl.multiple_of(x_at[k] * 128, 128), 128)
        x1_group.send(s1.at[:, cols], x1_recv.at[k - 1], to_x[k])

    x1_group.arrived()
    total = s1[:, x_cols].astype(F32)
    for k in range(3):
        total = total + x1_recv[k].astype(F32)
    v_recv[v, 1] = total.astype(BF16)
    u0_group.arrived()
    total = s0[u_rows, :].astype(F32)
    for k in range(7):
        total = total + u0_recv[k].astype(F32)
    v_recv[v, 0] = total.astype(BF16)
    v_group = Group(v_recv.at[pl.ds(0, 7)])
    for k in FAR8:
        v_group.send(v_recv.at[v], v_recv.at[v], to_v[k])
    wou_group.arrived()
    total = wou_recv[0]
    for k in range(1, 8):
        total = total + wou_recv[k]
    wov_recv[pl.ds(v, 1)] = total.reshape(1, 16, 128)
    wov_group = Group(wov_recv.at[pl.ds(0, 7)])
    for k in FAR8:
        wov_group.send(wov_recv.at[v], wov_recv.at[v], to_v[k])
    drain()

    base = c * 512

    def block(q, rows_at, rows, cols):
        return gw_ref.at[pl.ds(pl.multiple_of(base + q * 256 + rows_at, 32), rows), cols]

    v_group.arrived()
    total = v_recv[0].astype(F32)
    for k in range(1, 8):
        total = total + v_recv[k].astype(F32)
    total = total.astype(BF16)
    spot1 = block(1, u * 32, 32, x_cols)
    spot1[...] = total[1]
    spot0 = block(0, u * 32, 32, x_cols)
    spot0[...] = total[0]
    u0_group = Group(u0_recv)
    for k in FAR8:
        u0_group.send(spot0, spot0, to_u[k])
    x1_group = Group(x1_recv)
    for k in FAR4:
        x1_group.send(spot1, spot1, to_x[k])
    wov_group.arrived()
    total = wov_recv[0]
    for k in range(1, 8):
        total = total + wov_recv[k]
    spot = gwo.at[pl.ds(pl.multiple_of(c * 256 + x * 64 + u * 8, 8), 8)]
    spot[...] = total[0:8]
    wou_group = Group(loss_recv.at[pl.ds(0, 7)])
    for k in FAR8:
        wou_group.send(spot, spot, to_u[k])
    for i in range(4):
        gbin_ref[:, 128 * i:128 * i + 128] = total[8 + i:9 + i]
    gbo_ref[...] = total[12:13, 0:VARS]
    drain()

    x1_group.arrived()
    spot = block(1, u * 32, 32, pl.ds(0, 512))
    u1_group, last = Group(u1_recv), Group(part)
    for k in FAR8:
        u1_group.send(spot, spot, to_u[k])
        last.send(spot, spot, to_u_other[k])
    last.send(spot, spot, sibling)
    u0_group.arrived()
    spot = block(0, 0, 256, x_cols)
    x0_group = Group(x0_recv, apart=3)
    x0_copies = [x0_group.send(spot, spot, to_x[k]) for k in FAR4]
    last.send(spot, spot, sibling)
    wou_group.arrived()
    rows = pl.ds(pl.multiple_of(c * 256 + x * 64, 64), 64)
    spot = gwo_low.at[rows]
    spot[...] = gwo[rows].astype(BF16)
    wox_group = Group(wox_recv, apart=3)
    wox_copies = [wox_group.send(spot, spot, to_x[k]) for k in FAR4]
    last_wo = Group(wo_recv)
    last_wo.send(spot, spot, sibling)

    drain()
    loss_group.arrived()
    for t in range(4):
        loss_ref[:, 128 * t:128 * t + 128] = jnp.where(
            low_row, loss_recv[2 * t, 0:1, :], loss_recv[2 * t + 1, 0:1, :])

    for k, copy in reversed(list(zip(FAR4, x0_copies))):
        copy.wait_recv()
        cols = pl.ds(pl.multiple_of(x_at[4 - k] * 128, 128), 128)
        spot = block(0, 0, 256, cols)
        last.send(spot, spot, sibling)
    for k, copy in reversed(list(zip(FAR4, wox_copies))):
        copy.wait_recv()
        spot = gwo_low.at[pl.ds(pl.multiple_of(c * 256 + x_at[4 - k] * 64, 64), 64)]
        last_wo.send(spot, spot, sibling)
    last_wo.arrived()
    gwo_ref[...] = jnp.transpose(gwo_low[...].astype(F32))[0:VARS]
    u1_group.arrived()
    last.arrived()
    drain()
    drain()
    assert len(groups) == N_SENDS and received[0] == N_RECEIVES


def deliver(*refs):
    results, places, sems = refs[0:5], refs[5:10], refs[10]
    copies = [
        pltpu.make_async_copy(src, dst, sems.at[i])
        for i, (src, dst) in enumerate(zip(results, places))
    ]
    for copy in copies:
        copy.start()
    for copy in copies:
        copy.wait()


def per_device(latent, w_in, b_in, output_weight, output_bias, observed_field, area):
    total_columns = latent.shape[2] * lax.axis_size("grid")
    vmem = pl.BlockSpec(memory_space=pltpu.VMEM)
    hbm = pl.BlockSpec(memory_space=pltpu.HBM)

    def scratch(dtype, *shape):
        return pltpu.VMEM(shape, dtype)

    results = (
        jax.ShapeDtypeStruct((1, COLS), F32),
        jax.ShapeDtypeStruct((DIN, HID), BF16),
        jax.ShapeDtypeStruct((1, HID), F32),
        jax.ShapeDtypeStruct((VARS, HID), F32),
        jax.ShapeDtypeStruct((1, VARS), F32),
    )
    operands = (
        latent, w_in, b_in.reshape(1, HID), output_weight.T, output_bias.reshape(1, VARS),
        observed_field, area.reshape(1, COLS),
    )
    made = pl.pallas_call(
        lambda *refs: kernel(total_columns, *refs),
        out_shape=results,
        in_specs=[hbm] * 7,
        out_specs=(vmem,) * 5,
        scratch_shapes=[
            scratch(F32, 1, HID), scratch(BF16, VARS, HID), scratch(F32, 1, VARS),
            scratch(F32, VARS, COLS), scratch(F32, 1, COLS), scratch(F32, HID, 128),
            scratch(BF16, HID, 128),
            scratch(BF16, DIN, COLS), scratch(BF16, DIN, HID),
            scratch(F32, HID, 128), scratch(F32, HID, COLS), scratch(F32, HID, COLS),
            scratch(BF16, HID, COLS), scratch(BF16, HID, 128), scratch(BF16, 128, HID),
            scratch(F32, 1, 128), scratch(F32, 2 * FOLD, 128),
            scratch(BF16, 2, 2, 2, FOLD, 128), scratch(BF16, 8, FOLD, 128),
            scratch(BF16, 8, FOLD, 128), scratch(BF16, 8, FOLD, 128),
            scratch(F32, 8, 8, 128), scratch(BF16, 128, COLS), scratch(BF16, HID, COLS),
            scratch(BF16, 2, 256, HID), scratch(BF16, 2, 256, HID),
            scratch(F32, 2, 256, HID), scratch(BF16, 2, 256, HID),
            scratch(BF16, 3, 256, 128), scratch(BF16, 256, 128),
            scratch(BF16, 7, 32, 128),
            scratch(BF16, 7, 32, HID), scratch(BF16, 32, HID),
            scratch(BF16, 3, 32, 128), scratch(BF16, 8, 2, 32, 128),
            scratch(F32, HID, 128), scratch(BF16, 256, 128), scratch(BF16, 256, 128),
            scratch(BF16, 256, 128), scratch(BF16, 3, 64, 128),
            scratch(F32, 8, 16, 128), scratch(F32, 8, 16, 128), scratch(F32, 8, 16, 128),
            scratch(F32, 2, 8, 128), scratch(F32, 4, 8, 128),
            pltpu.SemaphoreType.DMA((9,)),
            pltpu.SemaphoreType.DMA((N_SENDS,)), pltpu.SemaphoreType.DMA((N_RECEIVES,)),
        ],
        compiler_params=pltpu.CompilerParams(
            collective_id=0, has_side_effects=True, vmem_limit_bytes=40 * 2**20),
        cost_estimate=pl.CostEstimate(
            flops=4 * DIN * HID * COLS, bytes_accessed=4 * 2**20, transcendentals=2 * HID * COLS),
        name="energy_score_step",
    )(*[pltpu.with_memory_space_constraint(operand, pltpu.HBM) for operand in operands])
    loss, grad_w_in, grad_b_in, grad_w_out, grad_b_out = pl.pallas_call(
        deliver,
        out_shape=results,
        in_specs=[vmem] * 5,
        out_specs=(hbm,) * 5,
        scratch_shapes=[pltpu.SemaphoreType.DMA((5,))],
        compiler_params=pltpu.CompilerParams(vmem_limit_bytes=4 * 2**20),
        name="deliver",
    )(*made)
    return (
        loss.reshape(COLS), grad_w_in, grad_b_in.reshape(HID), grad_w_out.T,
        grad_b_out.reshape(VARS),
    )


def solution(mesh):
    placed = (P("member", None, "grid"), P(), P(), P(), P(), P(None, "grid"), P("grid"))
    return jax.shard_map(
        per_device,
        mesh=mesh,
        in_specs=placed,
        out_specs=(P("grid"), P(), P(), P(), P()),
        check_vma=False,
    )
```

```python
import math

import jax
import jax.numpy as jnp
from jax import lax
from jax.experimental import pallas as pl
from jax.experimental.pallas import tpu as pltpu
from jax.sharding import PartitionSpec as P

MESH = pl.DeviceIdType.MESH
F32 = jnp.float32
BF16 = jnp.bfloat16
EPSILON = 1e-05
GELU_A = math.sqrt(2.0 / math.pi)
GELU_B = 0.044715

DIN, HID, VARS = 1024, 512, 83
COLS = 512
FOLD = 48
NX, NU = 4, 8
FAR4 = (2, 1, 3)
FAR8 = (4, 3, 5, 2, 6, 1, 7)
N_SENDS, N_RECEIVES = 27, 49


def dot(a, b):
    return jnp.dot(a, b, preferred_element_type=F32)


def dot_nt(a, b):
    return lax.dot_general(a, b, (((1,), (1,)), ((), ())), preferred_element_type=F32)


def dot_tn(a, b):
    return lax.dot_general(a, b, (((0,), (0,)), ((), ())), preferred_element_type=F32)


def kernel(
    total_columns,
    lat_hbm, win_hbm, bin_hbm, wo_hbm, bo_hbm, obs_hbm, area_hbm,
    loss_ref, gw_ref, gbin_ref, gwo_ref, gbo_ref,
    bin_ref, wo_ref, bo_ref, obs_ref, area_ref, gwo, gwo_low,
    lat, win, bias, pre, dgelu, hidden, wop, wop_t, row, obs_pad,
    f_send, f_recv, g_send, g_recv, loss_recv, gl, gp,
    sib_send, sib_recv, own, part,
    x0_recv, s0, u0_recv, u1_recv, w1_recv, s1, x1_recv, v_recv, w_recv,
    wo_part, wo_send, wo_recv, wo_rs, wox_recv, wou_src, wou_recv, wov_recv,
    sm_c, sm_x,
    local_sems, send_sems, recv_sems,
):
    member, grid = lax.axis_index("member"), lax.axis_index("grid")
    c, zlo = member & 1, member >> 1
    a, b = zlo >> 1, zlo & 1
    zhi, y, x = grid & 1, (grid >> 1) & 7, grid >> 4
    z = zhi * 4 + zlo
    on_y = 1 - c
    u = y * on_y + z * c
    v = z * on_y + y * c

    def device(x, y, z):
        return ((z & 3) * 2 + c, (x * 8 + y) * 2 + (z >> 2))

    x_at = [(x + k) & 3 for k in range(4)]
    u_at = [(u + k) & 7 for k in range(8)]
    v_at = [(v + k) & 7 for k in range(8)]
    to_x = [(member, (x_at[k] * 8 + y) * 2 + zhi) for k in range(4)]
    to_u = [device(x, u_at[k] * on_y + y * c, z * on_y + u_at[k] * c) for k in range(8)]
    to_v = [device(x, y * on_y + v_at[k] * c, v_at[k] * on_y + z * c) for k in range(8)]

    sibling = (zlo * 2 + 1 - c, grid)

    def flip(bit, by):
        return 1 - bit if by else bit

    def member_of(rel):
        ra, rb, rc = rel
        return (2 * flip(a, ra) + flip(b, rb)) * 2 + flip(c, rc)

    rels = [(ra, rb, rc) for ra in (1, 0) for rb in (1, 0) for rc in (1, 0)][:-1]

    there = {rel: member_of(rel) for rel in rels}

    groups, fences, received = [], [0, 0], [0]

    class Group:
        def __init__(self, size, apart=0):
            self.size, self.index = size, len(groups)
            self.first, self.apart, self.count = received[0], apart, 0
            received[0] += max(apart, 1)
            groups.append(self)

        def copy(self, src, dst, to, number=0):
            return pltpu.make_async_remote_copy(
                src_ref=src, dst_ref=dst, send_sem=send_sems.at[self.index],
                recv_sem=recv_sems.at[self.first + number], device_id=to, device_id_type=MESH,
            )

        def send(self, src, dst, to):
            copy = self.copy(src, dst, to, self.count if self.apart else 0)
            self.count += 1
            copy.start()
            return copy

        def arrived(self):
            self.copy(self.size, self.size, sibling).wait_recv()

        def left(self):
            self.copy(self.size, self.size, sibling).wait_send()

    def drain():
        for group in groups[fences[-2]:fences[-1]]:
            group.left()
        fences.append(len(groups))

    halves = [1 - a, a]
    load_w = [
        pltpu.make_async_copy(
            win_hbm.at[pl.ds(512 * i, 512)], win.at[pl.ds(512 * i, 512)], local_sems.at[i])
        for i in range(2)
    ]
    load_l = [
        pltpu.make_async_copy(
            lat_hbm.at[0, :, pl.ds(pl.multiple_of(h * 256, 256), 256)],
            lat.at[:, pl.ds(pl.multiple_of(h * 256, 256), 256)], local_sems.at[2 + i])
        for i, h in enumerate(halves)
    ]
    load_small = [
        pltpu.make_async_copy(src, dst, local_sems.at[4 + i])
        for i, (src, dst) in enumerate((
            (bin_hbm, bin_ref), (wo_hbm, wo_ref), (bo_hbm, bo_ref),
            (obs_hbm, obs_ref), (area_hbm, area_ref)))
    ]
    for copy in load_w + load_l[:1] + load_small[:3]:
        copy.start()

    barrier = pltpu.get_barrier_semaphore()
    far, near = rels[:4], rels[4:]
    partners = (
        [way[k] for k in (4, 3, 5) for way in (to_u, to_v)]
        + [(there[rel], grid) for rel in far]
        + [way[k] for k in (2, 6) for way in (to_u, to_v)] + [to_x[2]]
        + [(there[rel], grid) for rel in near]
        + [way[k] for k in (1, 7) for way in (to_u, to_v)] + [to_x[1], to_x[3]]
    )
    for partner in partners:
        pl.semaphore_signal(barrier, inc=1, device_id=partner, device_id_type=MESH)
    for copy in load_l[1:] + load_small[3:]:
        copy.start()

    wop_t[...] = jnp.zeros_like(wop_t)
    row[...] = jnp.zeros_like(row)
    for copy in load_small[:3]:
        copy.wait()
    for i in range(4):
        bias[pl.ds(128 * i, 128), :] = jnp.transpose(
            jnp.broadcast_to(bin_ref[:, pl.ds(128 * i, 128)], (128, 128)))
    wop_t[0:VARS, :] = wo_ref[...]
    row[:, 0:VARS] = bo_ref[...]
    bias_out = jnp.transpose(jnp.broadcast_to(row[...], (128, 128)))[0:2 * FOLD]
    lane = lax.broadcasted_iota(jnp.int32, (FOLD, 128), 1)
    low_lane = lane < 64
    low_row = lax.broadcasted_iota(jnp.int32, (1, 128), 1) < 64

    def swap(value):
        return pltpu.roll(value, 64, 1)

    for copy in load_w:
        copy.wait()

    f_group = Group(f_recv.at[pl.ds(0, 7)])
    for i, h in enumerate(halves):
        cols = pl.ds(pl.multiple_of(h * 256, 256), 256)
        load_l[i].wait()
        pre[:, cols] = dot_tn(win[...], lat[:, cols])

        def activate(r, _):
            rows = pl.ds(pl.multiple_of(r * 128, 128), 128)
            shift = bias[rows, :]
            value = pre[rows, cols] + jnp.concatenate([shift, shift], axis=1)
            pre[rows, cols] = value
            inner = GELU_A * (value + GELU_B * (value * value * value))
            hidden[rows, cols] = (0.5 * value * (1.0 + jnp.tanh(inner))).astype(BF16)
            return 0

        lax.fori_loop(0, HID // 128, activate, 0)
        field = dot(wop_t[0:2 * FOLD, :], hidden[:, cols])
        for t in range(2):
            chunk = (field[:, 128 * t:128 * t + 128] + bias_out).astype(BF16).astype(F32)
            lo, hi = chunk[0:FOLD], chunk[FOLD:2 * FOLD]
            f_send[i, t, 0] = jnp.where(low_lane, lo, swap(hi)).astype(BF16)
            f_send[i, t, 1] = jnp.where(low_lane, swap(lo), hi).astype(BF16)
        if i == 0:
            pl.semaphore_wait(barrier, len(partners))
        for rel in rels:
            if rel[0] == 1 - i:
                src = f_send.at[i, flip(b, rel[1]), flip(c, rel[2])]
                f_group.send(src, f_recv.at[member], (there[rel], grid))
    f_recv[pl.ds(member, 1)] = f_send[1, pl.ds(b, 1), pl.ds(c, 1)].reshape(1, FOLD, 128)

    def derive(r, _):
        rows = pl.ds(pl.multiple_of(r * 128, 128), 128)
        value = pre[rows, :]
        square = value * value
        t = jnp.tanh(GELU_A * (value + GELU_B * (value * square)))
        dgelu[rows, :] = 0.5 * (1.0 + t) + (0.5 * GELU_A) * value * (1.0 - t * t) * (
            1.0 + (3.0 * GELU_B) * square)
        return 0

    lax.fori_loop(0, HID // 128, derive, 0)
    wop[...] = jnp.transpose(wop_t[...])
    for copy in load_small[3:]:
        copy.wait()
    obs_pad[...] = jnp.zeros_like(obs_pad)
    own_cols = pl.ds(pl.multiple_of(zlo * 128, 128), 128)
    obs_pad[0:VARS, :] = obs_ref[:, own_cols]
    lo, hi = obs_pad[0:FOLD], obs_pad[FOLD:2 * FOLD]
    first = c == 0
    observed = jnp.where(low_lane, jnp.where(first, lo, swap(lo)), jnp.where(first, swap(hi), hi))
    area = area_ref[:, own_cols]
    area = jnp.where(low_row, jnp.where(first, area, swap(area)), jnp.where(first, swap(area), area))
    factor = area * (VARS * math.sqrt(8 / total_columns))
    gl[2 * FOLD:128, :] = jnp.zeros((128 - 2 * FOLD, COLS), BF16)

    def norm(difference):
        total = jnp.sum(difference * difference, axis=0, keepdims=True)
        square = (total + swap(total)) / VARS + EPSILON
        inverse = lax.rsqrt(square)
        return square * inverse, inverse

    f_group.arrived()
    fields = [f_recv[i].astype(F32) for i in range(8)]
    grads = []
    true_total = jnp.zeros((1, 128), F32)
    for m in range(8):
        difference = fields[m] - observed
        distance, inverse = norm(difference)
        true_total = true_total + distance
        grads.append(difference * (factor * inverse * (1.0 / (VARS * 8))))
    pair_total = jnp.full((1, 128), 8.0 * math.sqrt(EPSILON), F32)
    for m in range(8):
        for n in range(m + 1, 8):
            difference = fields[m] - fields[n]
            distance, inverse = norm(difference)
            pair_total = pair_total + 2.0 * distance
            pull = difference * (factor * inverse * (1.0 / (VARS * 64)))
            grads[m] = grads[m] - pull
            grads[n] = grads[n] + pull
    for m in range(8):
        g_send[m] = grads[m].astype(BF16)
    g_group = Group(g_recv.at[pl.ds(0, 7)], apart=7)
    g_copies = {
        rel: g_group.send(g_send.at[there[rel]], g_recv.at[member], (there[rel], grid))
        for rel in rels}
    g_recv[pl.ds(member, 1)] = g_send[pl.ds(member, 1)]
    loss = true_total * (1.0 / 8) - pair_total * (1.0 / 128)
    loss_recv[pl.ds(member, 1)] = jnp.broadcast_to(loss, (1, 8, 128))
    loss_group = Group(loss_recv.at[pl.ds(0, 7)])
    for rel in rels:
        loss_group.send(loss_recv.at[member], loss_recv.at[member], (there[rel], grid))

    drain()
    for ra, rb in ((0, 0), (0, 1), (1, 0), (1, 1)):
        for rel in rels:
            if rel[:2] == (ra, rb):
                g_copies[rel].wait_recv()
        t = 2 * flip(a, ra) + flip(b, rb)
        left, right = g_recv[2 * t].astype(F32), g_recv[2 * t + 1].astype(F32)
        cols = pl.ds(pl.multiple_of(128 * t, 128), 128)
        gl[0:FOLD, cols] = jnp.where(low_lane, left, swap(right)).astype(BF16)
        gl[FOLD:2 * FOLD, cols] = jnp.where(low_lane, swap(left), right).astype(BF16)
        gp[:, cols] = (dot(wop[...], gl[:, cols]) * dgelu[:, cols]).astype(BF16)

    sib_groups = [Group(sib_recv.at[q]) for q in range(2)]
    for q in range(2):
        rows = pl.ds(pl.multiple_of((1 - c) * 512 + q * 256, 256), 256)
        sib_send[q] = dot_nt(lat[rows, :], gp[...]).astype(BF16)
        sib_groups[q].send(sib_send.at[q], sib_recv.at[q], sibling)
    wo_part[...] = dot_nt(hidden[...], gl[...])
    wo_send[...] = wo_part[pl.ds(pl.multiple_of((1 - c) * 256, 256), 256), :].astype(BF16)
    wo_group = Group(wo_recv)
    wo_group.send(wo_send, wo_recv, sibling)
    ones = jnp.ones((16, COLS), BF16)
    sum_in = dot_nt(ones, gp[...])[0:1]
    sum_out = dot_nt(ones, gl[...])[0:1]
    rows8 = lax.broadcasted_iota(jnp.int32, (8, 128), 0)
    tile = jnp.where(rows8 == 4, sum_out, 0.0)
    for i in range(4):
        tile = jnp.where(rows8 == i, sum_in[:, 128 * i:128 * i + 128], tile)
    sm_c[pl.ds(c, 1)] = tile.reshape(1, 8, 128)
    smc_group = Group(sm_c.at[0])
    smc_group.send(sm_c.at[c], sm_c.at[c], sibling)

    x_cols = pl.ds(pl.multiple_of(x * 128, 128), 128)
    u_rows = pl.ds(pl.multiple_of(u * 32, 32), 32)

    def own_half(q):
        rows = pl.ds(pl.multiple_of(c * 512 + q * 256, 256), 256)
        own[q] = dot_nt(lat[rows, :], gp[...])

    def merge(q):
        sib_groups[q].arrived()
        part[q] = (own[q] + sib_recv[q].astype(F32)).astype(BF16)

    own_half(0)
    own_half(1)
    merge(0)
    x0_group = Group(x0_recv)
    for k in FAR4:
        cols = pl.ds(pl.multiple_of(x_at[k] * 128, 128), 128)
        x0_group.send(part.at[0, :, cols], x0_recv.at[k - 1], to_x[k])
    merge(1)
    u1_group, w1_group = Group(u1_recv), Group(w1_recv)
    for k in FAR8:
        rows = pl.ds(pl.multiple_of(u_at[k] * 16, 16), 16)
        u1_group.send(part.at[1, rows], u1_recv.at[k - 1], to_u[k])
        rows = pl.ds(pl.multiple_of(128 + v_at[k] * 16, 16), 16)
        w1_group.send(part.at[1, rows], w1_recv.at[k - 1], to_v[k])
    wo_group.arrived()
    wo_rs[...] = (
        wo_part[pl.ds(pl.multiple_of(c * 256, 256), 256), :] + wo_recv[...].astype(F32)).astype(BF16)
    wox_group = Group(wox_recv)
    for k in FAR4:
        rows = pl.ds(pl.multiple_of(x_at[k] * 64, 64), 64)
        wox_group.send(wo_rs.at[rows], wox_recv.at[k - 1], to_x[k])
    smc_group.arrived()
    sm_x[pl.ds(x, 1)] = (sm_c[0] + sm_c[1]).reshape(1, 8, 128)
    smx_group = Group(sm_x.at[pl.ds(0, 3)])
    for k in FAR4:
        smx_group.send(sm_x.at[x], sm_x.at[x], to_x[k])

    drain()
    x0_group.arrived()
    total = part[0, :, x_cols].astype(F32)
    for k in range(3):
        total = total + x0_recv[k].astype(F32)
    s0[...] = total.astype(BF16)
    u0_group = Group(u0_recv)
    for k in FAR8:
        rows = pl.ds(pl.multiple_of(u_at[k] * 32, 32), 32)
        u0_group.send(s0.at[rows], u0_recv.at[k - 1], to_u[k])
    wox_group.arrived()
    total = wo_rs[pl.ds(pl.multiple_of(x * 64, 64), 64), :].astype(F32)
    for k in range(3):
        total = total + wox_recv[k].astype(F32)
    smx_group.arrived()
    small = sm_x[0] + sm_x[1] + sm_x[2] + sm_x[3]
    for j in range(8):
        wou_src[j, 0:8] = total[8 * j:8 * j + 8]
        wou_src[j, 8:16] = small
    wou_recv[pl.ds(u, 1)] = wou_src[pl.ds(u, 1)]
    wou_group = Group(wou_recv.at[pl.ds(0, 7)])
    for k in FAR8:
        wou_group.send(wou_src.at[u_at[k]], wou_recv.at[u], to_u[k])
    for group, received_1, at, place in ((u1_group, u1_recv, u * 16, 0), (w1_group, w1_recv, 128 + v * 16, 16)):
        group.arrived()
        total = part[1, pl.ds(pl.multiple_of(at, 16), 16), :].astype(F32)
        for k in range(7):
            total = total + received_1[k].astype(F32)
        s1[place:place + 16, :] = total.astype(BF16)
    x1_group = Group(x1_recv)
    for k in FAR4:
        cols = pl.ds(pl.multiple_of(x_at[k] * 128, 128), 128)
        x1_group.send(s1.at[:, cols], x1_recv.at[k - 1], to_x[k])

    x1_group.arrived()
    total = s1[:, x_cols].astype(F32)
    for k in range(3):
        total = total + x1_recv[k].astype(F32)
    total = total.astype(BF16)
    v_recv[v, 32:48] = total[0:16]
    w_recv[u] = total[16:32]
    u0_group.arrived()
    total = s0[u_rows, :].astype(F32)
    for k in range(7):
        total = total + u0_recv[k].astype(F32)
    v_recv[v, 0:32] = total.astype(BF16)
    v_group, w_group = Group(v_recv.at[pl.ds(0, 7)]), Group(w_recv.at[pl.ds(0, 7)])
    for k in FAR8:
        v_group.send(v_recv.at[v], v_recv.at[v], to_v[k])
        w_group.send(w_recv.at[u], w_recv.at[u], to_u[k])
    wou_group.arrived()
    total = wou_recv[0]
    for k in range(1, 8):
        total = total + wou_recv[k]
    wov_recv[pl.ds(v, 1)] = total.reshape(1, 16, 128)
    wov_group = Group(wov_recv.at[pl.ds(0, 7)])
    for k in FAR8:
        wov_group.send(wov_recv.at[v], wov_recv.at[v], to_v[k])
    drain()

    base = c * 512

    def block(q, rows_at, rows, cols):
        return gw_ref.at[pl.ds(pl.multiple_of(base + q * 256 + rows_at, 16), rows), cols]

    v_group.arrived()
    total = v_recv[0].astype(F32)
    for k in range(1, 8):
        total = total + v_recv[k].astype(F32)
    total = total.astype(BF16)
    spot0 = block(0, u * 32, 32, x_cols)
    spot0[...] = total[0:32]
    u0_group = Group(u0_recv)
    for k in FAR8:
        u0_group.send(spot0, spot0, to_u[k])
    spot1 = block(1, u * 16, 16, x_cols)
    spot1[...] = total[32:48]
    w_group.arrived()
    total = w_recv[0].astype(F32)
    for k in range(1, 8):
        total = total + w_recv[k].astype(F32)
    spot2 = block(1, 128 + v * 16, 16, x_cols)
    spot2[...] = total.astype(BF16)
    x1_group = Group(x1_recv)
    for k in FAR4:
        x1_group.send(spot1, spot1, to_x[k])
        x1_group.send(spot2, spot2, to_x[k])
    wov_group.arrived()
    total = wov_recv[0]
    for k in range(1, 8):
        total = total + wov_recv[k]
    spot = gwo.at[pl.ds(pl.multiple_of(c * 256 + x * 64 + u * 8, 8), 8)]
    spot[...] = total[0:8]
    wou_group = Group(loss_recv.at[pl.ds(0, 7)])
    for k in FAR8:
        wou_group.send(spot, spot, to_u[k])
    for i in range(4):
        gbin_ref[:, 128 * i:128 * i + 128] = total[8 + i:9 + i]
    gbo_ref[...] = total[12:13, 0:VARS]
    drain()

    x1_group.arrived()
    spot1 = block(1, u * 16, 16, pl.ds(0, 512))
    spot2 = block(1, 128 + v * 16, 16, pl.ds(0, 512))
    u1_group, w1_group, last = Group(u1_recv, apart=7), Group(w1_recv, apart=7), Group(part)
    u1_copies, w1_copies = [], []
    for k in FAR8:
        u1_copies.append(u1_group.send(spot1, spot1, to_u[k]))
        w1_copies.append(w1_group.send(spot2, spot2, to_v[k]))
    last.send(spot1, spot1, sibling)
    last.send(spot2, spot2, sibling)
    u0_group.arrived()
    spot = block(0, 0, 256, x_cols)
    x0_group = Group(x0_recv, apart=3)
    x0_copies = [x0_group.send(spot, spot, to_x[k]) for k in FAR4]
    last.send(spot, spot, sibling)
    wou_group.arrived()
    rows = pl.ds(pl.multiple_of(c * 256 + x * 64, 64), 64)
    spot = gwo_low.at[rows]
    spot[...] = gwo[rows].astype(BF16)
    wox_group = Group(wox_recv, apart=3)
    wox_copies = [wox_group.send(spot, spot, to_x[k]) for k in FAR4]
    last_wo = Group(wo_recv)
    last_wo.send(spot, spot, sibling)

    drain()
    loss_group.arrived()
    for t in range(4):
        loss_ref[:, 128 * t:128 * t + 128] = jnp.where(
            low_row, loss_recv[2 * t, 0:1, :], loss_recv[2 * t + 1, 0:1, :])

    def forward(copy, spot):
        copy.wait_recv()
        last.send(spot, spot, sibling)

    def forward_rows(steps):
        for i in steps:
            k = FAR8[i]
            forward(u1_copies[i], block(1, u_at[8 - k] * 16, 16, pl.ds(0, 512)))
            forward(w1_copies[i], block(1, 128 + v_at[8 - k] * 16, 16, pl.ds(0, 512)))

    def forward_columns(steps):
        for i in steps:
            cols = pl.ds(pl.multiple_of(x_at[4 - FAR4[i]] * 128, 128), 128)
            forward(x0_copies[i], block(0, 0, 256, cols))

    forward_rows((6, 5, 4, 3))
    forward_columns((2, 1))
    forward_rows((2, 1, 0))
    forward_columns((0,))
    for k, copy in reversed(list(zip(FAR4, wox_copies))):
        copy.wait_recv()
        spot = gwo_low.at[pl.ds(pl.multiple_of(c * 256 + x_at[4 - k] * 64, 64), 64)]
        last_wo.send(spot, spot, sibling)
    last_wo.arrived()
    gwo_ref[...] = jnp.transpose(gwo_low[...].astype(F32))[0:VARS]
    last.arrived()
    drain()
    drain()
    assert len(groups) == N_SENDS and received[0] == N_RECEIVES


def deliver(*refs):
    results, places, sems = refs[0:5], refs[5:10], refs[10]
    copies = [
        pltpu.make_async_copy(src, dst, sems.at[i])
        for i, (src, dst) in enumerate(zip(results, places))
    ]
    for copy in copies:
        copy.start()
    for copy in copies:
        copy.wait()


def per_device(latent, w_in, b_in, output_weight, output_bias, observed_field, area):
    total_columns = latent.shape[2] * lax.axis_size("grid")
    vmem = pl.BlockSpec(memory_space=pltpu.VMEM)
    hbm = pl.BlockSpec(memory_space=pltpu.HBM)

    def scratch(dtype, *shape):
        return pltpu.VMEM(shape, dtype)

    results = (
        jax.ShapeDtypeStruct((1, COLS), F32),
        jax.ShapeDtypeStruct((DIN, HID), BF16),
        jax.ShapeDtypeStruct((1, HID), F32),
        jax.ShapeDtypeStruct((VARS, HID), F32),
        jax.ShapeDtypeStruct((1, VARS), F32),
    )
    operands = (
        latent, w_in, b_in.reshape(1, HID), output_weight.T, output_bias.reshape(1, VARS),
        observed_field, area.reshape(1, COLS),
    )
    made = pl.pallas_call(
        lambda *refs: kernel(total_columns, *refs),
        out_shape=results,
        in_specs=[hbm] * 7,
        out_specs=(vmem,) * 5,
        scratch_shapes=[
            scratch(F32, 1, HID), scratch(BF16, VARS, HID), scratch(F32, 1, VARS),
            scratch(F32, VARS, COLS), scratch(F32, 1, COLS), scratch(F32, HID, 128),
            scratch(BF16, HID, 128),
            scratch(BF16, DIN, COLS), scratch(BF16, DIN, HID),
            scratch(F32, HID, 128), scratch(F32, HID, COLS), scratch(F32, HID, COLS),
            scratch(BF16, HID, COLS), scratch(BF16, HID, 128), scratch(BF16, 128, HID),
            scratch(F32, 1, 128), scratch(F32, 2 * FOLD, 128),
            scratch(BF16, 2, 2, 2, FOLD, 128), scratch(BF16, 8, FOLD, 128),
            scratch(BF16, 8, FOLD, 128), scratch(BF16, 8, FOLD, 128),
            scratch(F32, 8, 8, 128), scratch(BF16, 128, COLS), scratch(BF16, HID, COLS),
            scratch(BF16, 2, 256, HID), scratch(BF16, 2, 256, HID),
            scratch(F32, 2, 256, HID), scratch(BF16, 2, 256, HID),
            scratch(BF16, 3, 256, 128), scratch(BF16, 256, 128),
            scratch(BF16, 7, 32, 128),
            scratch(BF16, 7, 16, HID), scratch(BF16, 7, 16, HID), scratch(BF16, 32, HID),
            scratch(BF16, 3, 32, 128), scratch(BF16, 8, 48, 128), scratch(BF16, 8, 16, 128),
            scratch(F32, HID, 128), scratch(BF16, 256, 128), scratch(BF16, 256, 128),
            scratch(BF16, 256, 128), scratch(BF16, 3, 64, 128),
            scratch(F32, 8, 16, 128), scratch(F32, 8, 16, 128), scratch(F32, 8, 16, 128),
            scratch(F32, 2, 8, 128), scratch(F32, 4, 8, 128),
            pltpu.SemaphoreType.DMA((9,)),
            pltpu.SemaphoreType.DMA((N_SENDS,)), pltpu.SemaphoreType.DMA((N_RECEIVES,)),
        ],
        compiler_params=pltpu.CompilerParams(
            collective_id=0, has_side_effects=True, vmem_limit_bytes=40 * 2**20),
        cost_estimate=pl.CostEstimate(
            flops=4 * DIN * HID * COLS, bytes_accessed=4 * 2**20, transcendentals=2 * HID * COLS),
        name="energy_score_step",
    )(*[pltpu.with_memory_space_constraint(operand, pltpu.HBM) for operand in operands])
    loss, grad_w_in, grad_b_in, grad_w_out, grad_b_out = pl.pallas_call(
        deliver,
        out_shape=results,
        in_specs=[vmem] * 5,
        out_specs=(hbm,) * 5,
        scratch_shapes=[pltpu.SemaphoreType.DMA((5,))],
        compiler_params=pltpu.CompilerParams(vmem_limit_bytes=4 * 2**20),
        name="deliver",
    )(*made)
    return (
        loss.reshape(COLS), grad_w_in, grad_b_in.reshape(HID), grad_w_out.T,
        grad_b_out.reshape(VARS),
    )


def solution(mesh):
    placed = (P("member", None, "grid"), P(), P(), P(), P(), P(None, "grid"), P("grid"))
    return jax.shard_map(
        per_device,
        mesh=mesh,
        in_specs=placed,
        out_specs=(P("grid"), P(), P(), P(), P()),
        check_vma=False,
    )
```

```python
import math

import jax
import jax.numpy as jnp
from jax import lax
from jax.experimental import pallas as pl
from jax.experimental.pallas import tpu as pltpu
from jax.sharding import PartitionSpec as P

MESH = pl.DeviceIdType.MESH
F32 = jnp.float32
BF16 = jnp.bfloat16
EPSILON = 1e-05
GELU_A = math.sqrt(2.0 / math.pi)
GELU_B = 0.044715

DIN, HID, VARS = 1024, 512, 83
COLS = 512
FOLD = 48
NX, NU = 4, 8
FAR4 = (2, 1, 3)
FAR8 = (4, 3, 5, 2, 6, 1, 7)
N_SENDS, N_RECEIVES = 27, 49


def dot(a, b):
    return jnp.dot(a, b, preferred_element_type=F32)


def dot_nt(a, b):
    return lax.dot_general(a, b, (((1,), (1,)), ((), ())), preferred_element_type=F32)


def dot_tn(a, b):
    return lax.dot_general(a, b, (((0,), (0,)), ((), ())), preferred_element_type=F32)


def kernel(
    total_columns,
    lat_hbm, win_hbm, bin_hbm, wo_ref, bo_hbm, obs_hbm, area_hbm,
    loss_ref, gw_ref, gbin_ref, gwo_ref, gbo_ref,
    bin_ref, bo_ref, obs_ref, area_ref, gwo, gwo_low,
    lat, win, bias, pre, dgelu, hidden, wop, wop_t, row, obs_pad,
    f_send, f_recv, g_send, g_recv, loss_recv, gl, gp,
    sib_send, sib_recv, own, part,
    x0_recv, s0, u0_recv, u1_recv, w1_recv, s1, x1_recv, v_recv, w_recv,
    wo_part, wo_send, wo_recv, wo_rs, wox_recv, wou_src, wou_recv, wov_recv,
    sm_c, sm_x,
    local_sems, send_sems, recv_sems,
):
    member, grid = lax.axis_index("member"), lax.axis_index("grid")
    c, zlo = member & 1, member >> 1
    a, b = zlo >> 1, zlo & 1
    zhi, y, x = grid & 1, (grid >> 1) & 7, grid >> 4
    z = zhi * 4 + zlo
    on_y = 1 - c
    u = y * on_y + z * c
    v = z * on_y + y * c

    def device(x, y, z):
        return ((z & 3) * 2 + c, (x * 8 + y) * 2 + (z >> 2))

    x_at = [(x + k) & 3 for k in range(4)]
    u_at = [(u + k) & 7 for k in range(8)]
    v_at = [(v + k) & 7 for k in range(8)]
    to_x = [(member, (x_at[k] * 8 + y) * 2 + zhi) for k in range(4)]
    to_u = [device(x, u_at[k] * on_y + y * c, z * on_y + u_at[k] * c) for k in range(8)]
    to_v = [device(x, y * on_y + v_at[k] * c, v_at[k] * on_y + z * c) for k in range(8)]

    sibling = (zlo * 2 + 1 - c, grid)

    def flip(bit, by):
        return 1 - bit if by else bit

    def member_of(rel):
        ra, rb, rc = rel
        return (2 * flip(a, ra) + flip(b, rb)) * 2 + flip(c, rc)

    rels = [(ra, rb, rc) for ra in (1, 0) for rb in (1, 0) for rc in (1, 0)][:-1]

    there = {rel: member_of(rel) for rel in rels}

    groups, fences, received = [], [0, 0], [0]

    class Group:
        def __init__(self, size, apart=0):
            self.size, self.index = size, len(groups)
            self.first, self.apart, self.count = received[0], apart, 0
            received[0] += max(apart, 1)
            groups.append(self)

        def copy(self, src, dst, to, number=0):
            return pltpu.make_async_remote_copy(
                src_ref=src, dst_ref=dst, send_sem=send_sems.at[self.index],
                recv_sem=recv_sems.at[self.first + number], device_id=to, device_id_type=MESH,
            )

        def send(self, src, dst, to):
            copy = self.copy(src, dst, to, self.count if self.apart else 0)
            self.count += 1
            copy.start()
            return copy

        def arrived(self):
            self.copy(self.size, self.size, sibling).wait_recv()

        def left(self):
            self.copy(self.size, self.size, sibling).wait_send()

    def drain():
        for group in groups[fences[-2]:fences[-1]]:
            group.left()
        fences.append(len(groups))

    halves = [1 - a, a]
    load_w = [
        pltpu.make_async_copy(
            win_hbm.at[pl.ds(512 * i, 512)], win.at[pl.ds(512 * i, 512)], local_sems.at[i])
        for i in range(2)
    ]
    load_l = [
        pltpu.make_async_copy(
            lat_hbm.at[0, :, pl.ds(pl.multiple_of(h * 256, 256), 256)],
            lat.at[:, pl.ds(pl.multiple_of(h * 256, 256), 256)], local_sems.at[2 + i])
        for i, h in enumerate(halves)
    ]
    load_small = [
        pltpu.make_async_copy(src, dst, local_sems.at[4 + i])
        for i, (src, dst) in enumerate((
            (bin_hbm, bin_ref), (bo_hbm, bo_ref), (obs_hbm, obs_ref), (area_hbm, area_ref)))
    ]
    for copy in load_w + load_l[:1] + load_small[:2]:
        copy.start()

    barrier = pltpu.get_barrier_semaphore()
    far, near = rels[:4], rels[4:]
    partners = (
        [way[k] for k in (4, 3, 5) for way in (to_u, to_v)]
        + [(there[rel], grid) for rel in far]
        + [way[k] for k in (2, 6) for way in (to_u, to_v)] + [to_x[2]]
        + [(there[rel], grid) for rel in near]
        + [way[k] for k in (1, 7) for way in (to_u, to_v)] + [to_x[1], to_x[3]]
    )
    for partner in partners:
        pl.semaphore_signal(barrier, inc=1, device_id=partner, device_id_type=MESH)
    for copy in load_l[1:] + load_small[2:]:
        copy.start()

    wop_t[...] = jnp.zeros_like(wop_t)
    row[...] = jnp.zeros_like(row)
    for copy in load_small[:2]:
        copy.wait()
    for i in range(4):
        bias[pl.ds(128 * i, 128), :] = jnp.transpose(
            jnp.broadcast_to(bin_ref[:, pl.ds(128 * i, 128)], (128, 128)))
    wop_t[0:VARS, :] = wo_ref[...]
    row[:, 0:VARS] = bo_ref[...]
    bias_out = jnp.transpose(jnp.broadcast_to(row[...], (128, 128)))[0:2 * FOLD]
    lane = lax.broadcasted_iota(jnp.int32, (FOLD, 128), 1)
    low_lane = lane < 64
    low_row = lax.broadcasted_iota(jnp.int32, (1, 128), 1) < 64

    def swap(value):
        return pltpu.roll(value, 64, 1)

    for copy in load_w:
        copy.wait()

    f_group = Group(f_recv.at[pl.ds(0, 7)])
    for i, h in enumerate(halves):
        cols = pl.ds(pl.multiple_of(h * 256, 256), 256)
        load_l[i].wait()
        pre[:, cols] = dot_tn(win[...], lat[:, cols])

        def activate(r, _):
            rows = pl.ds(pl.multiple_of(r * 128, 128), 128)
            shift = bias[rows, :]
            value = pre[rows, cols] + jnp.concatenate([shift, shift], axis=1)
            pre[rows, cols] = value
            inner = GELU_A * (value + GELU_B * (value * value * value))
            hidden[rows, cols] = (0.5 * value * (1.0 + jnp.tanh(inner))).astype(BF16)
            return 0

        lax.fori_loop(0, HID // 128, activate, 0)
        field = dot(wop_t[0:2 * FOLD, :], hidden[:, cols])
        for t in range(2):
            chunk = (field[:, 128 * t:128 * t + 128] + bias_out).astype(BF16).astype(F32)
            lo, hi = chunk[0:FOLD], chunk[FOLD:2 * FOLD]
            f_send[i, t, 0] = jnp.where(low_lane, lo, swap(hi)).astype(BF16)
            f_send[i, t, 1] = jnp.where(low_lane, swap(lo), hi).astype(BF16)
        if i == 0:
            pl.semaphore_wait(barrier, len(partners))
        for rel in rels:
            if rel[0] == 1 - i:
                src = f_send.at[i, flip(b, rel[1]), flip(c, rel[2])]
                f_group.send(src, f_recv.at[member], (there[rel], grid))
    f_recv[pl.ds(member, 1)] = f_send[1, pl.ds(b, 1), pl.ds(c, 1)].reshape(1, FOLD, 128)

    def derive(r, _):
        rows = pl.ds(pl.multiple_of(r * 128, 128), 128)
        value = pre[rows, :]
        square = value * value
        t = jnp.tanh(GELU_A * (value + GELU_B * (value * square)))
        dgelu[rows, :] = 0.5 * (1.0 + t) + (0.5 * GELU_A) * value * (1.0 - t * t) * (
            1.0 + (3.0 * GELU_B) * square)
        return 0

    lax.fori_loop(0, HID // 128, derive, 0)
    wop[...] = jnp.transpose(wop_t[...])
    for copy in load_small[2:]:
        copy.wait()
    obs_pad[...] = jnp.zeros_like(obs_pad)
    own_cols = pl.ds(pl.multiple_of(zlo * 128, 128), 128)
    obs_pad[0:VARS, :] = obs_ref[:, own_cols]
    lo, hi = obs_pad[0:FOLD], obs_pad[FOLD:2 * FOLD]
    first = c == 0
    observed = jnp.where(low_lane, jnp.where(first, lo, swap(lo)), jnp.where(first, swap(hi), hi))
    area = area_ref[:, own_cols]
    area = jnp.where(low_row, jnp.where(first, area, swap(area)), jnp.where(first, swap(area), area))
    factor = area * (VARS * math.sqrt(8 / total_columns))
    gl[2 * FOLD:128, :] = jnp.zeros((128 - 2 * FOLD, COLS), BF16)

    def norm(difference):
        total = jnp.sum(difference * difference, axis=0, keepdims=True)
        square = (total + swap(total)) / VARS + EPSILON
        inverse = lax.rsqrt(square)
        return square * inverse, inverse

    f_group.arrived()
    fields = [f_recv[i].astype(F32) for i in range(8)]
    grads = []
    true_total = jnp.zeros((1, 128), F32)
    for m in range(8):
        difference = fields[m] - observed
        distance, inverse = norm(difference)
        true_total = true_total + distance
        grads.append(difference * (factor * inverse * (1.0 / (VARS * 8))))
    pair_total = jnp.full((1, 128), 8.0 * math.sqrt(EPSILON), F32)
    for m in range(8):
        for n in range(m + 1, 8):
            difference = fields[m] - fields[n]
            distance, inverse = norm(difference)
            pair_total = pair_total + 2.0 * distance
            pull = difference * (factor * inverse * (1.0 / (VARS * 64)))
            grads[m] = grads[m] - pull
            grads[n] = grads[n] + pull
    for m in range(8):
        g_send[m] = grads[m].astype(BF16)
    g_group = Group(g_recv.at[pl.ds(0, 7)], apart=7)
    g_copies = {
        rel: g_group.send(g_send.at[there[rel]], g_recv.at[member], (there[rel], grid))
        for rel in rels}
    g_recv[pl.ds(member, 1)] = g_send[pl.ds(member, 1)]
    loss = true_total * (1.0 / 8) - pair_total * (1.0 / 128)
    loss_recv[pl.ds(member, 1)] = jnp.broadcast_to(loss, (1, 8, 128))
    loss_group = Group(loss_recv.at[pl.ds(0, 7)])
    for rel in rels:
        loss_group.send(loss_recv.at[member], loss_recv.at[member], (there[rel], grid))

    drain()
    for ra, rb in ((0, 0), (0, 1), (1, 0), (1, 1)):
        for rel in rels:
            if rel[:2] == (ra, rb):
                g_copies[rel].wait_recv()
        t = 2 * flip(a, ra) + flip(b, rb)
        left, right = g_recv[2 * t].astype(F32), g_recv[2 * t + 1].astype(F32)
        cols = pl.ds(pl.multiple_of(128 * t, 128), 128)
        gl[0:FOLD, cols] = jnp.where(low_lane, left, swap(right)).astype(BF16)
        gl[FOLD:2 * FOLD, cols] = jnp.where(low_lane, swap(left), right).astype(BF16)
        gp[:, cols] = (dot(wop[...], gl[:, cols]) * dgelu[:, cols]).astype(BF16)

    sib_groups = [Group(sib_recv.at[q]) for q in range(2)]
    for q in range(2):
        rows = pl.ds(pl.multiple_of((1 - c) * 512 + q * 256, 256), 256)
        sib_send[q] = dot_nt(lat[rows, :], gp[...]).astype(BF16)
        sib_groups[q].send(sib_send.at[q], sib_recv.at[q], sibling)
    wo_part[...] = dot_nt(hidden[...], gl[...])
    wo_send[...] = wo_part[pl.ds(pl.multiple_of((1 - c) * 256, 256), 256), :].astype(BF16)
    wo_group = Group(wo_recv)
    wo_group.send(wo_send, wo_recv, sibling)
    ones = jnp.ones((16, COLS), BF16)
    sum_in = dot_nt(ones, gp[...])[0:1]
    sum_out = dot_nt(ones, gl[...])[0:1]
    rows8 = lax.broadcasted_iota(jnp.int32, (8, 128), 0)
    tile = jnp.where(rows8 == 4, sum_out, 0.0)
    for i in range(4):
        tile = jnp.where(rows8 == i, sum_in[:, 128 * i:128 * i + 128], tile)
    sm_c[pl.ds(c, 1)] = tile.reshape(1, 8, 128)
    smc_group = Group(sm_c.at[0])
    smc_group.send(sm_c.at[c], sm_c.at[c], sibling)

    x_cols = pl.ds(pl.multiple_of(x * 128, 128), 128)
    u_rows = pl.ds(pl.multiple_of(u * 32, 32), 32)

    def own_half(q):
        rows = pl.ds(pl.multiple_of(c * 512 + q * 256, 256), 256)
        own[q] = dot_nt(lat[rows, :], gp[...])

    def merge(q):
        sib_groups[q].arrived()
        part[q] = (own[q] + sib_recv[q].astype(F32)).astype(BF16)

    own_half(0)
    own_half(1)
    merge(0)
    x0_group = Group(x0_recv)
    for k in FAR4:
        cols = pl.ds(pl.multiple_of(x_at[k] * 128, 128), 128)
        x0_group.send(part.at[0, :, cols], x0_recv.at[k - 1], to_x[k])
    merge(1)
    u1_group, w1_group = Group(u1_recv), Group(w1_recv)
    for k in FAR8:
        rows = pl.ds(pl.multiple_of(u_at[k] * 16, 16), 16)
        u1_group.send(part.at[1, rows], u1_recv.at[k - 1], to_u[k])
        rows = pl.ds(pl.multiple_of(128 + v_at[k] * 16, 16), 16)
        w1_group.send(part.at[1, rows], w1_recv.at[k - 1], to_v[k])
    wo_group.arrived()
    wo_rs[...] = (
        wo_part[pl.ds(pl.multiple_of(c * 256, 256), 256), :] + wo_recv[...].astype(F32)).astype(BF16)
    wox_group = Group(wox_recv)
    for k in FAR4:
        rows = pl.ds(pl.multiple_of(x_at[k] * 64, 64), 64)
        wox_group.send(wo_rs.at[rows], wox_recv.at[k - 1], to_x[k])
    smc_group.arrived()
    sm_x[pl.ds(x, 1)] = (sm_c[0] + sm_c[1]).reshape(1, 8, 128)
    smx_group = Group(sm_x.at[pl.ds(0, 3)])
    for k in FAR4:
        smx_group.send(sm_x.at[x], sm_x.at[x], to_x[k])

    drain()
    x0_group.arrived()
    total = part[0, :, x_cols].astype(F32)
    for k in range(3):
        total = total + x0_recv[k].astype(F32)
    s0[...] = total.astype(BF16)
    u0_group = Group(u0_recv)
    for k in FAR8:
        rows = pl.ds(pl.multiple_of(u_at[k] * 32, 32), 32)
        u0_group.send(s0.at[rows], u0_recv.at[k - 1], to_u[k])
    wox_group.arrived()
    total = wo_rs[pl.ds(pl.multiple_of(x * 64, 64), 64), :].astype(F32)
    for k in range(3):
        total = total + wox_recv[k].astype(F32)
    smx_group.arrived()
    small = sm_x[0] + sm_x[1] + sm_x[2] + sm_x[3]
    for j in range(8):
        wou_src[j, 0:8] = total[8 * j:8 * j + 8]
        wou_src[j, 8:16] = small
    wou_recv[pl.ds(u, 1)] = wou_src[pl.ds(u, 1)]
    wou_group = Group(wou_recv.at[pl.ds(0, 7)])
    for k in FAR8:
        wou_group.send(wou_src.at[u_at[k]], wou_recv.at[u], to_u[k])
    for group, received_1, at, place in ((u1_group, u1_recv, u * 16, 0), (w1_group, w1_recv, 128 + v * 16, 16)):
        group.arrived()
        total = part[1, pl.ds(pl.multiple_of(at, 16), 16), :].astype(F32)
        for k in range(7):
            total = total + received_1[k].astype(F32)
        s1[place:place + 16, :] = total.astype(BF16)
    x1_group = Group(x1_recv)
    for k in FAR4:
        cols = pl.ds(pl.multiple_of(x_at[k] * 128, 128), 128)
        x1_group.send(s1.at[:, cols], x1_recv.at[k - 1], to_x[k])

    x1_group.arrived()
    total = s1[:, x_cols].astype(F32)
    for k in range(3):
        total = total + x1_recv[k].astype(F32)
    total = total.astype(BF16)
    v_recv[v, 32:48] = total[0:16]
    w_recv[u] = total[16:32]
    u0_group.arrived()
    total = s0[u_rows, :].astype(F32)
    for k in range(7):
        total = total + u0_recv[k].astype(F32)
    v_recv[v, 0:32] = total.astype(BF16)
    v_group, w_group = Group(v_recv.at[pl.ds(0, 7)]), Group(w_recv.at[pl.ds(0, 7)])
    for k in FAR8:
        v_group.send(v_recv.at[v], v_recv.at[v], to_v[k])
        w_group.send(w_recv.at[u], w_recv.at[u], to_u[k])
    wou_group.arrived()
    total = wou_recv[0]
    for k in range(1, 8):
        total = total + wou_recv[k]
    wov_recv[pl.ds(v, 1)] = total.reshape(1, 16, 128)
    wov_group = Group(wov_recv.at[pl.ds(0, 7)])
    for k in FAR8:
        wov_group.send(wov_recv.at[v], wov_recv.at[v], to_v[k])
    drain()

    base = c * 512

    def block(q, rows_at, rows, cols):
        return gw_ref.at[pl.ds(pl.multiple_of(base + q * 256 + rows_at, 16), rows), cols]

    v_group.arrived()
    total = v_recv[0].astype(F32)
    for k in range(1, 8):
        total = total + v_recv[k].astype(F32)
    total = total.astype(BF16)
    spot0 = block(0, u * 32, 32, x_cols)
    spot0[...] = total[0:32]
    u0_group = Group(u0_recv)
    for k in FAR8:
        u0_group.send(spot0, spot0, to_u[k])
    spot1 = block(1, u * 16, 16, x_cols)
    spot1[...] = total[32:48]
    w_group.arrived()
    total = w_recv[0].astype(F32)
    for k in range(1, 8):
        total = total + w_recv[k].astype(F32)
    spot2 = block(1, 128 + v * 16, 16, x_cols)
    spot2[...] = total.astype(BF16)
    x1_group = Group(x1_recv)
    for k in FAR4:
        x1_group.send(spot1, spot1, to_x[k])
        x1_group.send(spot2, spot2, to_x[k])
    wov_group.arrived()
    total = wov_recv[0]
    for k in range(1, 8):
        total = total + wov_recv[k]
    spot = gwo.at[pl.ds(pl.multiple_of(c * 256 + x * 64 + u * 8, 8), 8)]
    spot[...] = total[0:8]
    wou_group = Group(loss_recv.at[pl.ds(0, 7)])
    for k in FAR8:
        wou_group.send(spot, spot, to_u[k])
    for i in range(4):
        gbin_ref[:, 128 * i:128 * i + 128] = total[8 + i:9 + i]
    gbo_ref[...] = total[12:13, 0:VARS]
    drain()

    x1_group.arrived()
    spot1 = block(1, u * 16, 16, pl.ds(0, 512))
    spot2 = block(1, 128 + v * 16, 16, pl.ds(0, 512))
    u1_group, w1_group, last = Group(u1_recv, apart=7), Group(w1_recv, apart=7), Group(part)
    u1_copies, w1_copies = [], []
    for k in FAR8:
        u1_copies.append(u1_group.send(spot1, spot1, to_u[k]))
        w1_copies.append(w1_group.send(spot2, spot2, to_v[k]))
    last.send(spot1, spot1, sibling)
    last.send(spot2, spot2, sibling)
    u0_group.arrived()
    spot = block(0, 0, 256, x_cols)
    x0_group = Group(x0_recv, apart=3)
    x0_copies = [x0_group.send(spot, spot, to_x[k]) for k in FAR4]
    last.send(spot, spot, sibling)
    wou_group.arrived()
    rows = pl.ds(pl.multiple_of(c * 256 + x * 64, 64), 64)
    spot = gwo_low.at[rows]
    spot[...] = gwo[rows].astype(BF16)
    wox_group = Group(wox_recv, apart=3)
    wox_copies = [wox_group.send(spot, spot, to_x[k]) for k in FAR4]
    last_wo = Group(wo_recv)
    last_wo.send(spot, spot, sibling)

    drain()
    loss_group.arrived()
    for t in range(4):
        loss_ref[:, 128 * t:128 * t + 128] = jnp.where(
            low_row, loss_recv[2 * t, 0:1, :], loss_recv[2 * t + 1, 0:1, :])

    def forward(copy, spot):
        copy.wait_recv()
        last.send(spot, spot, sibling)

    def forward_rows(steps):
        for i in steps:
            k = FAR8[i]
            forward(u1_copies[i], block(1, u_at[8 - k] * 16, 16, pl.ds(0, 512)))
            forward(w1_copies[i], block(1, 128 + v_at[8 - k] * 16, 16, pl.ds(0, 512)))

    def forward_columns(steps):
        for i in steps:
            cols = pl.ds(pl.multiple_of(x_at[4 - FAR4[i]] * 128, 128), 128)
            forward(x0_copies[i], block(0, 0, 256, cols))

    forward_rows((6, 5, 4, 3))
    forward_columns((2, 1))
    forward_rows((2, 1, 0))
    forward_columns((0,))
    for k, copy in reversed(list(zip(FAR4, wox_copies))):
        copy.wait_recv()
        spot = gwo_low.at[pl.ds(pl.multiple_of(c * 256 + x_at[4 - k] * 64, 64), 64)]
        last_wo.send(spot, spot, sibling)
    last_wo.arrived()
    gwo_ref[...] = jnp.transpose(gwo_low[...].astype(F32))[0:VARS]
    last.arrived()
    drain()
    drain()
    assert len(groups) == N_SENDS and received[0] == N_RECEIVES


def deliver(*refs):
    results, places, sems = refs[0:5], refs[5:10], refs[10]
    copies = [
        pltpu.make_async_copy(src, dst, sems.at[i])
        for i, (src, dst) in enumerate(zip(results, places))
    ]
    for copy in copies:
        copy.start()
    for copy in copies:
        copy.wait()


def per_device(latent, w_in, b_in, output_weight, output_bias, observed_field, area):
    total_columns = latent.shape[2] * lax.axis_size("grid")
    vmem = pl.BlockSpec(memory_space=pltpu.VMEM)
    hbm = pl.BlockSpec(memory_space=pltpu.HBM)

    def scratch(dtype, *shape):
        return pltpu.VMEM(shape, dtype)

    results = (
        jax.ShapeDtypeStruct((1, COLS), F32),
        jax.ShapeDtypeStruct((DIN, HID), BF16),
        jax.ShapeDtypeStruct((1, HID), F32),
        jax.ShapeDtypeStruct((VARS, HID), F32),
        jax.ShapeDtypeStruct((1, VARS), F32),
    )
    operands = (
        latent, w_in, b_in.reshape(1, HID), output_weight.T, output_bias.reshape(1, VARS),
        observed_field, area.reshape(1, COLS),
    )
    made = pl.pallas_call(
        lambda *refs: kernel(total_columns, *refs),
        out_shape=results,
        in_specs=[hbm] * 3 + [vmem] + [hbm] * 3,
        out_specs=(vmem,) * 5,
        scratch_shapes=[
            scratch(F32, 1, HID), scratch(F32, 1, VARS),
            scratch(F32, VARS, COLS), scratch(F32, 1, COLS), scratch(F32, HID, 128),
            scratch(BF16, HID, 128),
            scratch(BF16, DIN, COLS), scratch(BF16, DIN, HID),
            scratch(F32, HID, 128), scratch(F32, HID, COLS), scratch(F32, HID, COLS),
            scratch(BF16, HID, COLS), scratch(BF16, HID, 128), scratch(BF16, 128, HID),
            scratch(F32, 1, 128), scratch(F32, 2 * FOLD, 128),
            scratch(BF16, 2, 2, 2, FOLD, 128), scratch(BF16, 8, FOLD, 128),
            scratch(BF16, 8, FOLD, 128), scratch(BF16, 8, FOLD, 128),
            scratch(F32, 8, 8, 128), scratch(BF16, 128, COLS), scratch(BF16, HID, COLS),
            scratch(BF16, 2, 256, HID), scratch(BF16, 2, 256, HID),
            scratch(F32, 2, 256, HID), scratch(BF16, 2, 256, HID),
            scratch(BF16, 3, 256, 128), scratch(BF16, 256, 128),
            scratch(BF16, 7, 32, 128),
            scratch(BF16, 7, 16, HID), scratch(BF16, 7, 16, HID), scratch(BF16, 32, HID),
            scratch(BF16, 3, 32, 128), scratch(BF16, 8, 48, 128), scratch(BF16, 8, 16, 128),
            scratch(F32, HID, 128), scratch(BF16, 256, 128), scratch(BF16, 256, 128),
            scratch(BF16, 256, 128), scratch(BF16, 3, 64, 128),
            scratch(F32, 8, 16, 128), scratch(F32, 8, 16, 128), scratch(F32, 8, 16, 128),
            scratch(F32, 2, 8, 128), scratch(F32, 4, 8, 128),
            pltpu.SemaphoreType.DMA((8,)),
            pltpu.SemaphoreType.DMA((N_SENDS,)), pltpu.SemaphoreType.DMA((N_RECEIVES,)),
        ],
        compiler_params=pltpu.CompilerParams(
            collective_id=0, has_side_effects=True, vmem_limit_bytes=40 * 2**20),
        cost_estimate=pl.CostEstimate(
            flops=4 * DIN * HID * COLS, bytes_accessed=4 * 2**20, transcendentals=2 * HID * COLS),
        name="energy_score_step",
    )(*[
        operand if i == 3 else pltpu.with_memory_space_constraint(operand, pltpu.HBM)
        for i, operand in enumerate(operands)])
    loss, grad_w_in, grad_b_in, grad_w_out, grad_b_out = pl.pallas_call(
        deliver,
        out_shape=results,
        in_specs=[vmem] * 5,
        out_specs=(hbm,) * 5,
        scratch_shapes=[pltpu.SemaphoreType.DMA((5,))],
        compiler_params=pltpu.CompilerParams(vmem_limit_bytes=4 * 2**20),
        name="deliver",
    )(*made)
    return (
        loss.reshape(COLS), grad_w_in, grad_b_in.reshape(HID), grad_w_out.T,
        grad_b_out.reshape(VARS),
    )


def solution(mesh):
    placed = (P("member", None, "grid"), P(), P(), P(), P(), P(None, "grid"), P("grid"))
    return jax.shard_map(
        per_device,
        mesh=mesh,
        in_specs=placed,
        out_specs=(P("grid"), P(), P(), P(), P()),
        check_vma=False,
    )
```

```python
import math

import jax
import jax.numpy as jnp
from jax import lax
from jax.experimental import pallas as pl
from jax.experimental.pallas import tpu as pltpu
from jax.sharding import PartitionSpec as P

MESH = pl.DeviceIdType.MESH
F32 = jnp.float32
BF16 = jnp.bfloat16
EPSILON = 1e-05
GELU_A = math.sqrt(2.0 / math.pi)
GELU_B = 0.044715

DIN, HID, VARS = 1024, 512, 83
COLS = 512
FOLD = 48
NX, NU = 4, 8
FAR4 = (2, 1, 3)
FAR8 = (4, 3, 5, 2, 6, 1, 7)
N_SENDS, N_RECEIVES = 27, 49


def dot(a, b):
    return jnp.dot(a, b, preferred_element_type=F32)


def dot_nt(a, b):
    return lax.dot_general(a, b, (((1,), (1,)), ((), ())), preferred_element_type=F32)


def dot_tn(a, b):
    return lax.dot_general(a, b, (((0,), (0,)), ((), ())), preferred_element_type=F32)


def kernel(
    total_columns,
    lat_hbm, win_hbm, bin_hbm, wop_t, bo_hbm, obs_hbm, area_hbm,
    loss_ref, gw_ref, gbin_ref, gwo_ref, gbo_ref,
    bin_ref, bo_ref, obs_ref, area_ref, gwo, gwo_low,
    lat, win, bias, pre, dgelu, hidden, wop, row, obs_pad,
    f_send, f_recv, g_send, g_recv, loss_recv, gl, gp,
    sib_send, sib_recv, own, part,
    x0_recv, s0, u0_recv, u1_recv, w1_recv, s1, x1_recv, v_recv, w_recv,
    wo_part, wo_send, wo_recv, wo_rs, wox_recv, wou_src, wou_recv, wov_recv,
    sm_c, sm_x,
    local_sems, send_sems, recv_sems,
):
    member, grid = lax.axis_index("member"), lax.axis_index("grid")
    c, zlo = member & 1, member >> 1
    a, b = zlo >> 1, zlo & 1
    zhi, y, x = grid & 1, (grid >> 1) & 7, grid >> 4
    z = zhi * 4 + zlo
    on_y = 1 - c
    u = y * on_y + z * c
    v = z * on_y + y * c

    def device(x, y, z):
        return ((z & 3) * 2 + c, (x * 8 + y) * 2 + (z >> 2))

    x_at = [(x + k) & 3 for k in range(4)]
    u_at = [(u + k) & 7 for k in range(8)]
    v_at = [(v + k) & 7 for k in range(8)]
    to_x = [(member, (x_at[k] * 8 + y) * 2 + zhi) for k in range(4)]
    to_u = [device(x, u_at[k] * on_y + y * c, z * on_y + u_at[k] * c) for k in range(8)]
    to_v = [device(x, y * on_y + v_at[k] * c, v_at[k] * on_y + z * c) for k in range(8)]

    sibling = (zlo * 2 + 1 - c, grid)

    def flip(bit, by):
        return 1 - bit if by else bit

    def member_of(rel):
        ra, rb, rc = rel
        return (2 * flip(a, ra) + flip(b, rb)) * 2 + flip(c, rc)

    rels = [(ra, rb, rc) for ra in (1, 0) for rb in (1, 0) for rc in (1, 0)][:-1]

    there = {rel: member_of(rel) for rel in rels}

    groups, fences, received = [], [0, 0], [0]

    class Group:
        def __init__(self, size, apart=0):
            self.size, self.index = size, len(groups)
            self.first, self.apart, self.count = received[0], apart, 0
            received[0] += max(apart, 1)
            groups.append(self)

        def copy(self, src, dst, to, number=0):
            return pltpu.make_async_remote_copy(
                src_ref=src, dst_ref=dst, send_sem=send_sems.at[self.index],
                recv_sem=recv_sems.at[self.first + number], device_id=to, device_id_type=MESH,
            )

        def send(self, src, dst, to):
            copy = self.copy(src, dst, to, self.count if self.apart else 0)
            self.count += 1
            copy.start()
            return copy

        def arrived(self):
            self.copy(self.size, self.size, sibling).wait_recv()

        def left(self):
            self.copy(self.size, self.size, sibling).wait_send()

    def drain():
        for group in groups[fences[-2]:fences[-1]]:
            group.left()
        fences.append(len(groups))

    halves = [1 - a, a]
    load_w = [
        pltpu.make_async_copy(
            win_hbm.at[pl.ds(512 * i, 512)], win.at[pl.ds(512 * i, 512)], local_sems.at[i])
        for i in range(2)
    ]
    load_l = [
        pltpu.make_async_copy(
            lat_hbm.at[0, :, pl.ds(pl.multiple_of(h * 256, 256), 256)],
            lat.at[:, pl.ds(pl.multiple_of(h * 256, 256), 256)], local_sems.at[2 + i])
        for i, h in enumerate(halves)
    ]
    load_small = [
        pltpu.make_async_copy(src, dst, local_sems.at[4 + i])
        for i, (src, dst) in enumerate((
            (bin_hbm, bin_ref), (bo_hbm, bo_ref), (obs_hbm, obs_ref), (area_hbm, area_ref)))
    ]
    for copy in load_w + load_l[:1] + load_small[:2]:
        copy.start()

    barrier = pltpu.get_barrier_semaphore()
    far, near = rels[:4], rels[4:]
    partners = (
        [way[k] for k in (4, 3, 5) for way in (to_u, to_v)]
        + [(there[rel], grid) for rel in far]
        + [way[k] for k in (2, 6) for way in (to_u, to_v)] + [to_x[2]]
        + [(there[rel], grid) for rel in near]
        + [way[k] for k in (1, 7) for way in (to_u, to_v)] + [to_x[1], to_x[3]]
    )
    for partner in partners:
        pl.semaphore_signal(barrier, inc=1, device_id=partner, device_id_type=MESH)
    for copy in load_l[1:] + load_small[2:]:
        copy.start()

    row[...] = jnp.zeros_like(row)
    for copy in load_small[:2]:
        copy.wait()
    for i in range(4):
        bias[pl.ds(128 * i, 128), :] = jnp.transpose(
            jnp.broadcast_to(bin_ref[:, pl.ds(128 * i, 128)], (128, 128)))
    row[:, 0:VARS] = bo_ref[...]
    bias_out = jnp.transpose(jnp.broadcast_to(row[...], (128, 128)))[0:2 * FOLD]
    lane = lax.broadcasted_iota(jnp.int32, (FOLD, 128), 1)
    low_lane = lane < 64
    low_row = lax.broadcasted_iota(jnp.int32, (1, 128), 1) < 64

    def swap(value):
        return pltpu.roll(value, 64, 1)

    for copy in load_w:
        copy.wait()

    f_group = Group(f_recv.at[pl.ds(0, 7)])
    for i, h in enumerate(halves):
        cols = pl.ds(pl.multiple_of(h * 256, 256), 256)
        load_l[i].wait()
        pre[:, cols] = dot_tn(win[...], lat[:, cols])

        def activate(r, _):
            rows = pl.ds(pl.multiple_of(r * 128, 128), 128)
            shift = bias[rows, :]
            value = pre[rows, cols] + jnp.concatenate([shift, shift], axis=1)
            pre[rows, cols] = value
            inner = GELU_A * (value + GELU_B * (value * value * value))
            hidden[rows, cols] = (0.5 * value * (1.0 + jnp.tanh(inner))).astype(BF16)
            return 0

        lax.fori_loop(0, HID // 128, activate, 0)
        field = dot(wop_t[0:2 * FOLD, :], hidden[:, cols])
        for t in range(2):
            chunk = (field[:, 128 * t:128 * t + 128] + bias_out).astype(BF16).astype(F32)
            lo, hi = chunk[0:FOLD], chunk[FOLD:2 * FOLD]
            f_send[i, t, 0] = jnp.where(low_lane, lo, swap(hi)).astype(BF16)
            f_send[i, t, 1] = jnp.where(low_lane, swap(lo), hi).astype(BF16)
        if i == 0:
            pl.semaphore_wait(barrier, len(partners))
        for rel in rels:
            if rel[0] == 1 - i:
                src = f_send.at[i, flip(b, rel[1]), flip(c, rel[2])]
                f_group.send(src, f_recv.at[member], (there[rel], grid))
    f_recv[pl.ds(member, 1)] = f_send[1, pl.ds(b, 1), pl.ds(c, 1)].reshape(1, FOLD, 128)

    def derive(r, _):
        rows = pl.ds(pl.multiple_of(r * 128, 128), 128)
        value = pre[rows, :]
        square = value * value
        t = jnp.tanh(GELU_A * (value + GELU_B * (value * square)))
        dgelu[rows, :] = 0.5 * (1.0 + t) + (0.5 * GELU_A) * value * (1.0 - t * t) * (
            1.0 + (3.0 * GELU_B) * square)
        return 0

    lax.fori_loop(0, HID // 128, derive, 0)
    wop[...] = jnp.transpose(wop_t[...])
    for copy in load_small[2:]:
        copy.wait()
    obs_pad[...] = jnp.zeros_like(obs_pad)
    own_cols = pl.ds(pl.multiple_of(zlo * 128, 128), 128)
    obs_pad[0:VARS, :] = obs_ref[:, own_cols]
    lo, hi = obs_pad[0:FOLD], obs_pad[FOLD:2 * FOLD]
    first = c == 0
    observed = jnp.where(low_lane, jnp.where(first, lo, swap(lo)), jnp.where(first, swap(hi), hi))
    area = area_ref[:, own_cols]
    area = jnp.where(low_row, jnp.where(first, area, swap(area)), jnp.where(first, swap(area), area))
    factor = area * (VARS * math.sqrt(8 / total_columns))
    gl[2 * FOLD:128, :] = jnp.zeros((128 - 2 * FOLD, COLS), BF16)

    def norm(difference):
        total = jnp.sum(difference * difference, axis=0, keepdims=True)
        square = (total + swap(total)) / VARS + EPSILON
        inverse = lax.rsqrt(square)
        return square * inverse, inverse

    f_group.arrived()
    fields = [f_recv[i].astype(F32) for i in range(8)]
    grads = []
    true_total = jnp.zeros((1, 128), F32)
    for m in range(8):
        difference = fields[m] - observed
        distance, inverse = norm(difference)
        true_total = true_total + distance
        grads.append(difference * (factor * inverse * (1.0 / (VARS * 8))))
    pair_total = jnp.full((1, 128), 8.0 * math.sqrt(EPSILON), F32)
    for m in range(8):
        for n in range(m + 1, 8):
            difference = fields[m] - fields[n]
            distance, inverse = norm(difference)
            pair_total = pair_total + 2.0 * distance
            pull = difference * (factor * inverse * (1.0 / (VARS * 64)))
            grads[m] = grads[m] - pull
            grads[n] = grads[n] + pull
    for m in range(8):
        g_send[m] = grads[m].astype(BF16)
    g_group = Group(g_recv.at[pl.ds(0, 7)], apart=7)
    g_copies = {
        rel: g_group.send(g_send.at[there[rel]], g_recv.at[member], (there[rel], grid))
        for rel in rels}
    g_recv[pl.ds(member, 1)] = g_send[pl.ds(member, 1)]
    loss = true_total * (1.0 / 8) - pair_total * (1.0 / 128)
    loss_recv[pl.ds(member, 1)] = jnp.broadcast_to(loss, (1, 8, 128))
    loss_group = Group(loss_recv.at[pl.ds(0, 7)])
    for rel in rels:
        loss_group.send(loss_recv.at[member], loss_recv.at[member], (there[rel], grid))

    drain()
    for ra, rb in ((0, 0), (0, 1), (1, 0), (1, 1)):
        for rel in rels:
            if rel[:2] == (ra, rb):
                g_copies[rel].wait_recv()
        t = 2 * flip(a, ra) + flip(b, rb)
        left, right = g_recv[2 * t].astype(F32), g_recv[2 * t + 1].astype(F32)
        cols = pl.ds(pl.multiple_of(128 * t, 128), 128)
        gl[0:FOLD, cols] = jnp.where(low_lane, left, swap(right)).astype(BF16)
        gl[FOLD:2 * FOLD, cols] = jnp.where(low_lane, swap(left), right).astype(BF16)
        gp[:, cols] = (dot(wop[...], gl[:, cols]) * dgelu[:, cols]).astype(BF16)

    sib_groups = [Group(sib_recv.at[q]) for q in range(2)]
    for q in range(2):
        rows = pl.ds(pl.multiple_of((1 - c) * 512 + q * 256, 256), 256)
        sib_send[q] = dot_nt(lat[rows, :], gp[...]).astype(BF16)
        sib_groups[q].send(sib_send.at[q], sib_recv.at[q], sibling)
    wo_part[...] = dot_nt(hidden[...], gl[...])
    wo_send[...] = wo_part[pl.ds(pl.multiple_of((1 - c) * 256, 256), 256), :].astype(BF16)
    wo_group = Group(wo_recv)
    wo_group.send(wo_send, wo_recv, sibling)
    ones = jnp.ones((16, COLS), BF16)
    sum_in = dot_nt(ones, gp[...])[0:1]
    sum_out = dot_nt(ones, gl[...])[0:1]
    rows8 = lax.broadcasted_iota(jnp.int32, (8, 128), 0)
    tile = jnp.where(rows8 == 4, sum_out, 0.0)
    for i in range(4):
        tile = jnp.where(rows8 == i, sum_in[:, 128 * i:128 * i + 128], tile)
    sm_c[pl.ds(c, 1)] = tile.reshape(1, 8, 128)
    smc_group = Group(sm_c.at[0])
    smc_group.send(sm_c.at[c], sm_c.at[c], sibling)

    x_cols = pl.ds(pl.multiple_of(x * 128, 128), 128)
    u_rows = pl.ds(pl.multiple_of(u * 32, 32), 32)

    def own_half(q):
        rows = pl.ds(pl.multiple_of(c * 512 + q * 256, 256), 256)
        own[q] = dot_nt(lat[rows, :], gp[...])

    def merge(q):
        sib_groups[q].arrived()
        part[q] = (own[q] + sib_recv[q].astype(F32)).astype(BF16)

    own_half(0)
    own_half(1)
    merge(0)
    x0_group = Group(x0_recv)
    for k in FAR4:
        cols = pl.ds(pl.multiple_of(x_at[k] * 128, 128), 128)
        x0_group.send(part.at[0, :, cols], x0_recv.at[k - 1], to_x[k])
    merge(1)
    u1_group, w1_group = Group(u1_recv), Group(w1_recv)
    for k in FAR8:
        rows = pl.ds(pl.multiple_of(u_at[k] * 16, 16), 16)
        u1_group.send(part.at[1, rows], u1_recv.at[k - 1], to_u[k])
        rows = pl.ds(pl.multiple_of(128 + v_at[k] * 16, 16), 16)
        w1_group.send(part.at[1, rows], w1_recv.at[k - 1], to_v[k])
    wo_group.arrived()
    wo_rs[...] = (
        wo_part[pl.ds(pl.multiple_of(c * 256, 256), 256), :] + wo_recv[...].astype(F32)).astype(BF16)
    wox_group = Group(wox_recv)
    for k in FAR4:
        rows = pl.ds(pl.multiple_of(x_at[k] * 64, 64), 64)
        wox_group.send(wo_rs.at[rows], wox_recv.at[k - 1], to_x[k])
    smc_group.arrived()
    sm_x[pl.ds(x, 1)] = (sm_c[0] + sm_c[1]).reshape(1, 8, 128)
    smx_group = Group(sm_x.at[pl.ds(0, 3)])
    for k in FAR4:
        smx_group.send(sm_x.at[x], sm_x.at[x], to_x[k])

    drain()
    x0_group.arrived()
    total = part[0, :, x_cols].astype(F32)
    for k in range(3):
        total = total + x0_recv[k].astype(F32)
    s0[...] = total.astype(BF16)
    u0_group = Group(u0_recv)
    for k in FAR8:
        rows = pl.ds(pl.multiple_of(u_at[k] * 32, 32), 32)
        u0_group.send(s0.at[rows], u0_recv.at[k - 1], to_u[k])
    wox_group.arrived()
    total = wo_rs[pl.ds(pl.multiple_of(x * 64, 64), 64), :].astype(F32)
    for k in range(3):
        total = total + wox_recv[k].astype(F32)
    smx_group.arrived()
    small = sm_x[0] + sm_x[1] + sm_x[2] + sm_x[3]
    for j in range(8):
        wou_src[j, 0:8] = total[8 * j:8 * j + 8]
        wou_src[j, 8:16] = small
    wou_recv[pl.ds(u, 1)] = wou_src[pl.ds(u, 1)]
    wou_group = Group(wou_recv.at[pl.ds(0, 7)])
    for k in FAR8:
        wou_group.send(wou_src.at[u_at[k]], wou_recv.at[u], to_u[k])
    for group, received_1, at, place in ((u1_group, u1_recv, u * 16, 0), (w1_group, w1_recv, 128 + v * 16, 16)):
        group.arrived()
        total = part[1, pl.ds(pl.multiple_of(at, 16), 16), :].astype(F32)
        for k in range(7):
            total = total + received_1[k].astype(F32)
        s1[place:place + 16, :] = total.astype(BF16)
    x1_group = Group(x1_recv)
    for k in FAR4:
        cols = pl.ds(pl.multiple_of(x_at[k] * 128, 128), 128)
        x1_group.send(s1.at[:, cols], x1_recv.at[k - 1], to_x[k])

    x1_group.arrived()
    total = s1[:, x_cols].astype(F32)
    for k in range(3):
        total = total + x1_recv[k].astype(F32)
    total = total.astype(BF16)
    v_recv[v, 32:48] = total[0:16]
    w_recv[u] = total[16:32]
    u0_group.arrived()
    total = s0[u_rows, :].astype(F32)
    for k in range(7):
        total = total + u0_recv[k].astype(F32)
    v_recv[v, 0:32] = total.astype(BF16)
    v_group, w_group = Group(v_recv.at[pl.ds(0, 7)]), Group(w_recv.at[pl.ds(0, 7)])
    for k in FAR8:
        v_group.send(v_recv.at[v], v_recv.at[v], to_v[k])
        w_group.send(w_recv.at[u], w_recv.at[u], to_u[k])
    wou_group.arrived()
    total = wou_recv[0]
    for k in range(1, 8):
        total = total + wou_recv[k]
    wov_recv[pl.ds(v, 1)] = total.reshape(1, 16, 128)
    wov_group = Group(wov_recv.at[pl.ds(0, 7)])
    for k in FAR8:
        wov_group.send(wov_recv.at[v], wov_recv.at[v], to_v[k])
    drain()

    base = c * 512

    def block(q, rows_at, rows, cols):
        return gw_ref.at[pl.ds(pl.multiple_of(base + q * 256 + rows_at, 16), rows), cols]

    v_group.arrived()
    total = v_recv[0].astype(F32)
    for k in range(1, 8):
        total = total + v_recv[k].astype(F32)
    total = total.astype(BF16)
    spot0 = block(0, u * 32, 32, x_cols)
    spot0[...] = total[0:32]
    u0_group = Group(u0_recv)
    for k in FAR8:
        u0_group.send(spot0, spot0, to_u[k])
    spot1 = block(1, u * 16, 16, x_cols)
    spot1[...] = total[32:48]
    w_group.arrived()
    total = w_recv[0].astype(F32)
    for k in range(1, 8):
        total = total + w_recv[k].astype(F32)
    spot2 = block(1, 128 + v * 16, 16, x_cols)
    spot2[...] = total.astype(BF16)
    x1_group = Group(x1_recv)
    for k in FAR4:
        x1_group.send(spot1, spot1, to_x[k])
        x1_group.send(spot2, spot2, to_x[k])
    wov_group.arrived()
    total = wov_recv[0]
    for k in range(1, 8):
        total = total + wov_recv[k]
    spot = gwo.at[pl.ds(pl.multiple_of(c * 256 + x * 64 + u * 8, 8), 8)]
    spot[...] = total[0:8]
    wou_group = Group(loss_recv.at[pl.ds(0, 7)])
    for k in FAR8:
        wou_group.send(spot, spot, to_u[k])
    for i in range(4):
        gbin_ref[:, 128 * i:128 * i + 128] = total[8 + i:9 + i]
    gbo_ref[...] = total[12:13, 0:VARS]
    drain()

    x1_group.arrived()
    spot1 = block(1, u * 16, 16, pl.ds(0, 512))
    spot2 = block(1, 128 + v * 16, 16, pl.ds(0, 512))
    u1_group, w1_group, last = Group(u1_recv, apart=7), Group(w1_recv, apart=7), Group(part)
    u1_copies, w1_copies = [], []
    for k in FAR8:
        u1_copies.append(u1_group.send(spot1, spot1, to_u[k]))
        w1_copies.append(w1_group.send(spot2, spot2, to_v[k]))
    last.send(spot1, spot1, sibling)
    last.send(spot2, spot2, sibling)
    u0_group.arrived()
    spot = block(0, 0, 256, x_cols)
    x0_group = Group(x0_recv, apart=3)
    x0_copies = [x0_group.send(spot, spot, to_x[k]) for k in FAR4]
    last.send(spot, spot, sibling)
    wou_group.arrived()
    rows = pl.ds(pl.multiple_of(c * 256 + x * 64, 64), 64)
    spot = gwo_low.at[rows]
    spot[...] = gwo[rows].astype(BF16)
    wox_group = Group(wox_recv, apart=3)
    wox_copies = [wox_group.send(spot, spot, to_x[k]) for k in FAR4]
    last_wo = Group(wo_recv)
    last_wo.send(spot, spot, sibling)

    drain()
    loss_group.arrived()
    for t in range(4):
        loss_ref[:, 128 * t:128 * t + 128] = jnp.where(
            low_row, loss_recv[2 * t, 0:1, :], loss_recv[2 * t + 1, 0:1, :])

    def forward(copy, spot):
        copy.wait_recv()
        last.send(spot, spot, sibling)

    def forward_rows(steps):
        for i in steps:
            k = FAR8[i]
            forward(u1_copies[i], block(1, u_at[8 - k] * 16, 16, pl.ds(0, 512)))
            forward(w1_copies[i], block(1, 128 + v_at[8 - k] * 16, 16, pl.ds(0, 512)))

    def forward_columns(steps):
        for i in steps:
            cols = pl.ds(pl.multiple_of(x_at[4 - FAR4[i]] * 128, 128), 128)
            forward(x0_copies[i], block(0, 0, 256, cols))

    forward_rows((6, 5, 4, 3))
    forward_columns((2, 1))
    forward_rows((2, 1, 0))
    forward_columns((0,))
    for k, copy in reversed(list(zip(FAR4, wox_copies))):
        copy.wait_recv()
        spot = gwo_low.at[pl.ds(pl.multiple_of(c * 256 + x_at[4 - k] * 64, 64), 64)]
        last_wo.send(spot, spot, sibling)
    last_wo.arrived()
    gwo_ref[...] = jnp.transpose(gwo_low[...].astype(F32))[0:VARS]
    last.arrived()
    drain()
    drain()
    assert len(groups) == N_SENDS and received[0] == N_RECEIVES


def deliver(*refs):
    results, places, sems = refs[0:5], refs[5:10], refs[10]
    copies = [
        pltpu.make_async_copy(src, dst, sems.at[i])
        for i, (src, dst) in enumerate(zip(results, places))
    ]
    for copy in copies:
        copy.start()
    for copy in copies:
        copy.wait()


def per_device(latent, w_in, b_in, output_weight, output_bias, observed_field, area):
    total_columns = latent.shape[2] * lax.axis_size("grid")
    vmem = pl.BlockSpec(memory_space=pltpu.VMEM)
    hbm = pl.BlockSpec(memory_space=pltpu.HBM)

    def scratch(dtype, *shape):
        return pltpu.VMEM(shape, dtype)

    results = (
        jax.ShapeDtypeStruct((1, COLS), F32),
        jax.ShapeDtypeStruct((DIN, HID), BF16),
        jax.ShapeDtypeStruct((1, HID), F32),
        jax.ShapeDtypeStruct((VARS, HID), F32),
        jax.ShapeDtypeStruct((1, VARS), F32),
    )
    operands = (
        latent, w_in, b_in.reshape(1, HID), jnp.pad(output_weight.T, ((0, 128 - VARS), (0, 0))), output_bias.reshape(1, VARS),
        observed_field, area.reshape(1, COLS),
    )
    made = pl.pallas_call(
        lambda *refs: kernel(total_columns, *refs),
        out_shape=results,
        in_specs=[hbm] * 3 + [vmem] + [hbm] * 3,
        out_specs=(vmem,) * 5,
        scratch_shapes=[
            scratch(F32, 1, HID), scratch(F32, 1, VARS),
            scratch(F32, VARS, COLS), scratch(F32, 1, COLS), scratch(F32, HID, 128),
            scratch(BF16, HID, 128),
            scratch(BF16, DIN, COLS), scratch(BF16, DIN, HID),
            scratch(F32, HID, 128), scratch(F32, HID, COLS), scratch(F32, HID, COLS),
            scratch(BF16, HID, COLS), scratch(BF16, HID, 128),
            scratch(F32, 1, 128), scratch(F32, 2 * FOLD, 128),
            scratch(BF16, 2, 2, 2, FOLD, 128), scratch(BF16, 8, FOLD, 128),
            scratch(BF16, 8, FOLD, 128), scratch(BF16, 8, FOLD, 128),
            scratch(F32, 8, 8, 128), scratch(BF16, 128, COLS), scratch(BF16, HID, COLS),
            scratch(BF16, 2, 256, HID), scratch(BF16, 2, 256, HID),
            scratch(F32, 2, 256, HID), scratch(BF16, 2, 256, HID),
            scratch(BF16, 3, 256, 128), scratch(BF16, 256, 128),
            scratch(BF16, 7, 32, 128),
            scratch(BF16, 7, 16, HID), scratch(BF16, 7, 16, HID), scratch(BF16, 32, HID),
            scratch(BF16, 3, 32, 128), scratch(BF16, 8, 48, 128), scratch(BF16, 8, 16, 128),
            scratch(F32, HID, 128), scratch(BF16, 256, 128), scratch(BF16, 256, 128),
            scratch(BF16, 256, 128), scratch(BF16, 3, 64, 128),
            scratch(F32, 8, 16, 128), scratch(F32, 8, 16, 128), scratch(F32, 8, 16, 128),
            scratch(F32, 2, 8, 128), scratch(F32, 4, 8, 128),
            pltpu.SemaphoreType.DMA((8,)),
            pltpu.SemaphoreType.DMA((N_SENDS,)), pltpu.SemaphoreType.DMA((N_RECEIVES,)),
        ],
        compiler_params=pltpu.CompilerParams(
            collective_id=0, has_side_effects=True, vmem_limit_bytes=40 * 2**20),
        cost_estimate=pl.CostEstimate(
            flops=4 * DIN * HID * COLS, bytes_accessed=4 * 2**20, transcendentals=2 * HID * COLS),
        name="energy_score_step",
    )(*[
        operand if i == 3 else pltpu.with_memory_space_constraint(operand, pltpu.HBM)
        for i, operand in enumerate(operands)])
    loss, grad_w_in, grad_b_in, grad_w_out, grad_b_out = pl.pallas_call(
        deliver,
        out_shape=results,
        in_specs=[vmem] * 5,
        out_specs=(hbm,) * 5,
        scratch_shapes=[pltpu.SemaphoreType.DMA((5,))],
        compiler_params=pltpu.CompilerParams(vmem_limit_bytes=4 * 2**20),
        name="deliver",
    )(*made)
    return (
        loss.reshape(COLS), grad_w_in, grad_b_in.reshape(HID), grad_w_out.T,
        grad_b_out.reshape(VARS),
    )


def solution(mesh):
    placed = (P("member", None, "grid"), P(), P(), P(), P(), P(None, "grid"), P("grid"))
    return jax.shard_map(
        per_device,
        mesh=mesh,
        in_specs=placed,
        out_specs=(P("grid"), P(), P(), P(), P()),
        check_vma=False,
    )
```
